32 devices in a mesh: expert: 16 (over z, y, x), shard: 2 (over core).
Axes of the slice: x: 2, y: 2, z: 4, core: 2. Of those that a mesh axis runs over, the one named last changes fastest.
Arguments:
- tokens: bfloat16 [4096, 2048], P(('expert', 'shard')), may hold values from -6 to 6
- cotangent: bfloat16 [4096, 2048], P(('expert', 'shard')), may hold values from -6 to 6
- seq_len: int32 [16], P('expert'), may hold values from 129 to 256, as said below
- routes: int32 [4096, 6], P(('expert', 'shard')), may hold values from 0 to 31, all different within a row; in each aligned block of 128 rows (0 to 127, 128 to 255, ...) at most 48 rows name the same one
- attention_gain: bfloat16 [2048], P('shard'), may hold values from 0.5 to 1.5
- query_down: bfloat16 [2048, 1536], P('shard'), may hold values from -0.125 to 0.125
- query_gain: bfloat16 [1536], P('shard'), may hold values from 0.5 to 1.5
- query_up: bfloat16 [1536, 3072], P('shard'), may hold values from -0.15625 to 0.15625
- latent_down: bfloat16 [2048, 576], P('shard'), may hold values from -0.125 to 0.125
- latent_gain: bfloat16 [512], P('shard'), may hold values from 0.5 to 1.5
- latent_up: bfloat16 [512, 4096], P('shard'), may hold values from -0.25 to 0.25
- attention_out: bfloat16 [2048, 2048], P('shard'), may hold values from -2 to 2
- feedforward_gain: bfloat16 [2048], P('shard'), may hold values from 0.5 to 1.5
- router: bfloat16 [2048, 32], P('shard'), may hold values from -0.0625 to 0.0625
- shared_gate: bfloat16 [2048, 2816], P('shard'), may hold values from -0.125 to 0.125
- shared_up: bfloat16 [2048, 2816], P('shard'), may hold values from -0.125 to 0.125
- shared_down: bfloat16 [2816, 2048], P('shard'), may hold values from -0.109375 to 0.109375
- expert_gate: bfloat16 [32, 2048, 1408], P('expert', None, 'shard'), may hold values from -0.125 to 0.125
- expert_up: bfloat16 [32, 2048, 1408], P('expert', None, 'shard'), may hold values from -0.125 to 0.125
- expert_down: bfloat16 [32, 1408, 2048], P('expert', 'shard'), may hold values from -0.15625 to 0.15625
Outputs:
- layer_out: bfloat16 [4096, 2048], P(('expert', 'shard'))
- grad_tokens: float32 [4096, 2048], P(('expert', 'shard'))
- grad_attention_gain: float32 [2048], P('shard')
- grad_query_down: float32 [2048, 1536], P('shard')
- grad_query_gain: float32 [1536], P('shard')
- grad_query_up: float32 [1536, 3072], P('shard')
- grad_latent_down: float32 [2048, 576], P('shard')
- grad_latent_gain: float32 [512], P('shard')
- grad_latent_up: float32 [512, 4096], P('shard')
- grad_attention_out: float32 [2048, 2048], P('shard')
- grad_feedforward_gain: float32 [2048], P('shard')
- grad_router: float32 [2048, 32], P('shard')
- grad_shared_gate: float32 [2048, 2816], P('shard')
- grad_shared_up: float32 [2048, 2816], P('shard')
- grad_shared_down: float32 [2816, 2048], P('shard')
- grad_expert_gate: float32 [32, 2048, 1408], P('expert', None, 'shard')
- grad_expert_up: float32 [32, 2048, 1408], P('expert', None, 'shard')
- grad_expert_down: float32 [32, 1408, 2048], P('expert', 'shard')
The draws below stay inside these ranges and needn't reach their ends.
Inputs may be any that keep to these rules, and one draw needn't show every extreme that they name: `seq_len`: every sequence has its valid length; some sequence has all 256. `routes`: in the rows of one device no expert is named by more than 48 rows, a bound that some block reaches.
All inputs are finite; a program needn't handle non-finite values.
Results may differ from the reference program's by a relative error of at most 0.025.
Values may be sent and summed in bfloat16 or wider, within the bound.
No kernel may reach another device: no remote copies, remote signals or barrier semaphores. Data moves between devices by JAX's collectives and lax.ppermute only.
A program may use at most 512 MiB of HBM per device.

```python
import math
import jax
import jax.numpy as jnp
import numpy as np
from jax import lax

D = 2048
HEADS = 16
NOPE = 128
ROPE = 64
VDIM = 128
KVL = 512
QL = 1536
FE = 1408
FS = 2816
TOP = 6
TOK_DEV = 128
EXPERTS = 32
LENGTH = 256
SEQS = 16
TOKENS = 4096
CAP = 48
N_SHARD = 2


def draw_seq_len(key, part):
    key = jax.random.fold_in(key, 7)
    first_key, second_key = jax.random.split(key)
    lengths = jax.random.randint(first_key, (SEQS,), (N_SHARD - 1) * TOK_DEV + 1, LENGTH + 1)
    chosen = jax.random.randint(second_key, (), 0, SEQS)
    return jnp.where(jnp.arange(SEQS) == chosen, LENGTH, lengths).astype(jnp.int32)


def block_scale(stream_key, shape, pieces, least, top_value):
    gain = 1.0
    for axis_at, blocks in pieces:
        steps = jax.random.uniform(jax.random.fold_in(jax.random.fold_in(stream_key, 6), axis_at), (blocks,), jnp.float32, least / len(pieces), top_value / len(pieces))
        gain = gain * jnp.repeat(jnp.exp(steps), shape[axis_at] // blocks).reshape((-1,) + (1,) * (len(shape) - 1 - axis_at))
    return gain


def deal_out(own_key, own, number, rows, count, top, bound, skew):
    order = jax.random.permutation(own_key, count)
    crowded, common = shares(count, rows * top, bound, skew, True), shares(count, rows * top, bound, skew, False)
    places = jnp.arange(count)

    def named(sizes, offset_by):
        used = int((sizes > 0).sum())
        fixed = max(1, used // 4)
        passed = fixed + (places - fixed + offset_by * (used - fixed)) % max(1, count - fixed)
        return jnp.zeros((count,), jnp.int32).at[order[jnp.where(places < fixed, places, passed)]].set(jnp.asarray(sizes, jnp.int32))

    sizes = jnp.where(number % 4 == 0, named(crowded, number // 4), named(common, number - number // 4 - 1))
    mixed = jax.random.permutation(jax.random.fold_in(own, 3), count)
    source_of, receiver = mixed[0:count // 2 * 2:2], mixed[1:count // 2 * 2:2]
    slack = jnp.minimum(sizes[source_of] - 1, bound - sizes[receiver]) // 2
    slack = jnp.where((source_of == order[0]) | (receiver == order[0]) | (sizes[receiver] == 0), 0, jnp.maximum(slack, 0))
    passed = jax.random.randint(jax.random.fold_in(own, 4), (count // 2,), 0, 1 << 20) % (slack + 1)
    sizes = sizes.at[source_of].add(-passed).at[receiver].add(passed)
    items = jnp.searchsorted(jnp.cumsum(sizes), jnp.arange(rows * top), side="right").astype(jnp.int32)
    grid = items.reshape(top, rows).T
    grid = grid[jax.random.permutation(jax.random.fold_in(own, 1), rows)]
    offset_by = jax.random.randint(jax.random.fold_in(own, 2), (rows, 1), 0, top)
    return jnp.take_along_axis(grid, (jnp.arange(top)[None, :] + offset_by) % top, axis=1)


def shares(amount, total, most, skew, full):
    weights = [(1 << 20) // math.isqrt(rank ** skew) + 1 for rank in range(1, amount + 1)]
    largest = most if full else min(most, max(-(-total // amount), total * weights[0] // sum(weights)))
    least = 1 if total - largest >= amount - 1 else 0
    holding, surplus = [largest] + [least] * (amount - 1), total - largest - least * (amount - 1)
    while surplus > 0:
        movable = [i for i in range(1, amount) if holding[i] < largest] or [i for i in range(1, amount) if holding[i] < most]
        mass, budget = sum([weights[i] for i in movable]), surplus
        for i in movable:
            more = min(most - holding[i], max(1, budget * weights[i] // mass), surplus)
            holding[i] = holding[i] + more
            surplus = surplus - more
    return np.array(holding)


def scatter_about(stream_key, shape, scale, most, shards=(), kind=jnp.bfloat16):
    values = jax.random.normal(stream_key, shape, jnp.float32) * scale
    if len(shards) > 0:
        values = block_scale(stream_key, shape, shards, -0.22, 0.18) * values
    return jnp.clip(values, min=-most, max=most).astype(kind)


def setup_inputs(seed: int = 0) -> dict:
    streams_of = jax.random.split(jax.random.key(seed), 21)
    tokens = scatter_about(streams_of[0], (TOKENS, D), 1.0, 6.0, ((0, 32),))
    cotangent = scatter_about(streams_of[1], (TOKENS, D), 1.0, 6.0, ((0, 32),))
    seq_len = draw_seq_len(jax.random.fold_in(streams_of[20], 71), 0)
    routes_keys = jax.random.split(jax.random.fold_in(streams_of[3], 1), TOKENS // TOK_DEV)
    routes_turns = jax.random.permutation(jax.random.fold_in(streams_of[3], 3), TOKENS // TOK_DEV)
    routes = jax.vmap(lambda own, number: deal_out(jax.random.fold_in(streams_of[3], 2), own, number, TOK_DEV, EXPERTS, TOP, CAP, 2))(routes_keys, routes_turns).reshape((TOKENS, TOP))
    attention_gain = jnp.clip(1.0 + 0.1 * jax.random.normal(streams_of[4], (D,), jnp.float32), 0.5, 1.5).astype(jnp.bfloat16)
    query_down = scatter_about(streams_of[5], (D, QL), D ** -0.5, 0.125, ((0, 2),))
    query_gain = jnp.clip(1.0 + 0.1 * jax.random.normal(streams_of[6], (QL,), jnp.float32), 0.5, 1.5).astype(jnp.bfloat16)
    query_up = scatter_about(streams_of[7], (QL, HEADS * (NOPE + ROPE)), QL ** -0.5, 0.15625, ((0, 2),))
    latent_down = scatter_about(streams_of[8], (D, KVL + ROPE), D ** -0.5, 0.125, ((0, 2),))
    latent_gain = jnp.clip(1.0 + 0.1 * jax.random.normal(streams_of[9], (KVL,), jnp.float32), 0.5, 1.5).astype(jnp.bfloat16)
    latent_up = scatter_about(streams_of[10], (KVL, HEADS * (NOPE + VDIM)), KVL ** -0.5, 0.25, ((0, 2),))
    attention_out = scatter_about(streams_of[11], (HEADS * VDIM, D), (max(HEADS * VDIM // 256, 1)) ** -0.5, 2.0, ((0, 2),))
    feedforward_gain = jnp.clip(1.0 + 0.1 * jax.random.normal(streams_of[12], (D,), jnp.float32), 0.5, 1.5).astype(jnp.bfloat16)
    router = scatter_about(streams_of[13], (D, EXPERTS), (4 * D) ** -0.5, 0.0625, ((0, 2),))
    shared_gate = scatter_about(streams_of[14], (D, FS), D ** -0.5, 0.125, ((0, 2),))
    shared_up = scatter_about(streams_of[15], (D, FS), D ** -0.5, 0.125, ((0, 2),))
    shared_down = scatter_about(streams_of[16], (FS, D), FS ** -0.5, 0.109375, ((0, 2),))
    expert_gate = scatter_about(streams_of[17], (EXPERTS, D, FE), D ** -0.5, 0.125, ((0, 16), (2, 2)))
    expert_up = scatter_about(streams_of[18], (EXPERTS, D, FE), D ** -0.5, 0.125, ((0, 16), (2, 2)))
    expert_down = scatter_about(streams_of[19], (EXPERTS, FE, D), FE ** -0.5, 0.15625, ((0, 16), (1, 2)))
    return {"tokens": tokens, "cotangent": cotangent, "seq_len": seq_len, "routes": routes, "attention_gain": attention_gain, "query_down": query_down, "query_gain": query_gain, "query_up": query_up, "latent_down": latent_down, "latent_gain": latent_gain, "latent_up": latent_up, "attention_out": attention_out, "feedforward_gain": feedforward_gain, "router": router, "shared_gate": shared_gate, "shared_up": shared_up, "shared_down": shared_down, "expert_gate": expert_gate, "expert_up": expert_up, "expert_down": expert_down}


EPS = 1e-06
ROUTE_SCALE = 2.446
ROPE_BASE = 50000.0
NEG = -1e+30
HIGH = lax.Precision.HIGHEST

@jax.custom_vjp
def low(v):
    return lax.optimization_barrier(v.astype(jnp.bfloat16)).astype(jnp.float32)

@jax.custom_vjp
def low_back(v):
    return v

def low_keep(v):
    return (low(v), None)

def low_pass(kept, grad):
    return (grad,)

def back_keep(v):
    return (v, None)

def back_low(kept, grad):
    return (low(grad),)
low.defvjp(low_keep, low_pass)
low_back.defvjp(back_keep, back_low)

def rms_norm(values, norm_gain):
    return values * lax.rsqrt(lax.optimization_barrier(jnp.mean(values * values, axis=-1, keepdims=True)) + EPS) * norm_gain

def tables(positions, rope_width):
    half_width = rope_width // 2
    frequencies = ROPE_BASE ** (-2.0 * jnp.arange(half_width, dtype=jnp.float32) / rope_width)
    angles = positions.astype(jnp.float32)[:, None] * frequencies[None, :]
    return (jnp.cos(angles), jnp.sin(angles))

def rotate(values, cosine_table, sine_table):
    half_width = values.shape[-1] // 2
    first_half = values[..., :half_width]
    second_half = values[..., half_width:]
    return jnp.concatenate([first_half * cosine_table - second_half * sine_table, second_half * cosine_table + first_half * sine_table], axis=-1)

def matmul(left_side, right_side):
    return jnp.dot(left_side, right_side, precision=HIGH)

def route_gates(logits, routes):
    chosen = jnp.take_along_axis(jax.nn.sigmoid(logits), routes, axis=1)
    return ROUTE_SCALE * chosen / lax.optimization_barrier(jnp.sum(chosen, axis=1, keepdims=True))

def expert_sum(ffn_in, gates, routes, expert_gate, expert_up, expert_down):
    route_flat = routes.reshape(-1)
    gate_flat = gates.reshape(-1)
    row_limit = N_SHARD * CAP

    def one_expert(running_total, item_parts):
        expert_index, weight_gate, weight_up, weight_down = item_parts
        misses = (route_flat != expert_index).astype(jnp.int32)
        sorted_pairs = jnp.argsort(misses, stable=True)[:row_limit].astype(jnp.int32)
        token_row = (sorted_pairs // TOP).astype(jnp.int32)
        row_block = low_back(ffn_in[token_row])
        gate_part = low_back(matmul(row_block, weight_gate))
        up_part = low_back(matmul(row_block, weight_up))
        hidden = low(jax.nn.silu(gate_part) * up_part)
        result = low(low_back(matmul(hidden, weight_down)))
        weight = jnp.where(misses[sorted_pairs] == 0, gate_flat[sorted_pairs], 0.0)
        return (running_total.at[token_row].add(weight[:, None] * result), None)
    zero_total = jnp.zeros_like(ffn_in)
    expert_ids = jnp.arange(EXPERTS, dtype=jnp.int32)
    running_total, ignored = lax.scan(jax.checkpoint(one_expert), zero_total, (expert_ids, expert_gate, expert_up, expert_down))
    return running_total

def layer_group(params, token_block, length, route_block):
    attention_gain, query_down, query_gain, query_up, latent_down, latent_gain, latent_up, attention_out, feedforward_gain, router, shared_gate, shared_up, shared_down, expert_gate, expert_up, expert_down = params
    rows_here = token_block.shape[0]
    positions = jnp.arange(rows_here, dtype=jnp.int32)
    cosine_table, sine_table = tables(positions, ROPE)
    normed = low(rms_norm(token_block, attention_gain))
    q_latent = low_back(matmul(normed, query_down))
    q_normed = low(rms_norm(q_latent, query_gain))
    q_raw = low_back(matmul(q_normed, query_up)).reshape(rows_here, HEADS, NOPE + ROPE)
    queries = low(jnp.concatenate([q_raw[..., :NOPE], rotate(q_raw[..., NOPE:], cosine_table[:, None, :], sine_table[:, None, :])], axis=-1))
    latent = low_back(matmul(normed, latent_down))
    c_normed = low(rms_norm(latent[:, :KVL], latent_gain))
    key_rope = low(rotate(latent[:, KVL:], cosine_table, sine_table))
    keys_values = low(low_back(matmul(c_normed, latent_up))).reshape(rows_here, HEADS, NOPE + VDIM)
    raw_scores = jnp.einsum('qhd,khd->hqk', queries[..., :NOPE], keys_values[..., :NOPE], precision=HIGH)
    raw_scores = low_back(raw_scores + jnp.einsum('qhr,kr->hqk', queries[..., NOPE:], key_rope, precision=HIGH))
    allowed = (positions[None, :] <= positions[:, None]) & (positions[None, :] < length)
    scores = jnp.where(allowed[None], raw_scores * (NOPE + ROPE) ** (-0.5), NEG)
    row_peak = lax.optimization_barrier(jnp.max(scores, axis=-1, keepdims=True))
    exp_terms = jnp.exp(scores - row_peak)
    probabilities = low(exp_terms / lax.optimization_barrier(jnp.sum(exp_terms, axis=-1, keepdims=True)))
    mixed = jnp.einsum('hqk,khv->qhv', probabilities, keys_values[..., NOPE:], precision=HIGH)
    mixed = low(low_back(mixed)).reshape(rows_here, HEADS * VDIM)
    resid = token_block + low_back(matmul(mixed, attention_out))
    ffn_in = low(rms_norm(resid, feedforward_gain))
    gates = route_gates(low_back(matmul(ffn_in, router)), route_block)
    gate_shared = low_back(matmul(ffn_in, shared_gate))
    up_shared = low_back(matmul(ffn_in, shared_up))
    shared_out = low_back(matmul(low(jax.nn.silu(gate_shared) * up_shared), shared_down))
    return resid + expert_sum(ffn_in, gates, route_block, expert_gate, expert_up, expert_down) + shared_out

def reference(tokens, cotangent, seq_len, routes, attention_gain, query_down, query_gain, query_up, latent_down, latent_gain, latent_up, attention_out, feedforward_gain, router, shared_gate, shared_up, shared_down, expert_gate, expert_up, expert_down):
    weights = tuple((weight.astype(jnp.float32) for weight in (attention_gain, query_down, query_gain, query_up, latent_down, latent_gain, latent_up, attention_out, feedforward_gain, router, shared_gate, shared_up, shared_down, expert_gate, expert_up, expert_down)))
    route_groups = routes.reshape(SEQS, LENGTH, TOP)

    def whole(source, *params):

        def group_step(carry_value, item_parts):
            token_block, length, route_block = item_parts
            return (carry_value, jax.checkpoint(layer_group)(params, token_block, length, route_block))
        carry_value, group_outputs = lax.scan(group_step, jnp.zeros((), jnp.float32), (source.reshape(SEQS, LENGTH, D), seq_len, route_groups))
        return group_outputs.reshape(TOKENS, D)
    primal, pullback = jax.vjp(whole, tokens.astype(jnp.float32), *weights)
    gradients = pullback(cotangent.astype(jnp.float32))
    return (primal.astype(jnp.bfloat16), gradients[0], gradients[1], gradients[2], gradients[3], gradients[4], gradients[5], gradients[6], gradients[7], gradients[8], gradients[9], gradients[10], gradients[11], gradients[12], gradients[13], gradients[14], gradients[15], gradients[16])
```

```python
import jax
import jax.numpy as jnp
from jax import lax
from jax.sharding import PartitionSpec as P

HEADS = 16
NOPE = 128
ROPE = 64
VDIM = 128
KVL = 512
TOP = 6

EPS = 1e-06
ROUTE_SCALE = 2.446
ROPE_BASE = 50000.0
NEG = -1e30

LOW = jnp.bfloat16
F32 = jnp.float32


def tables(positions, rope_width):
    half_width = rope_width // 2
    frequencies = ROPE_BASE ** (-2.0 * jnp.arange(half_width, dtype=F32) / rope_width)
    angles = positions.astype(F32)[:, None] * frequencies[None, :]
    return (jnp.cos(angles), jnp.sin(angles))


def rotate(values, cosine_table, sine_table):
    half_width = values.shape[-1] // 2
    first_half = values[..., :half_width]
    second_half = values[..., half_width:]
    return jnp.concatenate(
        [
            first_half * cosine_table - second_half * sine_table,
            second_half * cosine_table + first_half * sine_table,
        ],
        axis=-1,
    )


def product(left_side, right_side):
    return jnp.dot(left_side, right_side, preferred_element_type=F32)


def outer_sum(left_side, right_side):
    return lax.dot_general(
        left_side, right_side, (((0,), (0,)), ((), ())), preferred_element_type=F32
    )


def back_product(left_side, right_side):
    return lax.dot_general(
        left_side, right_side, (((1,), (1,)), ((), ())), preferred_element_type=F32
    )


def total(terms):
    result = terms[0]
    for term in terms[1:]:
        result = result + term
    return result


def inverse_rms(values):
    return lax.rsqrt(jnp.mean(values * values, axis=-1, keepdims=True) + EPS)


def norm_back(values, scale, gain, grad):
    weighted = grad * gain
    inner = jnp.mean(weighted * values, axis=-1, keepdims=True)
    return scale * weighted - values * (scale * scale * scale) * inner, grad * values * scale


def silu_parts(gate_part):
    sig = jax.nn.sigmoid(gate_part)
    return gate_part * sig, sig * (1.0 + gate_part * (1.0 - sig))


def local(
    tokens,
    cotangent,
    seq_len,
    routes,
    attention_gain,
    query_down,
    query_gain,
    query_up,
    latent_down,
    latent_gain,
    latent_up,
    attention_out,
    feedforward_gain,
    router,
    shared_gate,
    shared_up,
    shared_down,
    expert_gate,
    expert_up,
    expert_down,
):
    rows, width = tokens.shape
    shards = lax.axis_size("shard")
    owners = lax.axis_size("expert")
    core = lax.axis_index("shard")
    chip = lax.axis_index("expert")
    local_count = expert_gate.shape[0]
    all_experts = local_count * owners
    capacity = 2 * rows * TOP // all_experts
    span = rows * shards
    blocks = shards * owners
    own_heads = HEADS // shards
    part_cols = width // shards

    def place(s):
        return (core - s) % shards

    def from_core(values, s):
        return lax.ppermute(values, "shard", [(i, (i + s) % shards) for i in range(shards)])

    def to_core(values, s):
        return lax.ppermute(values, "shard", [(i, (i - s) % shards) for i in range(shards)])

    def relative(values):
        return [values] + [from_core(values, s) for s in range(1, shards)]

    def sum_parts(parts, kind):
        got = [to_core(parts[s].astype(kind), s).astype(F32) for s in range(1, shards)]
        return total([parts[0].astype(F32)] + got)

    def cut(values, axis):
        size = values.shape[axis] // shards
        return [
            lax.dynamic_slice_in_dim(values, place(s) * size, size, axis) for s in range(shards)
        ]

    def natural(parts, axis):
        pieces = []
        for i in range(shards):
            piece = parts[0]
            for s in range(1, shards):
                piece = jnp.where(place(s) == i, parts[s], piece)
            pieces.append(piece)
        return jnp.concatenate(pieces, axis=axis)

    with jax.named_scope("early_gathers"):
        token_parts = relative(tokens)
        gains_own = jnp.concatenate([attention_gain, query_gain, latent_gain, feedforward_gain])
        gain_parts = relative(gains_own)
        query_down_parts = relative(query_down)
        latent_down_parts = relative(latent_down)
        query_up_parts = relative(query_up)
        latent_up_parts = relative(latent_up)
        router_parts = relative(router)
        routes_all = jnp.stack(relative(lax.all_gather(routes, "expert", axis=0)))
        grad_all = jnp.stack(relative(lax.all_gather(cotangent, "expert", axis=0)))

    hidden_all = shared_gate.shape[1]
    hidden_own = hidden_all // blocks
    hidden_shard = hidden_all // shards

    def shared_columns(weight):
        pieces = [
            lax.dynamic_slice_in_dim(
                weight, place(s) * hidden_shard + chip * hidden_own, hidden_own, 1
            )
            for s in range(shards)
        ]
        got = [pieces[0]] + [None] * (shards - 1)
        for s in range(1, shards):
            got[shards - s] = to_core(pieces[s], s)
        return natural(got, 0)

    with jax.named_scope("shared_weights"):
        gate_cols = shared_columns(shared_gate)
        up_cols = shared_columns(shared_up)
        down_rows = lax.dynamic_slice_in_dim(shared_down, chip * hidden_own, hidden_own, 0)
        router_full = natural(router_parts, 0)

    bounds = [0]
    for size in (part_cols, query_gain.shape[0], latent_gain.shape[0], part_cols):
        bounds.append(bounds[-1] + size)
    attention_gain_parts = [g[bounds[0] : bounds[1]].astype(F32) for g in gain_parts]
    query_gain_full = natural([g[bounds[1] : bounds[2]] for g in gain_parts], 0).astype(F32)
    latent_gain_full = natural([g[bounds[2] : bounds[3]] for g in gain_parts], 0).astype(F32)
    feed_gain_full = natural([g[bounds[3] : bounds[4]] for g in gain_parts], 0).astype(F32)
    gain_rel = jnp.concatenate(attention_gain_parts)

    with jax.named_scope("attention_forward"):
        positions = jnp.concatenate(
            [place(s) * rows + jnp.arange(rows, dtype=jnp.int32) for s in range(shards)]
        )
        cosine_table, sine_table = tables(positions, ROPE)
        length = seq_len[0]
        sequence = jnp.concatenate(token_parts, axis=0)
        source = jnp.concatenate(cut(sequence, 1), axis=1).astype(F32)
        source_scale = inverse_rms(source)
        normed = (source * source_scale * gain_rel).astype(LOW)
        normed_parts = jnp.split(normed, shards, axis=1)
        query_latent = total([product(a, w) for a, w in zip(normed_parts, query_down_parts)])
        query_scale = inverse_rms(query_latent)
        query_low = (query_latent * query_scale * query_gain_full).astype(LOW)
        latent = total([product(a, w) for a, w in zip(normed_parts, latent_down_parts)])
        latent_c = latent[:, :KVL]
        latent_scale = inverse_rms(latent_c)
        latent_low = (latent_c * latent_scale * latent_gain_full).astype(LOW)
        key_rope = rotate(latent[:, KVL:], cosine_table, sine_table).astype(LOW)
        query_low_parts = cut(query_low, 1)
        latent_low_parts = cut(latent_low, 1)
        query_raw = total(
            [product(a, cut(w, 1)[0]) for a, w in zip(query_low_parts, query_up_parts)]
        ).reshape(span, own_heads, NOPE + ROPE)
        query_nope = query_raw[..., :NOPE].astype(LOW)
        query_rope = rotate(
            query_raw[..., NOPE:], cosine_table[:, None, :], sine_table[:, None, :]
        ).astype(LOW)
        keys_values = (
            total([product(a, cut(w, 1)[0]) for a, w in zip(latent_low_parts, latent_up_parts)])
            .astype(LOW)
            .reshape(span, own_heads, NOPE + VDIM)
        )
        key_nope = keys_values[..., :NOPE]
        values = keys_values[..., NOPE:]
        score_scale = (NOPE + ROPE) ** (-0.5)
        allowed = (positions[None, :] <= positions[:, None]) & (positions[None, :] < length)
        raw_scores = jnp.einsum("qhd,khd->hqk", query_nope, key_nope, preferred_element_type=F32)
        raw_scores = raw_scores + jnp.einsum(
            "qhr,kr->hqk", query_rope, key_rope, preferred_element_type=F32
        )
        scores = jnp.where(allowed[None], raw_scores * score_scale, NEG)
        row_peak = jnp.max(scores, axis=-1, keepdims=True)
        exp_terms = jnp.exp(scores - row_peak)
        probabilities = exp_terms / jnp.sum(exp_terms, axis=-1, keepdims=True)
        p_low = probabilities.astype(LOW)
        mixed = jnp.einsum("hqk,khv->qhv", p_low, values, preferred_element_type=F32)
        mixed = mixed.astype(LOW).reshape(span, own_heads * VDIM)
        attended = product(mixed, attention_out)
        resid = tokens.astype(F32) + sum_parts(jnp.split(attended, shards, axis=0), F32)
        resid_scale = inverse_rms(resid)
        ffn_low = (resid * resid_scale * feed_gain_full).astype(LOW)

    with jax.named_scope("token_gather"):
        ffn_all = jnp.stack(relative(lax.all_gather(ffn_low, "expert", axis=0)))
        inputs = ffn_all.reshape(blocks * rows, width)
        grads = grad_all.reshape(blocks * rows, width)
        input_blocks = ffn_all.reshape(blocks, rows, width)
        grad_blocks = grad_all.reshape(blocks, rows, width)

    with jax.named_scope("gates"):
        expert_ids = jnp.arange(all_experts, dtype=jnp.int32)
        hit_all = jnp.any(
            routes_all.reshape(blocks * rows, TOP, 1) == expert_ids, axis=1
        ).astype(F32)
        sig_all = jax.nn.sigmoid(product(inputs, router_full))
        chosen_all = sig_all * hit_all
        chosen_sum = jnp.sum(chosen_all, axis=1, keepdims=True)
        first = chip * local_count
        gate_local = (
            ROUTE_SCALE * lax.dynamic_slice_in_dim(chosen_all, first, local_count, 1) / chosen_sum
        ).reshape(blocks, rows, local_count)
        hit = lax.dynamic_slice_in_dim(hit_all, first, local_count, 1).reshape(
            blocks, rows, local_count
        )
        hit = jnp.swapaxes(hit, 1, 2)
        gate_local = jnp.swapaxes(gate_local, 1, 2)
        rank = (jnp.cumsum(hit, axis=2) - hit).astype(jnp.int32)
        slots = jnp.arange(capacity, dtype=jnp.int32)
        select = (rank[:, :, None, :] == slots[None, None, :, None]) & (hit[:, :, None, :] > 0)

    with jax.named_scope("shared_experts"):
        sg_part = product(inputs, gate_cols)
        su_part = product(inputs, up_cols)
        sg_silu, sg_slope = silu_parts(sg_part)
        shared_hidden = (sg_silu * su_part).astype(LOW)
        shared_back = back_product(grads, down_rows)
        grad_sg = (shared_back * su_part * sg_slope).astype(LOW)
        grad_su = (shared_back * sg_silu).astype(LOW)
        out_sum = product(shared_hidden, down_rows).reshape(blocks, rows, width)
        back_sum = (back_product(grad_sg, gate_cols) + back_product(grad_su, up_cols)).reshape(
            blocks, rows, width
        )
        delta_shared_gate = outer_sum(grad_sg, inputs).astype(LOW)
        delta_shared_up = outer_sum(grad_su, inputs).astype(LOW)
        delta_shared_down = outer_sum(shared_hidden, grads).astype(LOW)

    def shared_delta(delta):
        parts = cut(delta, 1)
        got = [parts[0]] + [None] * (shards - 1)
        for s in range(1, shards):
            got[shards - s] = to_core(parts[s], s)
        mine = jnp.stack([got[s] for s in range(shards)])
        every = lax.all_gather(mine, "expert", axis=1)
        ordered = natural(
            [every[s].reshape(hidden_shard, part_cols) for s in range(shards)], 0
        )
        return ordered.T.astype(F32)

    with jax.named_scope("shared_gradients"):
        grad_shared_gate = shared_delta(delta_shared_gate)
        grad_shared_up = shared_delta(delta_shared_up)
        grad_shared_down = (
            lax.all_gather(delta_shared_down, "expert", axis=0, tiled=True).astype(F32)
        )

    grad_experts = []
    gate_grads = []
    for e in range(local_count):
        with jax.named_scope("routed_expert"):
            pick = select[:, e].astype(LOW)
            row_block = jnp.einsum(
                "brt,btd->brd", pick, input_blocks, preferred_element_type=F32
            ).astype(LOW)
            grad_block = jnp.einsum(
                "brt,btd->brd", pick, grad_blocks, preferred_element_type=F32
            ).astype(LOW)
            row_block = row_block.reshape(blocks * capacity, width)
            grad_block = grad_block.reshape(blocks * capacity, width)
            row_gate = jnp.sum(
                jnp.where(select[:, e], gate_local[:, e, None, :], 0.0), axis=2
            ).reshape(blocks * capacity, 1)
            gate_part = product(row_block, expert_gate[e])
            up_part = product(row_block, expert_up[e])
            silu_part, slope = silu_parts(gate_part)
            hidden = silu_part * up_part
            hidden_low = hidden.astype(LOW)
            result = (row_gate * product(hidden_low, expert_down[e])).astype(LOW)
            back = back_product(grad_block, expert_down[e])
            gate_grad = jnp.sum(hidden_low.astype(F32) * back, axis=1).reshape(
                blocks, capacity, 1
            )
            back = back * row_gate
            grad_gate = (back * up_part * slope).astype(LOW)
            grad_up = (back * silu_part).astype(LOW)
            weighted_hidden = (hidden_low.astype(F32) * row_gate).astype(LOW)
            grad_row = (
                back_product(grad_gate, expert_gate[e]) + back_product(grad_up, expert_up[e])
            ).astype(LOW)
            out_sum = out_sum + jnp.einsum(
                "brt,brd->btd",
                pick,
                result.reshape(blocks, capacity, width),
                preferred_element_type=F32,
            )
            back_sum = back_sum + jnp.einsum(
                "brt,brd->btd",
                pick,
                grad_row.reshape(blocks, capacity, width),
                preferred_element_type=F32,
            )
            gate_grads.append(jnp.sum(jnp.where(select[:, e], gate_grad, 0.0), axis=1))
            grad_experts.append(
                (
                    outer_sum(row_block, grad_gate),
                    outer_sum(row_block, grad_up),
                    outer_sum(weighted_hidden, grad_block),
                )
            )
    grad_expert_gate = jnp.stack([g[0] for g in grad_experts])
    grad_expert_up = jnp.stack([g[1] for g in grad_experts])
    grad_expert_down = jnp.stack([g[2] for g in grad_experts])

    def to_tokens(sums):
        parts = sums.reshape(shards, owners, rows, -1)
        mine = sum_parts([parts[s] for s in range(shards)], LOW)
        return lax.psum_scatter(mine.astype(LOW), "expert", scatter_dimension=0).astype(F32)

    with jax.named_scope("to_tokens"):
        grad_from_experts = to_tokens(back_sum.astype(LOW))
        gate_grid = jnp.stack(gate_grads, axis=-1).reshape(shards, owners, rows, local_count)
        gate_grid = sum_parts([gate_grid[s] for s in range(shards)], F32)
        grad_gates = lax.all_to_all(gate_grid, "expert", split_axis=0, concat_axis=0, tiled=True)
        grad_gates = jnp.swapaxes(grad_gates, 0, 1).reshape(rows, all_experts)
        moe_out = to_tokens(out_sum.astype(LOW))
        layer_out = (resid + moe_out).astype(LOW)

    with jax.named_scope("feed_backward"):
        grad_out = cotangent.astype(F32)
        hit_own = hit_all.reshape(blocks, rows, all_experts)
        hit_own = lax.dynamic_index_in_dim(hit_own, chip, 0, keepdims=False)
        sig = jax.nn.sigmoid(product(ffn_low, router_full))
        chosen = sig * hit_own
        own_sum = jnp.sum(chosen, axis=1, keepdims=True)
        inner = jnp.sum(grad_gates * chosen, axis=1, keepdims=True)
        grad_chosen = ROUTE_SCALE * (grad_gates / own_sum - inner / (own_sum * own_sum))
        grad_logits = (grad_chosen * hit_own * sig * (1.0 - sig)).astype(LOW)
        grad_ffn = back_product(grad_logits, router_full) + grad_from_experts
        grad_resid_part, feed_terms = norm_back(resid, resid_scale, feed_gain_full, grad_ffn)
        grad_resid = grad_out + grad_resid_part
        grad_attended = grad_resid.astype(LOW)
        feed_gain_delta = jnp.sum(feed_terms, axis=0)

    def over_chips(delta):
        mine = lax.psum_scatter(delta.astype(LOW), "expert", scatter_dimension=0, tiled=True)
        return lax.all_gather(mine, "expert", axis=0, tiled=True).astype(F32)

    with jax.named_scope("attention_backward"):
        attended_grads = jnp.concatenate(relative(grad_attended), axis=0)
        logit_grads = jnp.concatenate(relative(grad_logits), axis=0)
        grad_attention_out = over_chips(outer_sum(mixed, attended_grads))
        ffn_sequence = lax.dynamic_index_in_dim(ffn_all, chip, 1, keepdims=False)
        ffn_sequence = cut(ffn_sequence.reshape(span, width), 1)[0]
        delta_router = outer_sum(ffn_sequence, logit_grads)
        grad_mixed = (
            back_product(attended_grads, attention_out).astype(LOW).reshape(span, own_heads, VDIM)
        )
        grad_probs = jnp.einsum("qhv,khv->hqk", grad_mixed, values, preferred_element_type=F32)
        row_delta = jnp.sum(grad_probs * probabilities, axis=-1, keepdims=True)
        grad_raw = (score_scale * probabilities * (grad_probs - row_delta)).astype(LOW)
        grad_query_nope = jnp.einsum("hqk,khd->qhd", grad_raw, key_nope, preferred_element_type=F32)
        grad_query_rope = jnp.einsum("hqk,kr->qhr", grad_raw, key_rope, preferred_element_type=F32)
        grad_key_nope = jnp.einsum("hqk,qhd->khd", grad_raw, query_nope, preferred_element_type=F32)
        grad_key_rope = jnp.einsum("hqk,qhr->kr", grad_raw, query_rope, preferred_element_type=F32)
        grad_values = jnp.einsum("hqk,qhv->khv", p_low, grad_mixed, preferred_element_type=F32)
        grad_keys = (
            jnp.concatenate([grad_key_nope, grad_values], axis=-1)
            .reshape(span, own_heads * (NOPE + VDIM))
            .astype(LOW)
        )
        grad_query_turned = rotate(
            grad_query_rope, cosine_table[:, None, :], -sine_table[:, None, :]
        )
        grad_queries = (
            jnp.concatenate([grad_query_nope, grad_query_turned], axis=-1)
            .reshape(span, own_heads * (NOPE + ROPE))
            .astype(LOW)
        )

        def reorder(values, s):
            pieces = jnp.split(values, shards, axis=0)
            return jnp.concatenate([pieces[(t - s) % shards] for t in range(shards)], axis=0)

        def every_core(values):
            return [values] + [reorder(from_core(values, s), s) for s in range(1, shards)]

        queries_back = natural(every_core(grad_queries), 1)
        keys_back = natural(every_core(grad_keys), 1)
        rope_back = total(every_core(grad_key_rope))
        grad_latent_normed = natural([back_product(keys_back, w) for w in latent_up_parts], 1)
        grad_latent_part, latent_terms = norm_back(
            latent_c, latent_scale, latent_gain_full, grad_latent_normed
        )
        grad_latent = jnp.concatenate(
            [grad_latent_part, rotate(rope_back, cosine_table, -sine_table)], axis=-1
        ).astype(LOW)
        grad_query_normed = natural([back_product(queries_back, w) for w in query_up_parts], 1)
        grad_query_part, query_terms = norm_back(
            query_latent, query_scale, query_gain_full, grad_query_normed
        )
        grad_query_latent = grad_query_part.astype(LOW)
        grad_query_up = over_chips(outer_sum(query_low_parts[0], queries_back))
        grad_latent_up = over_chips(outer_sum(latent_low_parts[0], keys_back))
        grad_query_down = over_chips(outer_sum(normed_parts[0], grad_query_latent))
        grad_latent_down = over_chips(outer_sum(normed_parts[0], grad_latent))
        grad_router = over_chips(delta_router)
        grad_normed = jnp.concatenate(
            [
                back_product(grad_query_latent[:rows], a) + back_product(grad_latent[:rows], b)
                for a, b in zip(query_down_parts, latent_down_parts)
            ],
            axis=1,
        )
        grad_source, attention_terms = norm_back(
            source[:rows], source_scale[:rows], gain_rel, grad_normed
        )
        grad_tokens = grad_resid + natural(jnp.split(grad_source, shards, axis=1), 1)

    with jax.named_scope("gain_gradients"):
        attention_delta = jnp.split(jnp.sum(attention_terms, axis=0), shards)
        feed_delta = cut(feed_gain_delta, 0)
        both = sum_parts(
            [jnp.concatenate([a, f]) for a, f in zip(attention_delta, feed_delta)], F32
        )
        query_delta = cut(jnp.sum(query_terms, axis=0), 0)[0]
        latent_delta = cut(jnp.sum(latent_terms, axis=0), 0)[0]
        gains = lax.psum(jnp.concatenate([both, query_delta, latent_delta]), "expert")
        sizes = [part_cols, part_cols, query_gain.shape[0], latent_gain.shape[0]]
        marks = [0]
        for size in sizes:
            marks.append(marks[-1] + size)
        grad_attention_gain, grad_feed_gain, grad_query_gain, grad_latent_gain = [
            gains[a:b] for a, b in zip(marks, marks[1:])
        ]

    return (
        layer_out,
        grad_tokens,
        grad_attention_gain,
        grad_query_down,
        grad_query_gain,
        grad_query_up,
        grad_latent_down,
        grad_latent_gain,
        grad_latent_up,
        grad_attention_out,
        grad_feed_gain,
        grad_router,
        grad_shared_gate,
        grad_shared_up,
        grad_shared_down,
        grad_expert_gate,
        grad_expert_up,
        grad_expert_down,
    )


def solution(mesh):
    tokens_spec = P(("expert", "shard"), None)
    rows_spec = P("shard", None)
    gain_spec = P("shard")
    expert_specs = (
        P("expert", None, "shard"),
        P("expert", None, "shard"),
        P("expert", "shard", None),
    )
    weight_specs = (
        gain_spec,
        rows_spec,
        gain_spec,
        rows_spec,
        rows_spec,
        gain_spec,
        rows_spec,
        rows_spec,
        gain_spec,
        rows_spec,
        rows_spec,
        rows_spec,
        rows_spec,
    ) + expert_specs
    return jax.shard_map(
        local,
        mesh=mesh,
        in_specs=(tokens_spec, tokens_spec, P("expert"), tokens_spec) + weight_specs,
        out_specs=(tokens_spec, tokens_spec) + weight_specs,
        check_vma=False,
    )
```

```python
import jax
import jax.numpy as jnp
import functools

from jax import lax
from jax.experimental import pallas as pl
from jax.experimental.pallas import tpu as pltpu
from jax.sharding import PartitionSpec as P

HEADS = 16
NOPE = 128
ROPE = 64
VDIM = 128
KVL = 512
TOP = 6

EPS = 1e-06
ROUTE_SCALE = 2.446
ROPE_BASE = 50000.0
NEG = -1e30

LOW = jnp.bfloat16
F32 = jnp.float32

LANES = 128
ROW_TILE = 256
ROW_STEP = 16
VMEM_BYTES = 56 << 20


def tables(positions, rope_width):
    half_width = rope_width // 2
    frequencies = ROPE_BASE ** (-2.0 * jnp.arange(half_width, dtype=F32) / rope_width)
    angles = positions.astype(F32)[:, None] * frequencies[None, :]
    return (jnp.cos(angles), jnp.sin(angles))


def rotate(values, cosine_table, sine_table):
    half_width = values.shape[-1] // 2
    first_half = values[..., :half_width]
    second_half = values[..., half_width:]
    return jnp.concatenate(
        [
            first_half * cosine_table - second_half * sine_table,
            second_half * cosine_table + first_half * sine_table,
        ],
        axis=-1,
    )


def product(left_side, right_side):
    return jnp.dot(left_side, right_side, preferred_element_type=F32)


def outer_sum(left_side, right_side):
    return lax.dot_general(
        left_side, right_side, (((0,), (0,)), ((), ())), preferred_element_type=F32
    )


def back_product(left_side, right_side):
    return lax.dot_general(
        left_side, right_side, (((1,), (1,)), ((), ())), preferred_element_type=F32
    )


def total(terms):
    result = terms[0]
    for term in terms[1:]:
        result = result + term
    return result


def inverse_rms(values):
    return lax.rsqrt(jnp.mean(values * values, axis=-1, keepdims=True) + EPS)


def norm_back(values, scale, gain, grad):
    weighted = grad * gain
    inner = jnp.mean(weighted * values, axis=-1, keepdims=True)
    return scale * weighted - values * (scale * scale * scale) * inner, grad * values * scale


def silu_parts(gate_part):
    sig = jax.nn.sigmoid(gate_part)
    return gate_part * sig, sig * (1.0 + gate_part * (1.0 - sig))


def fetch_group(parts, buffers, sems, slot, q, ring, rows):
    col, step = q // ring, q % ring
    for kind, (arrays, buffer) in enumerate(zip(parts, buffers)):
        for s, (own, side_x, side_y, left, right) in enumerate(arrays):
            sem = sems.at[slot, kind, s]
            half = left.shape[-1]
            here = buffer.at[slot, pl.ds(s * rows, rows)]
            for number, array in enumerate((own, side_x, side_y)):

                @pl.when(col == number)
                def _(array=array, here=here, sem=sem):
                    pltpu.make_async_copy(array.at[step], here, sem).start()

            @pl.when(col == 3)
            def _(here=here, sem=sem, left=left, right=right, half=half):
                pltpu.make_async_copy(left.at[step], here.at[:, pl.ds(0, half)], sem).start()
                pltpu.make_async_copy(
                    right.at[step], here.at[:, pl.ds(half, right.shape[-1])], sem
                ).start()


def wait_group(parts, buffers, sems, slot, rows):
    for kind, (arrays, buffer) in enumerate(zip(parts, buffers)):
        for s, array in enumerate(arrays):
            here = buffer.at[slot, pl.ds(s * rows, rows)]
            pltpu.make_async_copy(array[0].at[0], here, sems.at[slot, kind, s]).wait()


def dispatch_kernel(ring, shards, rows, room, offsets, first, hits, pos, router_t, pair_w, down_w, *rest):
    x_parts = [rest[5 * s : 5 * s + 5] for s in range(shards)]
    g_parts = [rest[5 * (shards + s) : 5 * (shards + s) + 5] for s in range(shards)]
    rest = rest[10 * shards :]
    x_rows, g_rows, row_gates, feats, hiddens, delta_pair, delta_down = rest[:7]
    x_buf, g_buf, in_sem, x_stage, g_stage, gate_stage, out_sem, zeros, zero_gates, acc_pair, acc_down = rest[7:]
    parts, buffers = (x_parts, g_parts), (x_buf, g_buf)
    q, count = pl.program_id(0), pl.num_programs(0)
    slot = lax.rem(q, 2)
    local_count = pos.shape[1]
    width = down_w.shape[0]

    @pl.when(q == 0)
    def _():
        fetch_group(parts, buffers, in_sem, 0, 0, ring, rows)
        acc_pair[...] = jnp.zeros_like(acc_pair)
        acc_down[...] = jnp.zeros_like(acc_down)
        zeros[...] = jnp.zeros_like(zeros)
        zero_gates[...] = jnp.zeros_like(zero_gates)

    @pl.when(q + 1 < count)
    def _():
        fetch_group(parts, buffers, in_sem, 1 - slot, q + 1, ring, rows)

    wait_group(parts, buffers, in_sem, slot, rows)
    x, g = x_buf[slot], g_buf[slot]

    sig = jax.nn.sigmoid(back_product(router_t[...], x))
    chosen = sig * hits[0]
    gates = ROUTE_SCALE * chosen / jnp.sum(chosen, axis=0, keepdims=True)
    numbers = lax.broadcasted_iota(jnp.int32, gates.shape, 0)
    places = lax.broadcasted_iota(jnp.int32, (room, x.shape[0]), 0)
    picks = []
    for e in range(local_count):
        gate = jnp.sum(jnp.where(numbers == first[0] + e, gates, 0.0), axis=0, keepdims=True)
        pick = places == pos[0, e : e + 1]
        row_gate = jnp.sum(jnp.where(pick, gate, 0.0), axis=1, keepdims=True)
        gate_stage[slot, e] = jnp.broadcast_to(row_gate, (room, LANES))
        picks.append(jnp.where(pick, 1.0, 0.0).astype(LOW))
    picks = jnp.concatenate(picks, axis=0)
    x_stage[slot] = product(picks, x).astype(LOW).reshape(local_count, room, -1)
    g_stage[slot] = product(picks, g).astype(LOW).reshape(local_count, room, -1)

    def writes(which, at):
        start = [pl.multiple_of(offsets[e * count + at], ROW_STEP) for e in range(local_count)]
        return [
            pltpu.make_async_copy(
                stage.at[which, e], array.at[e, pl.ds(start[e], room)], out_sem.at[which, k, e]
            )
            for e in range(local_count)
            for k, (stage, array) in enumerate(
                ((x_stage, x_rows), (g_stage, g_rows), (gate_stage, row_gates))
            )
        ]

    @pl.when(q > 0)
    def _():
        for copy in writes(1 - slot, q - 1):
            copy.wait()

    for copy in writes(slot, q):
        copy.start()

    both = back_product(x, pair_w[...])
    gate_part, up_part = both[:, :width], both[:, width:]
    silu_part, slope = silu_parts(gate_part)
    hidden = (silu_part * up_part).astype(LOW)
    back = back_product(g, down_w[...])
    feat = jnp.concatenate(
        [(back * up_part * slope).astype(LOW), (back * silu_part).astype(LOW)], axis=1
    )
    feats[...] = feat
    hiddens[...] = hidden
    acc_pair[...] += outer_sum(feat, x)
    acc_down[...] += outer_sum(hidden, g)

    @pl.when(q == count - 1)
    def _():
        for copy in writes(slot, q):
            copy.wait()
        tails = []
        for e in range(local_count):
            end = pl.multiple_of(offsets[local_count * count + e], ROW_STEP)
            for k, (stage, array) in enumerate(
                ((zeros, x_rows), (zeros, g_rows), (zero_gates, row_gates))
            ):
                tails.append(
                    pltpu.make_async_copy(
                        stage, array.at[e, pl.ds(end, ROW_TILE)], out_sem.at[slot, k, e]
                    )
                )
        for copy in tails:
            copy.start()
        delta_pair[...] = acc_pair[...].astype(LOW)
        delta_down[...] = acc_down[...].astype(LOW)
        for copy in tails:
            copy.wait()


def expert_kernel(totals, first, x, g, row_gate, w_gate, w_up, w_down, result, grad_row, grad_gate, grad_up, weighted, gate_grad):
    e, t = pl.program_id(0), pl.program_id(1)

    @pl.when(t * ROW_TILE < totals[e])
    def _():
        gate = row_gate[0][:, :1]
        gate_part = product(x[0], w_gate[0])
        up_part = product(x[0], w_up[0])
        silu_part, slope = silu_parts(gate_part)
        hidden = (silu_part * up_part).astype(LOW)
        back = back_product(g[0], w_down[0])
        wide = hidden.astype(F32)
        own = jnp.sum(wide * back, axis=1, keepdims=True)
        lanes = lax.broadcasted_iota(jnp.int32, (ROW_TILE, LANES), 1)
        gate_grad[0] = jnp.where(lanes == first[0] + e, own, 0.0)
        back = back * gate
        low_gate = (back * up_part * slope).astype(LOW)
        low_up = (back * silu_part).astype(LOW)
        grad_gate[0] = low_gate
        grad_up[0] = low_up
        weighted[0] = (wide * gate).astype(LOW)
        grad_row[0] = (
            back_product(low_gate, w_gate[0]) + back_product(low_up, w_up[0])
        ).astype(LOW)
        result[0] = (gate * product(hidden, w_down[0])).astype(LOW)


def delta_kernel(totals, x, g, grad_gate, grad_up, weighted, delta_gate, delta_up, delta_down):
    e, t = pl.program_id(0), pl.program_id(1)

    @pl.when(t == 0)
    def _():
        delta_gate[...] = jnp.zeros_like(delta_gate)
        delta_up[...] = jnp.zeros_like(delta_up)
        delta_down[...] = jnp.zeros_like(delta_down)

    @pl.when(t * ROW_TILE < totals[e])
    def _():
        delta_gate[0] += outer_sum(x[0], grad_gate[0])
        delta_up[0] += outer_sum(x[0], grad_up[0])
        delta_down[0] += outer_sum(weighted[0], g[0])


def combine_kernel(base, count, room, shards, with_gates, offsets, counts, rows_all, gates_all, pos, feat, weight, *rest):
    outs, rest = rest[:shards], rest[shards:]
    if with_gates:
        gate_out, rest = rest[0], rest[1:]
    rows_buf, gates_buf, sems = rest
    step, steps = pl.program_id(0), pl.num_programs(0)
    slot = lax.rem(step, 2)
    local_count = rows_all.shape[0]

    def reads(which, at):
        copies = []
        for e in range(local_count):
            start = pl.multiple_of(offsets[e * count + base + at], ROW_STEP)
            copies.append(
                pltpu.make_async_copy(
                    rows_all.at[e, pl.ds(start, room)], rows_buf.at[which, e], sems.at[which, 0, e]
                )
            )
            if with_gates:
                copies.append(
                    pltpu.make_async_copy(
                        gates_all.at[e, pl.ds(start, room)],
                        gates_buf.at[which, e],
                        sems.at[which, 1, e],
                    )
                )
        return copies

    @pl.when(step == 0)
    def _():
        for copy in reads(0, 0):
            copy.start()

    @pl.when(step + 1 < steps)
    def _():
        for copy in reads(1 - slot, step + 1):
            copy.start()

    for copy in reads(slot, step):
        copy.wait()

    tokens = pos.shape[1]
    places = lax.broadcasted_iota(jnp.int32, (tokens, room), 1)
    row_ids = lax.broadcasted_iota(jnp.int32, (room, 1), 0)
    total_rows = product(feat[...], weight[...])
    gate_sum = None
    for e in range(local_count):
        valid = row_ids < counts[e * count + base + step]
        pick = places == pos[0][:, e : e + 1]
        rows = jnp.where(valid, rows_buf[slot, e], jnp.zeros((), LOW))
        total_rows += product(jnp.where(pick, 1.0, 0.0).astype(LOW), rows)
        if with_gates:
            gates = jnp.where(valid, gates_buf[slot, e], 0.0)
            term = jnp.dot(
                jnp.where(pick, 1.0, 0.0),
                gates,
                preferred_element_type=F32,
                precision=lax.Precision.HIGHEST,
            )
            gate_sum = term if gate_sum is None else gate_sum + term
    low = total_rows.astype(LOW)
    share = tokens // shards
    for s in range(shards):
        outs[s][0] = low[s * share : (s + 1) * share]
    if with_gates:
        gate_out[0] = gate_sum


def assemble_kernel(ring, order, own, side_x, side_y, left, right, out):
    col = pl.program_id(0) // ring
    for number, array in enumerate((own, side_x, side_y)):

        @pl.when(col == number)
        def _(array=array):
            out[0] = array[0].astype(out.dtype)

    @pl.when(col == 3)
    def _():
        out[0] = jnp.concatenate([left[0], right[0]], axis=-1).astype(out.dtype)


def params(*semantics):
    return pltpu.CompilerParams(dimension_semantics=semantics, vmem_limit_bytes=VMEM_BYTES)


def assemble(ring, order, arrays, kind):
    owners = 4 * ring
    rows, cols = arrays[0].shape[1:]

    def spec(number, width):
        return pl.BlockSpec(
            (1, rows, width), lambda q, order: (jnp.clip(q - number * ring, 0, ring - 1), 0, 0)
        )

    return pl.pallas_call(
        functools.partial(assemble_kernel, ring),
        grid_spec=pltpu.PrefetchScalarGridSpec(
            num_scalar_prefetch=1,
            grid=(owners,),
            in_specs=[
                spec(0, cols),
                spec(1, cols),
                spec(2, cols),
                spec(3, arrays[3].shape[2]),
                spec(3, arrays[4].shape[2]),
            ],
            out_specs=pl.BlockSpec((1, rows, cols), lambda q, order: (order[q], 0, 0)),
        ),
        out_shape=jax.ShapeDtypeStruct((owners, rows, cols), kind),
        compiler_params=params("arbitrary"),
        cost_estimate=pl.CostEstimate(
            flops=0, bytes_accessed=owners * rows * cols * 6, transcendentals=0
        ),
    )(order, *arrays)


def dispatch(ring, shards, rows, room, offsets, first, hits, pos, router_t, pair_w, down_w, x_parts, g_parts):
    owners, all_experts, span = hits.shape
    local_count = pos.shape[1]
    width = router_t.shape[1]
    hidden = down_w.shape[0]
    capacity = owners * room + ROW_TILE
    flat = [a for part in x_parts for a in part] + [a for part in g_parts for a in part]
    whole = lambda q, *_: (0, 0)
    anywhere = pl.BlockSpec(memory_space=pl.ANY)
    return pl.pallas_call(
        functools.partial(dispatch_kernel, ring, shards, rows, room),
        grid_spec=pltpu.PrefetchScalarGridSpec(
            num_scalar_prefetch=2,
            grid=(owners,),
            in_specs=[
                pl.BlockSpec((1, all_experts, span), lambda q, *_: (q, 0, 0)),
                pl.BlockSpec((1, local_count, span), lambda q, *_: (q, 0, 0)),
                pl.BlockSpec((all_experts, width), whole),
                pl.BlockSpec((2 * hidden, width), whole),
                pl.BlockSpec((hidden, width), whole),
            ]
            + [anywhere] * len(flat),
            out_specs=[
                anywhere,
                anywhere,
                anywhere,
                pl.BlockSpec((span, 2 * hidden), lambda q, *_: (q, 0)),
                pl.BlockSpec((span, hidden), lambda q, *_: (q, 0)),
                pl.BlockSpec((2 * hidden, width), whole),
                pl.BlockSpec((hidden, width), whole),
            ],
            scratch_shapes=[
                pltpu.VMEM((2, span, width), LOW),
                pltpu.VMEM((2, span, width), LOW),
                pltpu.SemaphoreType.DMA((2, 2, shards)),
                pltpu.VMEM((2, local_count, room, width), LOW),
                pltpu.VMEM((2, local_count, room, width), LOW),
                pltpu.VMEM((2, local_count, room, LANES), F32),
                pltpu.SemaphoreType.DMA((2, 3, local_count)),
                pltpu.VMEM((ROW_TILE, width), LOW),
                pltpu.VMEM((ROW_TILE, LANES), F32),
                pltpu.VMEM((2 * hidden, width), F32),
                pltpu.VMEM((hidden, width), F32),
            ],
        ),
        out_shape=[
            jax.ShapeDtypeStruct((local_count, capacity, width), LOW),
            jax.ShapeDtypeStruct((local_count, capacity, width), LOW),
            jax.ShapeDtypeStruct((local_count, capacity, LANES), F32),
            jax.ShapeDtypeStruct((owners * span, 2 * hidden), LOW),
            jax.ShapeDtypeStruct((owners * span, hidden), LOW),
            jax.ShapeDtypeStruct((2 * hidden, width), LOW),
            jax.ShapeDtypeStruct((hidden, width), LOW),
        ],
        compiler_params=params("arbitrary"),
        cost_estimate=pl.CostEstimate(
            flops=14 * owners * span * width * span,
            bytes_accessed=4 * owners * span * width,
            transcendentals=0,
        ),
    )(offsets, first, hits, pos, router_t, pair_w, down_w, *flat)


def tile_map(e, t, totals, *_):
    last = jnp.maximum((totals[e] + ROW_TILE - 1) // ROW_TILE - 1, 0)
    return (e, jnp.minimum(t, last), 0)


def expert_map(e, t, *_):
    return (e, 0, 0)


def run_experts(totals, first, x, g, row_gate, w_gate, w_up, w_down):
    local_count, capacity, width = x.shape
    hidden = w_gate.shape[2]
    tiles = capacity // ROW_TILE
    wide = pl.BlockSpec((1, ROW_TILE, width), tile_map)
    slim = pl.BlockSpec((1, ROW_TILE, hidden), tile_map)
    lane = pl.BlockSpec((1, ROW_TILE, LANES), tile_map)
    return pl.pallas_call(
        expert_kernel,
        grid_spec=pltpu.PrefetchScalarGridSpec(
            num_scalar_prefetch=2,
            grid=(local_count, tiles),
            in_specs=[
                wide,
                wide,
                lane,
                pl.BlockSpec((1, width, hidden), expert_map),
                pl.BlockSpec((1, width, hidden), expert_map),
                pl.BlockSpec((1, hidden, width), expert_map),
            ],
            out_specs=[wide, wide, slim, slim, slim, lane],
        ),
        out_shape=[
            jax.ShapeDtypeStruct(x.shape, LOW),
            jax.ShapeDtypeStruct(x.shape, LOW),
            jax.ShapeDtypeStruct((local_count, capacity, hidden), LOW),
            jax.ShapeDtypeStruct((local_count, capacity, hidden), LOW),
            jax.ShapeDtypeStruct((local_count, capacity, hidden), LOW),
            jax.ShapeDtypeStruct(row_gate.shape, F32),
        ],
        compiler_params=params("arbitrary", "arbitrary"),
        cost_estimate=pl.CostEstimate(
            flops=6 * local_count * capacity * width * hidden,
            bytes_accessed=6 * local_count * width * (capacity + hidden),
            transcendentals=0,
        ),
    )(totals, first, x, g, row_gate, w_gate, w_up, w_down)


def run_deltas(totals, x, g, grad_gate, grad_up, weighted):
    local_count, capacity, width = x.shape
    hidden = grad_gate.shape[2]
    tiles = capacity // ROW_TILE
    wide = pl.BlockSpec((1, ROW_TILE, width), tile_map)
    slim = pl.BlockSpec((1, ROW_TILE, hidden), tile_map)
    return pl.pallas_call(
        delta_kernel,
        grid_spec=pltpu.PrefetchScalarGridSpec(
            num_scalar_prefetch=1,
            grid=(local_count, tiles),
            in_specs=[wide, wide, slim, slim, slim],
            out_specs=[
                pl.BlockSpec((1, width, hidden), expert_map),
                pl.BlockSpec((1, width, hidden), expert_map),
                pl.BlockSpec((1, hidden, width), expert_map),
            ],
        ),
        out_shape=[
            jax.ShapeDtypeStruct((local_count, width, hidden), F32),
            jax.ShapeDtypeStruct((local_count, width, hidden), F32),
            jax.ShapeDtypeStruct((local_count, hidden, width), F32),
        ],
        compiler_params=params("arbitrary", "arbitrary"),
        cost_estimate=pl.CostEstimate(
            flops=3 * local_count * capacity * width * hidden,
            bytes_accessed=12 * local_count * width * hidden,
            transcendentals=0,
        ),
    )(totals, x, g, grad_gate, grad_up, weighted)


def combine(col, ring, rows, shards, room, offsets, counts, rows_all, gates_all, pos, feat, weight):
    local_count, capacity, width = rows_all.shape
    owners, span = pos.shape[:2]
    base = col * ring
    with_gates = gates_all is not None
    out_shape = [jax.ShapeDtypeStruct((ring, rows, width), LOW)] * shards
    out_specs = [pl.BlockSpec((1, rows, width), lambda q, *_: (q, 0, 0))] * shards
    if with_gates:
        out_shape = out_shape + [jax.ShapeDtypeStruct((ring, span, LANES), F32)]
        out_specs = out_specs + [pl.BlockSpec((1, span, LANES), lambda q, *_: (q, 0, 0))]
    return pl.pallas_call(
        functools.partial(combine_kernel, base, owners, room, shards, with_gates),
        grid_spec=pltpu.PrefetchScalarGridSpec(
            num_scalar_prefetch=2,
            grid=(ring,),
            in_specs=[
                pl.BlockSpec(memory_space=pl.ANY),
                pl.BlockSpec(memory_space=pl.ANY),
                pl.BlockSpec((1, span, local_count), lambda q, *_: (base + q, 0, 0)),
                pl.BlockSpec((span, feat.shape[1]), lambda q, *_: (base + q, 0)),
                pl.BlockSpec(weight.shape, lambda q, *_: (0, 0)),
            ],
            out_specs=out_specs,
            scratch_shapes=[
                pltpu.VMEM((2, local_count, room, width), LOW),
                pltpu.VMEM((2, local_count, room, LANES), F32),
                pltpu.SemaphoreType.DMA((2, 2, local_count)),
            ],
        ),
        out_shape=out_shape,
        compiler_params=params("arbitrary"),
        cost_estimate=pl.CostEstimate(
            flops=4 * ring * span * width * span,
            bytes_accessed=4 * ring * span * width,
            transcendentals=0,
        ),
    )(offsets, counts, rows_all, gates_all if with_gates else rows_all, pos, feat, weight)


def local(
    tokens,
    cotangent,
    seq_len,
    routes,
    attention_gain,
    query_down,
    query_gain,
    query_up,
    latent_down,
    latent_gain,
    latent_up,
    attention_out,
    feedforward_gain,
    router,
    shared_gate,
    shared_up,
    shared_down,
    expert_gate,
    expert_up,
    expert_down,
):
    rows, width = tokens.shape
    shards = lax.axis_size("shard")
    owners = lax.axis_size("expert")
    core = lax.axis_index("shard")
    chip = lax.axis_index("expert")
    local_count = expert_gate.shape[0]
    all_experts = local_count * owners
    capacity = 2 * rows * TOP // all_experts
    span = rows * shards
    blocks = shards * owners
    own_heads = HEADS // shards
    part_cols = width // shards

    def place(s):
        return (core - s) % shards

    def from_core(values, s):
        return lax.ppermute(values, "shard", [(i, (i + s) % shards) for i in range(shards)])

    def to_core(values, s):
        return lax.ppermute(values, "shard", [(i, (i - s) % shards) for i in range(shards)])

    def relative(values):
        return [values] + [from_core(values, s) for s in range(1, shards)]

    def sum_parts(parts, kind):
        got = [to_core(parts[s].astype(kind), s).astype(F32) for s in range(1, shards)]
        return total([parts[0].astype(F32)] + got)

    ring = owners // 4
    z_at, y_at, x_at = chip // 4, chip // 2 % 2, chip % 2

    def send(values, dz=0, dy=0, dx=0):
        pairs = []
        for i in range(owners):
            z, y, x = i // 4, i // 2 % 2, i % 2
            pairs.append((i, (z + dz) % ring * 4 + (y ^ dy) * 2 + (x ^ dx)))
        return lax.ppermute(values, "expert", pairs)

    slot_chip = jnp.stack(
        [
            (z_at - k) % ring * 4 + (y_at ^ (col // 2)) * 2 + (x_at ^ (col % 2))
            for col in range(4)
            for k in range(ring)
        ]
    ).astype(jnp.int32)

    def middle(values):
        return max(values.shape[-1] // 2 // LANES * LANES, 1)

    def gather_plane(own):
        half = middle(own)
        side_x, side_y = send(own, dx=1), send(own, dy=1)
        left = send(side_y[..., :half], dx=1)
        right = send(side_x[..., half:], dy=1)
        return [own, side_x, side_y, left, right]

    def gather_chips(values):
        return gather_plane(jnp.stack([values] + [send(values, dz=k) for k in range(1, ring)]))

    def scatter_plane(own, side_x, side_y, both):
        half = middle(own)
        for_y = send(both[..., :half], dx=1)
        for_x = send(both[..., half:], dy=1)
        side_y = jnp.concatenate([side_y[..., :half] + for_y, side_y[..., half:]], axis=-1)
        side_x = jnp.concatenate([side_x[..., :half], side_x[..., half:] + for_x], axis=-1)
        got_x, got_y = send(side_x, dx=1), send(side_y, dy=1)
        return (own.astype(F32) + got_x.astype(F32) + got_y.astype(F32)).astype(LOW)

    def scatter_ring(parts):
        got = [send(parts[k], dz=-k) for k in range(1, ring)]
        return total([parts[0].astype(F32)] + [v.astype(F32) for v in got])

    def sum_chips(values):
        values = values + send(values, dx=1)
        values = values + send(values, dy=1)
        return total([values] + [send(values, dz=k) for k in range(1, ring)])

    def over_chips(delta):
        grid = delta.astype(LOW).reshape(ring, 2, 2, delta.shape[0] // owners, delta.shape[1])

        def column(dy, dx):
            at = lax.dynamic_index_in_dim(grid, y_at ^ dy, 1, keepdims=False)
            return lax.dynamic_index_in_dim(at, x_at ^ dx, 1, keepdims=False)

        mine = scatter_plane(column(0, 0), column(0, 1), column(1, 0), column(1, 1))
        mine = scatter_ring(
            [
                lax.dynamic_index_in_dim(mine, (z_at - k) % ring, 0, keepdims=False)
                for k in range(ring)
            ]
        ).astype(LOW)
        return assemble(ring, slot_chip, gather_chips(mine), F32).reshape(delta.shape)

    def cut(values, axis):
        size = values.shape[axis] // shards
        return [
            lax.dynamic_slice_in_dim(values, place(s) * size, size, axis) for s in range(shards)
        ]

    def natural(parts, axis):
        pieces = []
        for i in range(shards):
            piece = parts[0]
            for s in range(1, shards):
                piece = jnp.where(place(s) == i, parts[s], piece)
            pieces.append(piece)
        return jnp.concatenate(pieces, axis=axis)

    with jax.named_scope("early_gathers"):
        token_parts = relative(tokens)
        gains_own = jnp.concatenate([attention_gain, query_gain, latent_gain, feedforward_gain])
        gain_parts = relative(gains_own)
        query_down_parts = relative(query_down)
        latent_down_parts = relative(latent_down)
        query_up_parts = relative(query_up)
        latent_up_parts = relative(latent_up)
        router_parts = relative(router)
        grad_parts = list(zip(*[relative(v) for v in gather_chips(cotangent)]))
        routes_own = sum_chips(
            jnp.zeros((owners, TOP, rows), jnp.int32).at[chip].set(routes.T)
        )

    hidden_all = shared_gate.shape[1]
    hidden_own = hidden_all // blocks
    hidden_shard = hidden_all // shards

    def shared_columns(weight):
        pieces = [
            lax.dynamic_slice_in_dim(
                weight, place(s) * hidden_shard + chip * hidden_own, hidden_own, 1
            ).T
            for s in range(shards)
        ]
        got = [pieces[0]] + [None] * (shards - 1)
        for s in range(1, shards):
            got[shards - s] = to_core(pieces[s], s)
        return natural(got, 1)

    with jax.named_scope("shared_weights"):
        padded = -(-hidden_own // LANES) * LANES
        pad = ((0, padded - hidden_own), (0, 0))
        pair_w = jnp.concatenate(
            [jnp.pad(shared_columns(shared_gate), pad), jnp.pad(shared_columns(shared_up), pad)]
        )
        down_w = jnp.pad(
            lax.dynamic_slice_in_dim(shared_down, chip * hidden_own, hidden_own, 0), pad
        )
        router_full = natural(router_parts, 0)

    with jax.named_scope("routing"):
        routes_all = jnp.stack(relative(routes_own), axis=2)[slot_chip].reshape(owners, TOP, span)
        expert_ids = jnp.arange(all_experts, dtype=jnp.int32)
        hits = jnp.any(
            routes_all[:, None] == expert_ids[None, :, None, None], axis=2
        )
        first = chip * local_count
        hit = lax.dynamic_slice_in_dim(hits, first, local_count, 1).astype(jnp.int32)
        pos = jnp.where(hit > 0, jnp.cumsum(hit, axis=2) - hit, -1)
        pos_cols = jnp.swapaxes(pos, 1, 2)
        room = shards * capacity
        counts = jnp.sum(hit, axis=2).T
        steps = (counts + ROW_STEP - 1) // ROW_STEP * ROW_STEP
        ends = jnp.cumsum(steps, axis=1)
        totals = ends[:, -1]
        offsets = jnp.concatenate([(ends - steps).reshape(-1), totals])
        counts = counts.reshape(-1)
        hits = hits.astype(F32)
        first_at = first.reshape(1).astype(jnp.int32)

    bounds = [0]
    for size in (part_cols, query_gain.shape[0], latent_gain.shape[0], part_cols):
        bounds.append(bounds[-1] + size)
    attention_gain_parts = [g[bounds[0] : bounds[1]].astype(F32) for g in gain_parts]
    query_gain_full = natural([g[bounds[1] : bounds[2]] for g in gain_parts], 0).astype(F32)
    latent_gain_full = natural([g[bounds[2] : bounds[3]] for g in gain_parts], 0).astype(F32)
    feed_gain_full = natural([g[bounds[3] : bounds[4]] for g in gain_parts], 0).astype(F32)
    gain_rel = jnp.concatenate(attention_gain_parts)

    with jax.named_scope("attention_forward"):
        positions = jnp.concatenate(
            [place(s) * rows + jnp.arange(rows, dtype=jnp.int32) for s in range(shards)]
        )
        cosine_table, sine_table = tables(positions, ROPE)
        length = seq_len[0]
        sequence = jnp.concatenate(token_parts, axis=0)
        source = jnp.concatenate(cut(sequence, 1), axis=1).astype(F32)
        source_scale = inverse_rms(source)
        normed = (source * source_scale * gain_rel).astype(LOW)
        normed_parts = jnp.split(normed, shards, axis=1)
        query_latent = total([product(a, w) for a, w in zip(normed_parts, query_down_parts)])
        query_scale = inverse_rms(query_latent)
        query_low = (query_latent * query_scale * query_gain_full).astype(LOW)
        latent = total([product(a, w) for a, w in zip(normed_parts, latent_down_parts)])
        latent_c = latent[:, :KVL]
        latent_scale = inverse_rms(latent_c)
        latent_low = (latent_c * latent_scale * latent_gain_full).astype(LOW)
        key_rope = rotate(latent[:, KVL:], cosine_table, sine_table).astype(LOW)
        query_low_parts = cut(query_low, 1)
        latent_low_parts = cut(latent_low, 1)
        query_raw = total(
            [product(a, cut(w, 1)[0]) for a, w in zip(query_low_parts, query_up_parts)]
        ).reshape(span, own_heads, NOPE + ROPE)
        query_nope = query_raw[..., :NOPE].astype(LOW)
        query_rope = rotate(
            query_raw[..., NOPE:], cosine_table[:, None, :], sine_table[:, None, :]
        ).astype(LOW)
        keys_values = (
            total([product(a, cut(w, 1)[0]) for a, w in zip(latent_low_parts, latent_up_parts)])
            .astype(LOW)
            .reshape(span, own_heads, NOPE + VDIM)
        )
        key_nope = keys_values[..., :NOPE]
        values = keys_values[..., NOPE:]
        score_scale = (NOPE + ROPE) ** (-0.5)
        allowed = (positions[None, :] <= positions[:, None]) & (positions[None, :] < length)
        raw_scores = jnp.einsum("qhd,khd->hqk", query_nope, key_nope, preferred_element_type=F32)
        raw_scores = raw_scores + jnp.einsum(
            "qhr,kr->hqk", query_rope, key_rope, preferred_element_type=F32
        )
        scores = jnp.where(allowed[None], raw_scores * score_scale, NEG)
        row_peak = jnp.max(scores, axis=-1, keepdims=True)
        exp_terms = jnp.exp(scores - row_peak)
        probabilities = exp_terms / jnp.sum(exp_terms, axis=-1, keepdims=True)
        p_low = probabilities.astype(LOW)
        mixed = jnp.einsum("hqk,khv->qhv", p_low, values, preferred_element_type=F32)
        mixed = mixed.astype(LOW).reshape(span, own_heads * VDIM)
        attended = product(mixed, attention_out)
        resid = tokens.astype(F32) + sum_parts(jnp.split(attended, shards, axis=0), F32)
        resid_scale = inverse_rms(resid)
        ffn_low = (resid * resid_scale * feed_gain_full).astype(LOW)

    with jax.named_scope("token_gather"):
        ffn_parts = list(zip(*[relative(v) for v in gather_chips(ffn_low)]))

    with jax.named_scope("dispatch"):
        x_rows, g_rows, row_gates, feats, hiddens, delta_pair, delta_down = dispatch(
            ring, shards, rows, room, offsets, first_at, hits, pos, router_full.T, pair_w, down_w,
            ffn_parts, grad_parts,
        )

    with jax.named_scope("routed_experts"):
        results, grad_rows, low_gate, low_up, weighted, gate_rows = run_experts(
            totals, first_at, x_rows, g_rows, row_gates, expert_gate, expert_up, expert_down
        )

    def to_tokens(rows_all, gates_all, feat, weight):
        cols, gate_cols = [None] * 4, [None] * 4
        for col in (3, 1, 2, 0):
            parts = combine(
                col, ring, rows, shards, room, offsets, counts, rows_all, gates_all, pos_cols,
                feat, weight,
            )
            gate_cols[col] = parts[shards:]
            cols[col] = sum_parts(parts[:shards], LOW).astype(LOW)
        return scatter_ring(scatter_plane(*cols)), gate_cols

    with jax.named_scope("to_tokens"):
        grad_from_experts, gate_cols = to_tokens(grad_rows, gate_rows, feats, pair_w)
        gate_grid = jnp.concatenate([g[0] for g in gate_cols])
        gate_grid = lax.dynamic_slice_in_dim(gate_grid, first, local_count, 2)
        gate_grid = gate_grid.reshape(owners, shards, rows, local_count)
        gate_grid = sum_parts([gate_grid[:, s] for s in range(shards)], F32)
        gate_grid = jnp.zeros_like(gate_grid).at[slot_chip].set(gate_grid)
        grad_gates = lax.all_to_all(gate_grid, "expert", split_axis=0, concat_axis=0, tiled=True)
        grad_gates = jnp.swapaxes(grad_gates, 0, 1).reshape(rows, all_experts)
        moe_out, unused = to_tokens(results, None, hiddens, down_w)
        layer_out = (resid + moe_out).astype(LOW)

    with jax.named_scope("expert_gradients"):
        grad_expert_gate, grad_expert_up, grad_expert_down = run_deltas(
            totals, x_rows, g_rows, low_gate, low_up, weighted
        )

    def shared_delta(delta):
        parts = cut(delta, 1)
        got = [parts[0]] + [None] * (shards - 1)
        for s in range(1, shards):
            got[shards - s] = to_core(parts[s], s)
        mine = natural([got[s][None] for s in range(shards)], 0)
        mine = mine.reshape(shards * hidden_own, part_cols)
        every = assemble(ring, slot_chip, gather_chips(mine), F32)
        every = every.reshape(owners, shards, hidden_own, part_cols)
        return jnp.swapaxes(every, 0, 1).reshape(hidden_all, part_cols).T

    with jax.named_scope("shared_gradients"):
        grad_shared_gate = shared_delta(delta_pair[:hidden_own])
        grad_shared_up = shared_delta(delta_pair[padded : padded + hidden_own])
        grad_shared_down = assemble(
            ring, slot_chip, gather_chips(delta_down[:hidden_own]), F32
        ).reshape(shared_down.shape)

    with jax.named_scope("feed_backward"):
        grad_out = cotangent.astype(F32)
        hit_own = jnp.any(routes[:, :, None] == expert_ids, axis=1).astype(F32)
        sig = jax.nn.sigmoid(product(ffn_low, router_full))
        chosen = sig * hit_own
        own_sum = jnp.sum(chosen, axis=1, keepdims=True)
        inner = jnp.sum(grad_gates * chosen, axis=1, keepdims=True)
        grad_chosen = ROUTE_SCALE * (grad_gates / own_sum - inner / (own_sum * own_sum))
        grad_logits = (grad_chosen * hit_own * sig * (1.0 - sig)).astype(LOW)
        grad_ffn = back_product(grad_logits, router_full) + grad_from_experts
        grad_resid_part, feed_terms = norm_back(resid, resid_scale, feed_gain_full, grad_ffn)
        grad_resid = grad_out + grad_resid_part
        grad_attended = grad_resid.astype(LOW)
        feed_gain_delta = jnp.sum(feed_terms, axis=0)

    with jax.named_scope("attention_backward"):
        attended_grads = jnp.concatenate(relative(grad_attended), axis=0)
        logit_grads = jnp.concatenate(relative(grad_logits), axis=0)
        grad_attention_out = over_chips(outer_sum(mixed, attended_grads))
        ffn_sequence = cut(jnp.concatenate([part[0][0] for part in ffn_parts]), 1)[0]
        delta_router = outer_sum(ffn_sequence, logit_grads)
        grad_mixed = (
            back_product(attended_grads, attention_out).astype(LOW).reshape(span, own_heads, VDIM)
        )
        grad_probs = jnp.einsum("qhv,khv->hqk", grad_mixed, values, preferred_element_type=F32)
        row_delta = jnp.sum(grad_probs * probabilities, axis=-1, keepdims=True)
        grad_raw = (score_scale * probabilities * (grad_probs - row_delta)).astype(LOW)
        grad_query_nope = jnp.einsum("hqk,khd->qhd", grad_raw, key_nope, preferred_element_type=F32)
        grad_query_rope = jnp.einsum("hqk,kr->qhr", grad_raw, key_rope, preferred_element_type=F32)
        grad_key_nope = jnp.einsum("hqk,qhd->khd", grad_raw, query_nope, preferred_element_type=F32)
        grad_key_rope = jnp.einsum("hqk,qhr->kr", grad_raw, query_rope, preferred_element_type=F32)
        grad_values = jnp.einsum("hqk,qhv->khv", p_low, grad_mixed, preferred_element_type=F32)
        grad_keys = (
            jnp.concatenate([grad_key_nope, grad_values], axis=-1)
            .reshape(span, own_heads * (NOPE + VDIM))
            .astype(LOW)
        )
        grad_query_turned = rotate(
            grad_query_rope, cosine_table[:, None, :], -sine_table[:, None, :]
        )
        grad_queries = (
            jnp.concatenate([grad_query_nope, grad_query_turned], axis=-1)
            .reshape(span, own_heads * (NOPE + ROPE))
            .astype(LOW)
        )

        def reorder(values, s):
            pieces = jnp.split(values, shards, axis=0)
            return jnp.concatenate([pieces[(t - s) % shards] for t in range(shards)], axis=0)

        def every_core(values):
            return [values] + [reorder(from_core(values, s), s) for s in range(1, shards)]

        queries_back = natural(every_core(grad_queries), 1)
        keys_back = natural(every_core(grad_keys), 1)
        rope_back = total(every_core(grad_key_rope))
        grad_latent_normed = natural([back_product(keys_back, w) for w in latent_up_parts], 1)
        grad_latent_part, latent_terms = norm_back(
            latent_c, latent_scale, latent_gain_full, grad_latent_normed
        )
        grad_latent = jnp.concatenate(
            [grad_latent_part, rotate(rope_back, cosine_table, -sine_table)], axis=-1
        ).astype(LOW)
        grad_query_normed = natural([back_product(queries_back, w) for w in query_up_parts], 1)
        grad_query_part, query_terms = norm_back(
            query_latent, query_scale, query_gain_full, grad_query_normed
        )
        grad_query_latent = grad_query_part.astype(LOW)
        grad_query_up = over_chips(outer_sum(query_low_parts[0], queries_back))
        grad_latent_up = over_chips(outer_sum(latent_low_parts[0], keys_back))
        grad_query_down = over_chips(outer_sum(normed_parts[0], grad_query_latent))
        grad_latent_down = over_chips(outer_sum(normed_parts[0], grad_latent))
        grad_router = sum_chips(delta_router)
        grad_normed = jnp.concatenate(
            [
                back_product(grad_query_latent[:rows], a) + back_product(grad_latent[:rows], b)
                for a, b in zip(query_down_parts, latent_down_parts)
            ],
            axis=1,
        )
        grad_source, attention_terms = norm_back(
            source[:rows], source_scale[:rows], gain_rel, grad_normed
        )
        grad_tokens = grad_resid + natural(jnp.split(grad_source, shards, axis=1), 1)

    with jax.named_scope("gain_gradients"):
        attention_delta = jnp.split(jnp.sum(attention_terms, axis=0), shards)
        feed_delta = cut(feed_gain_delta, 0)
        both = sum_parts(
            [jnp.concatenate([a, f]) for a, f in zip(attention_delta, feed_delta)], F32
        )
        query_delta = cut(jnp.sum(query_terms, axis=0), 0)[0]
        latent_delta = cut(jnp.sum(latent_terms, axis=0), 0)[0]
        gains = sum_chips(jnp.concatenate([both, query_delta, latent_delta]))
        sizes = [part_cols, part_cols, query_gain.shape[0], latent_gain.shape[0]]
        marks = [0]
        for size in sizes:
            marks.append(marks[-1] + size)
        grad_attention_gain, grad_feed_gain, grad_query_gain, grad_latent_gain = [
            gains[a:b] for a, b in zip(marks, marks[1:])
        ]

    return (
        layer_out,
        grad_tokens,
        grad_attention_gain,
        grad_query_down,
        grad_query_gain,
        grad_query_up,
        grad_latent_down,
        grad_latent_gain,
        grad_latent_up,
        grad_attention_out,
        grad_feed_gain,
        grad_router,
        grad_shared_gate,
        grad_shared_up,
        grad_shared_down,
        grad_expert_gate,
        grad_expert_up,
        grad_expert_down,
    )


def solution(mesh):
    tokens_spec = P(("expert", "shard"), None)
    rows_spec = P("shard", None)
    gain_spec = P("shard")
    expert_specs = (
        P("expert", None, "shard"),
        P("expert", None, "shard"),
        P("expert", "shard", None),
    )
    weight_specs = (
        gain_spec,
        rows_spec,
        gain_spec,
        rows_spec,
        rows_spec,
        gain_spec,
        rows_spec,
        rows_spec,
        gain_spec,
        rows_spec,
        rows_spec,
        rows_spec,
        rows_spec,
    ) + expert_specs
    return jax.shard_map(
        local,
        mesh=mesh,
        in_specs=(tokens_spec, tokens_spec, P("expert"), tokens_spec) + weight_specs,
        out_specs=(tokens_spec, tokens_spec) + weight_specs,
        check_vma=False,
    )
```

```python
import jax
import jax.numpy as jnp
import functools

from jax import lax
from jax.experimental import pallas as pl
from jax.experimental.pallas import tpu as pltpu
from jax.sharding import PartitionSpec as P

HEADS = 16
NOPE = 128
ROPE = 64
VDIM = 128
KVL = 512
TOP = 6

EPS = 1e-06
ROUTE_SCALE = 2.446
ROPE_BASE = 50000.0
NEG = -1e30

LOW = jnp.bfloat16
F32 = jnp.float32

LANES = 128
ROW_TILE = 512
HALF_TILE = 256
COL_TILE = 512
ROW_STEP = 16
VMEM_BYTES = 58 << 20


def tables(positions, rope_width):
    half_width = rope_width // 2
    frequencies = ROPE_BASE ** (-2.0 * jnp.arange(half_width, dtype=F32) / rope_width)
    angles = positions.astype(F32)[:, None] * frequencies[None, :]
    return (jnp.cos(angles), jnp.sin(angles))


def rotate(values, cosine_table, sine_table):
    half_width = values.shape[-1] // 2
    first_half = values[..., :half_width]
    second_half = values[..., half_width:]
    return jnp.concatenate(
        [
            first_half * cosine_table - second_half * sine_table,
            second_half * cosine_table + first_half * sine_table,
        ],
        axis=-1,
    )


def product(left_side, right_side):
    return jnp.dot(left_side, right_side, preferred_element_type=F32)


def outer_sum(left_side, right_side):
    return lax.dot_general(
        left_side, right_side, (((0,), (0,)), ((), ())), preferred_element_type=F32
    )


def back_product(left_side, right_side):
    return lax.dot_general(
        left_side, right_side, (((1,), (1,)), ((), ())), preferred_element_type=F32
    )


def total(terms):
    result = terms[0]
    for term in terms[1:]:
        result = result + term
    return result


def inverse_rms(values):
    return lax.rsqrt(jnp.mean(values * values, axis=-1, keepdims=True) + EPS)


def norm_back(values, scale, gain, grad):
    weighted = grad * gain
    inner = jnp.mean(weighted * values, axis=-1, keepdims=True)
    return scale * weighted - values * (scale * scale * scale) * inner, grad * values * scale


def silu_parts(gate_part):
    sig = jax.nn.sigmoid(gate_part)
    return gate_part * sig, sig * (1.0 + gate_part * (1.0 - sig))


def fetch_group(x_parts, g_parts, order, x_buf, g_buf, sems, slot, q, rows):
    for s, array in enumerate(g_parts):
        here = pl.ds(s * rows, rows)
        pltpu.make_async_copy(array.at[order[q]], g_buf.at[slot, here], sems.at[slot, 0, s]).start()
    for number in range(len(x_parts[0])):

        @pl.when(q == number)
        def _(number=number):
            for s, arrays in enumerate(x_parts):
                here = pl.ds(s * rows, rows)
                pltpu.make_async_copy(
                    arrays[number], x_buf.at[slot, here], sems.at[slot, 1, s]
                ).start()


def wait_group(x_parts, x_buf, g_buf, sems, slot, rows):
    for kind, buffer in enumerate((g_buf, x_buf)):
        for s, arrays in enumerate(x_parts):
            here = buffer.at[slot, pl.ds(s * rows, rows)]
            pltpu.make_async_copy(arrays[0], here, sems.at[slot, kind, s]).wait()


def dispatch_kernel(owners, shards, rows, room, offsets, first, order, hits, pos, router_t, pair_w, down_w, *rest):
    x_parts = [rest[owners * s : owners * (s + 1)] for s in range(shards)]
    g_parts = rest[owners * shards : (owners + 1) * shards]
    rest = rest[(owners + 1) * shards :]
    x_rows, g_rows, row_gates, feats, hiddens, delta_pair, delta_down = rest[:7]
    x_buf, g_buf, in_sem, x_stage, g_stage, gate_stage, out_sem, zeros, zero_gates, acc_pair, acc_down = rest[7:]
    q, count = pl.program_id(0), pl.num_programs(0)
    slot = lax.rem(q, 2)
    local_count = pos.shape[1]
    width = down_w.shape[0]

    @pl.when(q == 0)
    def _():
        fetch_group(x_parts, g_parts, order, x_buf, g_buf, in_sem, 0, 0, rows)
        acc_pair[...] = jnp.zeros_like(acc_pair)
        acc_down[...] = jnp.zeros_like(acc_down)
        zeros[...] = jnp.zeros_like(zeros)
        zero_gates[...] = jnp.zeros_like(zero_gates)

    @pl.when(q + 1 < count)
    def _():
        fetch_group(x_parts, g_parts, order, x_buf, g_buf, in_sem, 1 - slot, q + 1, rows)

    wait_group(x_parts, x_buf, g_buf, in_sem, slot, rows)
    x, g = x_buf[slot], g_buf[slot]

    sig = jax.nn.sigmoid(back_product(router_t[...], x))
    chosen = sig * hits[0]
    gates = ROUTE_SCALE * chosen / jnp.sum(chosen, axis=0, keepdims=True)
    numbers = lax.broadcasted_iota(jnp.int32, gates.shape, 0)
    places = lax.broadcasted_iota(jnp.int32, (room, x.shape[0]), 0)
    picks = []
    for e in range(local_count):
        gate = jnp.sum(jnp.where(numbers == first[0] + e, gates, 0.0), axis=0, keepdims=True)
        pick = places == pos[0, e : e + 1]
        row_gate = jnp.sum(jnp.where(pick, gate, 0.0), axis=1, keepdims=True)
        gate_stage[slot, e] = jnp.broadcast_to(row_gate, (room, LANES))
        picks.append(jnp.where(pick, 1.0, 0.0).astype(LOW))
    picks = jnp.concatenate(picks, axis=0)
    x_stage[slot] = product(picks, x).astype(LOW).reshape(local_count, room, -1)
    g_stage[slot] = product(picks, g).astype(LOW).reshape(local_count, room, -1)

    def writes(which, at):
        start = [pl.multiple_of(offsets[e * count + at], ROW_STEP) for e in range(local_count)]
        return [
            pltpu.make_async_copy(
                stage.at[which, e], array.at[e, pl.ds(start[e], room)], out_sem.at[which, k, e]
            )
            for e in range(local_count)
            for k, (stage, array) in enumerate(
                ((x_stage, x_rows), (g_stage, g_rows), (gate_stage, row_gates))
            )
        ]

    @pl.when(q > 0)
    def _():
        for copy in writes(1 - slot, q - 1):
            copy.wait()

    for copy in writes(slot, q):
        copy.start()

    both = back_product(x, pair_w[...])
    gate_part, up_part = both[:, :width], both[:, width:]
    silu_part, slope = silu_parts(gate_part)
    hidden = (silu_part * up_part).astype(LOW)
    back = back_product(g, down_w[...])
    feat = jnp.concatenate(
        [(back * up_part * slope).astype(LOW), (back * silu_part).astype(LOW)], axis=1
    )
    feats[...] = feat
    hiddens[...] = hidden
    acc_pair[...] += outer_sum(feat, x)
    acc_down[...] += outer_sum(hidden, g)

    @pl.when(q == count - 1)
    def _():
        for copy in writes(slot, q):
            copy.wait()
        tails = []
        for e in range(local_count):
            end = pl.multiple_of(offsets[local_count * count + e], ROW_STEP)
            for k, (stage, array) in enumerate(
                ((zeros, x_rows), (zeros, g_rows), (zero_gates, row_gates))
            ):
                tails.append(
                    pltpu.make_async_copy(
                        stage, array.at[e, pl.ds(end, HALF_TILE)], out_sem.at[slot, k, e]
                    )
                )
        for copy in tails:
            copy.start()
        delta_pair[...] = acc_pair[...].astype(LOW)
        delta_down[...] = acc_down[...].astype(LOW)
        for copy in tails:
            copy.wait()


def expert_kernel(totals, first, x, g, row_gate, w_gate, w_up, w_down, result, grad_row, grad_gate, grad_up, weighted, gate_grad):
    e, t = pl.program_id(0), pl.program_id(1)
    left = totals[e] - t * ROW_TILE

    def work(count):
        here = pl.ds(0, count)
        width = x.shape[2]
        gate = row_gate[0, here][:, :1]
        gate_part = back_product(x[0, here], w_gate[0])
        up_part = back_product(x[0, here], w_up[0])
        silu_part, slope = silu_parts(gate_part)
        hidden = (silu_part * up_part).astype(LOW)
        back = back_product(g[0, here], w_down[0])
        wide = hidden.astype(F32)
        own = jnp.sum(wide * back, axis=1, keepdims=True)
        lanes = lax.broadcasted_iota(jnp.int32, (count, LANES), 1)
        gate_grad[0, here] = jnp.where(lanes == first[0] + e, own, 0.0)
        back = back * gate
        low_gate = (back * up_part * slope).astype(LOW)
        low_up = (back * silu_part).astype(LOW)
        grad_gate[0, here] = low_gate
        grad_up[0, here] = low_up
        weighted[0, here] = (wide * gate).astype(LOW)
        for at in range(0, width, COL_TILE):
            cols = pl.ds(at, COL_TILE)
            grad_row[0, here, cols] = (
                product(low_gate, w_gate[0, :, cols]) + product(low_up, w_up[0, :, cols])
            ).astype(LOW)
            result[0, here, cols] = (gate * product(hidden, w_down[0, :, cols])).astype(LOW)

    @pl.when(left > HALF_TILE)
    def _():
        work(ROW_TILE)

    @pl.when((left > 0) & (left <= HALF_TILE))
    def _():
        work(HALF_TILE)


def delta_kernel(totals, x, g, grad_gate, grad_up, weighted, delta_gate, delta_up, delta_down):
    e, t = pl.program_id(0), pl.program_id(1)
    left = totals[e] - t * ROW_TILE

    @pl.when(t == 0)
    def _():
        delta_gate[...] = jnp.zeros_like(delta_gate)
        delta_up[...] = jnp.zeros_like(delta_up)
        delta_down[...] = jnp.zeros_like(delta_down)

    def work(count):
        here = pl.ds(0, count)
        delta_gate[0] += outer_sum(grad_gate[0, here], x[0, here])
        delta_up[0] += outer_sum(grad_up[0, here], x[0, here])
        delta_down[0] += outer_sum(weighted[0, here], g[0, here])

    @pl.when(left > HALF_TILE)
    def _():
        work(ROW_TILE)

    @pl.when((left > 0) & (left <= HALF_TILE))
    def _():
        work(HALF_TILE)


def combine_kernel(ring, room, shards, by_column, with_gates, offsets, counts, order, rows_all, gates_all, pos, feat, weight, *rest):
    number = 4 * shards if by_column else shards
    outs, rest = rest[:number], rest[number:]
    if with_gates:
        gate_out, rest = rest[0], rest[1:]
    rows_buf, gates_buf, sems = rest
    step, steps = pl.program_id(0), pl.num_programs(0)
    slot = lax.rem(step, 2)
    local_count = rows_all.shape[0]

    def reads(which, at):
        copies = []
        for e in range(local_count):
            start = pl.multiple_of(offsets[e * steps + at], ROW_STEP)
            copies.append(
                pltpu.make_async_copy(
                    rows_all.at[e, pl.ds(start, room)], rows_buf.at[which, e], sems.at[which, 0, e]
                )
            )
            if with_gates:
                copies.append(
                    pltpu.make_async_copy(
                        gates_all.at[e, pl.ds(start, room)],
                        gates_buf.at[which, e],
                        sems.at[which, 1, e],
                    )
                )
        return copies

    @pl.when(step == 0)
    def _():
        for copy in reads(0, 0):
            copy.start()

    @pl.when(step + 1 < steps)
    def _():
        for copy in reads(1 - slot, step + 1):
            copy.start()

    for copy in reads(slot, step):
        copy.wait()

    tokens = pos.shape[1]
    places = lax.broadcasted_iota(jnp.int32, (tokens, room), 1)
    row_ids = lax.broadcasted_iota(jnp.int32, (room, 1), 0)
    picks, rows, gate_sum = [], [], None
    for e in range(local_count):
        valid = row_ids < counts[e * steps + step]
        pick = jnp.where(places == pos[0][:, e : e + 1], 1.0, 0.0)
        picks.append(pick.astype(LOW))
        rows.append(jnp.where(valid, rows_buf[slot, e], jnp.zeros((), LOW)))
        if with_gates:
            gates = jnp.where(valid, gates_buf[slot, e], 0.0)
            for _ in range(3):
                term = gates.astype(LOW)
                gates = gates - term.astype(F32)
                term = product(picks[-1], term)
                gate_sum = term if gate_sum is None else gate_sum + term
    low = (
        product(feat[...], weight[...])
        + product(jnp.concatenate(picks, axis=1), jnp.concatenate(rows, axis=0))
    ).astype(LOW)
    share = tokens // shards
    for s in range(shards):
        mine = low[s * share : (s + 1) * share]
        if by_column:
            for col in range(4):

                @pl.when(step // ring == col)
                def _(col=col, s=s, mine=mine):
                    outs[4 * s + col][0] = mine
        else:
            outs[s][0] = mine
    if with_gates:
        gate_out[0] = gate_sum


def assemble_kernel(owners, widths, order, *refs):
    outs = refs[owners:]
    for q in range(owners):
        at = 0
        for out, width in zip(outs, widths):
            out[order[q]] = refs[q][:, at : at + width].astype(F32)
            at += width


def transpose_kernel(shards, owners, own, every, gate_out, up_out, table):
    which, k = pl.program_id(0), pl.program_id(1)

    @pl.when(k == 0)
    def _():
        for s in range(shards):
            for q in range(owners):
                table[pl.ds((s * owners + q) * own, own)] = every[q, s, 0].astype(F32)

    piece = table[pl.ds(pl.multiple_of(k * LANES, LANES), LANES)].T

    @pl.when(which == 0)
    def _():
        gate_out[...] = piece

    @pl.when(which == 1)
    def _():
        up_out[...] = piece


def params(*semantics):
    return pltpu.CompilerParams(dimension_semantics=semantics, vmem_limit_bytes=VMEM_BYTES)


def assemble(order, arrays, widths):
    owners = len(arrays)
    rows = arrays[0].shape[0]
    whole = lambda *_: (0, 0)
    return pl.pallas_call(
        functools.partial(assemble_kernel, owners, widths),
        grid_spec=pltpu.PrefetchScalarGridSpec(
            num_scalar_prefetch=1,
            grid=(1,),
            in_specs=[pl.BlockSpec(a.shape, whole) for a in arrays],
            out_specs=[pl.BlockSpec((owners, rows, w), lambda *_: (0, 0, 0)) for w in widths],
        ),
        out_shape=[jax.ShapeDtypeStruct((owners, rows, w), F32) for w in widths],
        compiler_params=params("arbitrary"),
        cost_estimate=pl.CostEstimate(
            flops=0, bytes_accessed=owners * rows * sum(widths) * 6, transcendentals=0
        ),
    )(order, *arrays)


def transpose_pair(every):
    owners, shards, unused, own, cols = every.shape
    hidden = owners * shards * own
    tiles = hidden // LANES
    return pl.pallas_call(
        functools.partial(transpose_kernel, shards, owners, own),
        grid=(2, tiles),
        in_specs=[
            pl.BlockSpec((owners, shards, 1, own, cols), lambda w, k: (0, 0, w, 0, 0)),
        ],
        out_specs=[
            pl.BlockSpec((cols, LANES), lambda w, k: (0, jnp.where(w == 0, k, tiles - 1))),
            pl.BlockSpec((cols, LANES), lambda w, k: (0, jnp.where(w == 0, 0, k))),
        ],
        out_shape=[jax.ShapeDtypeStruct((cols, hidden), F32)] * 2,
        scratch_shapes=[pltpu.VMEM((hidden, cols), F32)],
        compiler_params=params("arbitrary", "arbitrary"),
        cost_estimate=pl.CostEstimate(
            flops=0, bytes_accessed=12 * hidden * cols, transcendentals=0
        ),
    )(every)


def dispatch(shards, rows, room, offsets, first, order, hits, pos, router_t, pair_w, down_w, x_parts, g_parts):
    owners, all_experts, span = hits.shape
    local_count = pos.shape[1]
    width = router_t.shape[1]
    hidden = down_w.shape[0]
    capacity = -(-(owners * room + HALF_TILE) // ROW_TILE) * ROW_TILE
    flat = [a for part in x_parts for a in part] + list(g_parts)
    whole = lambda q, *_: (0, 0)
    anywhere = pl.BlockSpec(memory_space=pl.ANY)
    return pl.pallas_call(
        functools.partial(dispatch_kernel, owners, shards, rows, room),
        grid_spec=pltpu.PrefetchScalarGridSpec(
            num_scalar_prefetch=3,
            grid=(owners,),
            in_specs=[
                pl.BlockSpec((1, all_experts, span), lambda q, *_: (q, 0, 0)),
                pl.BlockSpec((1, local_count, span), lambda q, *_: (q, 0, 0)),
                pl.BlockSpec((all_experts, width), whole),
                pl.BlockSpec((2 * hidden, width), whole),
                pl.BlockSpec((hidden, width), whole),
            ]
            + [anywhere] * len(flat),
            out_specs=[
                anywhere,
                anywhere,
                anywhere,
                pl.BlockSpec((span, 2 * hidden), lambda q, *_: (q, 0)),
                pl.BlockSpec((span, hidden), lambda q, *_: (q, 0)),
                pl.BlockSpec((2 * hidden, width), whole),
                pl.BlockSpec((hidden, width), whole),
            ],
            scratch_shapes=[
                pltpu.VMEM((2, span, width), LOW),
                pltpu.VMEM((2, span, width), LOW),
                pltpu.SemaphoreType.DMA((2, 2, shards)),
                pltpu.VMEM((2, local_count, room, width), LOW),
                pltpu.VMEM((2, local_count, room, width), LOW),
                pltpu.VMEM((2, local_count, room, LANES), F32),
                pltpu.SemaphoreType.DMA((2, 3, local_count)),
                pltpu.VMEM((HALF_TILE, width), LOW),
                pltpu.VMEM((HALF_TILE, LANES), F32),
                pltpu.VMEM((2 * hidden, width), F32),
                pltpu.VMEM((hidden, width), F32),
            ],
        ),
        out_shape=[
            jax.ShapeDtypeStruct((local_count, capacity, width), LOW),
            jax.ShapeDtypeStruct((local_count, capacity, width), LOW),
            jax.ShapeDtypeStruct((local_count, capacity, LANES), F32),
            jax.ShapeDtypeStruct((owners * span, 2 * hidden), LOW),
            jax.ShapeDtypeStruct((owners * span, hidden), LOW),
            jax.ShapeDtypeStruct((2 * hidden, width), LOW),
            jax.ShapeDtypeStruct((hidden, width), LOW),
        ],
        compiler_params=params("arbitrary"),
        cost_estimate=pl.CostEstimate(
            flops=14 * owners * span * width * span,
            bytes_accessed=4 * owners * span * width,
            transcendentals=0,
        ),
    )(offsets, first, order, hits, pos, router_t, pair_w, down_w, *flat)


def tile_map(e, t, totals, *_):
    last = jnp.maximum((totals[e] + ROW_TILE - 1) // ROW_TILE - 1, 0)
    return (e, jnp.minimum(t, last), 0)


def expert_map(e, t, *_):
    return (e, 0, 0)


def run_experts(totals, first, x, g, row_gate, w_gate, w_up, w_down):
    local_count, capacity, width = x.shape
    hidden = w_gate.shape[1]
    tiles = capacity // ROW_TILE
    wide = pl.BlockSpec((1, ROW_TILE, width), tile_map)
    slim = pl.BlockSpec((1, ROW_TILE, hidden), tile_map)
    lane = pl.BlockSpec((1, ROW_TILE, LANES), tile_map)
    return pl.pallas_call(
        expert_kernel,
        grid_spec=pltpu.PrefetchScalarGridSpec(
            num_scalar_prefetch=2,
            grid=(local_count, tiles),
            in_specs=[
                wide,
                wide,
                lane,
                pl.BlockSpec((1, hidden, width), expert_map),
                pl.BlockSpec((1, hidden, width), expert_map),
                pl.BlockSpec((1, hidden, width), expert_map),
            ],
            out_specs=[wide, wide, slim, slim, slim, lane],
        ),
        out_shape=[
            jax.ShapeDtypeStruct(x.shape, LOW),
            jax.ShapeDtypeStruct(x.shape, LOW),
            jax.ShapeDtypeStruct((local_count, capacity, hidden), LOW),
            jax.ShapeDtypeStruct((local_count, capacity, hidden), LOW),
            jax.ShapeDtypeStruct((local_count, capacity, hidden), LOW),
            jax.ShapeDtypeStruct(row_gate.shape, F32),
        ],
        compiler_params=params("arbitrary", "arbitrary"),
        cost_estimate=pl.CostEstimate(
            flops=6 * local_count * capacity * width * hidden,
            bytes_accessed=6 * local_count * width * (capacity + hidden),
            transcendentals=0,
        ),
    )(totals, first, x, g, row_gate, w_gate, w_up, w_down)


def run_deltas(totals, x, g, grad_gate, grad_up, weighted):
    local_count, capacity, width = x.shape
    hidden = grad_gate.shape[2]
    tiles = capacity // ROW_TILE
    wide = pl.BlockSpec((1, ROW_TILE, width), tile_map)
    slim = pl.BlockSpec((1, ROW_TILE, hidden), tile_map)
    return pl.pallas_call(
        delta_kernel,
        grid_spec=pltpu.PrefetchScalarGridSpec(
            num_scalar_prefetch=1,
            grid=(local_count, tiles),
            in_specs=[wide, wide, slim, slim, slim],
            out_specs=[pl.BlockSpec((1, hidden, width), expert_map)] * 3,
        ),
        out_shape=[jax.ShapeDtypeStruct((local_count, hidden, width), F32)] * 3,
        compiler_params=params("arbitrary", "arbitrary"),
        cost_estimate=pl.CostEstimate(
            flops=3 * local_count * capacity * width * hidden,
            bytes_accessed=12 * local_count * width * hidden,
            transcendentals=0,
        ),
    )(totals, x, g, grad_gate, grad_up, weighted)


def combine(ring, rows, shards, room, by_column, offsets, counts, order, rows_all, gates_all, pos, feat, weight):
    local_count, capacity, width = rows_all.shape
    owners, span = pos.shape[:2]
    with_gates = gates_all is not None
    if by_column:
        out_shape = [jax.ShapeDtypeStruct((ring, rows, width), LOW)] * (4 * shards)
        out_specs = [
            pl.BlockSpec(
                (1, rows, width),
                lambda q, *_, col=col: (jnp.clip(q - col * ring, 0, ring - 1), 0, 0),
            )
            for s in range(shards)
            for col in range(4)
        ]
    else:
        out_shape = [jax.ShapeDtypeStruct((owners, rows, width), LOW)] * shards
        out_specs = [
            pl.BlockSpec((1, rows, width), lambda q, offsets, counts, order: (order[q], 0, 0))
        ] * shards
    if with_gates:
        out_shape = out_shape + [jax.ShapeDtypeStruct((owners, span, LANES), F32)]
        out_specs = out_specs + [pl.BlockSpec((1, span, LANES), lambda q, *_: (q, 0, 0))]
    return pl.pallas_call(
        functools.partial(combine_kernel, ring, room, shards, by_column, with_gates),
        grid_spec=pltpu.PrefetchScalarGridSpec(
            num_scalar_prefetch=3,
            grid=(owners,),
            in_specs=[
                pl.BlockSpec(memory_space=pl.ANY),
                pl.BlockSpec(memory_space=pl.ANY),
                pl.BlockSpec((1, span, local_count), lambda q, *_: (q, 0, 0)),
                pl.BlockSpec((span, feat.shape[1]), lambda q, *_: (q, 0)),
                pl.BlockSpec(weight.shape, lambda q, *_: (0, 0)),
            ],
            out_specs=out_specs,
            scratch_shapes=[
                pltpu.VMEM((2, local_count, room, width), LOW),
                pltpu.VMEM((2, local_count, room, LANES), F32),
                pltpu.SemaphoreType.DMA((2, 2, local_count)),
            ],
        ),
        out_shape=out_shape,
        compiler_params=params("arbitrary"),
        cost_estimate=pl.CostEstimate(
            flops=4 * owners * span * width * span,
            bytes_accessed=4 * owners * span * width,
            transcendentals=0,
        ),
    )(offsets, counts, order, rows_all, gates_all if with_gates else rows_all, pos, feat, weight)


def local(
    tokens,
    cotangent,
    seq_len,
    routes,
    attention_gain,
    query_down,
    query_gain,
    query_up,
    latent_down,
    latent_gain,
    latent_up,
    attention_out,
    feedforward_gain,
    router,
    shared_gate,
    shared_up,
    shared_down,
    expert_gate,
    expert_up,
    expert_down,
):
    rows, width = tokens.shape
    shards = lax.axis_size("shard")
    owners = lax.axis_size("expert")
    core = lax.axis_index("shard")
    chip = lax.axis_index("expert")
    local_count = expert_gate.shape[0]
    all_experts = local_count * owners
    capacity = 2 * rows * TOP // all_experts
    span = rows * shards
    blocks = shards * owners
    own_heads = HEADS // shards
    part_cols = width // shards

    def place(s):
        return (core - s) % shards

    def from_core(values, s):
        return lax.ppermute(values, "shard", [(i, (i + s) % shards) for i in range(shards)])

    def to_core(values, s):
        return lax.ppermute(values, "shard", [(i, (i - s) % shards) for i in range(shards)])

    def relative(values):
        return [values] + [from_core(values, s) for s in range(1, shards)]

    def sum_parts(parts, kind):
        got = [to_core(parts[s].astype(kind), s).astype(F32) for s in range(1, shards)]
        return total([parts[0].astype(F32)] + got)

    ring = owners // 4
    z_at, y_at, x_at = chip // 4, chip // 2 % 2, chip % 2

    def send(values, dz=0, dy=0, dx=0):
        pairs = []
        for i in range(owners):
            z, y, x = i // 4, i // 2 % 2, i % 2
            pairs.append((i, (z + dz) % ring * 4 + (y ^ dy) * 2 + (x ^ dx)))
        return lax.ppermute(values, "expert", pairs)

    slot_chip = jnp.stack(
        [
            (z_at - k) % ring * 4 + (y_at ^ (col // 2)) * 2 + (x_at ^ (col % 2))
            for col in range(4)
            for k in range(ring)
        ]
    ).astype(jnp.int32)

    half_ring = ring // 2

    def middle(values):
        return max(values.shape[-1] // 2 // LANES * LANES, 1)

    def gather_chips(values):
        half = middle(values)

        def corner(side_x, side_y):
            left = send(side_y[:, :half], dx=1)
            right = send(side_x[:, half:], dy=1)
            return jnp.concatenate([left, right], axis=1)

        own, side_x, side_y, both = ([None] * ring for _ in range(4))

        def sides(k):
            side_x[k], side_y[k] = send(own[k], dx=1), send(own[k], dy=1)

        own[0] = values
        sides(0)
        for k in [k for k in range(1, ring) if k != half_ring]:
            own[k] = send(values, dz=k)
        own[half_ring] = send(own[half_ring - 1], dz=1)
        both[0] = corner(side_x[0], side_y[0])
        for k in range(1, ring):
            sides(k)
        for k in [k for k in range(1, ring) if k != half_ring]:
            both[k] = send(both[0], dz=k)
        both[half_ring] = corner(side_x[half_ring], side_y[half_ring])
        return own + side_x + side_y + both

    def scatter_chips(parts, hooks=()):
        own, side_x, side_y, both = (list(parts[i * ring : (i + 1) * ring]) for i in range(4))
        half = middle(own[0])
        hooks = list(hooks) + [lambda got: got] * 2

        def add(a, *terms):
            return total([v.astype(F32) for v in (a,) + terms]).astype(LOW)

        def from_corner(block):
            return send(block[:, :half], dx=1), send(block[:, half:], dy=1)

        def spread(k, got):
            for_y, for_x = got
            side_y[k] = jnp.concatenate([add(side_y[k][:, :half], for_y), side_y[k][:, half:]], axis=1)
            side_x[k] = jnp.concatenate([side_x[k][:, :half], add(side_x[k][:, half:], for_x)], axis=1)

        def fold(k):
            return send(side_x[k], dx=1), send(side_y[k], dy=1)

        others = [k for k in range(1, ring) if k != half_ring]
        first = list(from_corner(both[half_ring])) + [send(both[k], dz=-k) for k in others]
        sides = [v for k in others for v in fold(k)]
        first = hooks[0](first)
        spread(half_ring, first[:2])
        both[0] = add(both[0], *first[2:])
        second = list(fold(half_ring)) + list(from_corner(both[0]))
        for n, k in enumerate(others):
            own[k] = add(own[k], *sides[2 * n : 2 * n + 2])
        late = [send(own[k], dz=-k) for k in others if k != half_ring - 1]
        second = hooks[1](second)
        own[half_ring] = add(own[half_ring], *second[:2])
        spread(0, second[2:])
        own[half_ring - 1] = add(own[half_ring - 1], send(own[half_ring], dz=-1))
        last = list(fold(0)) + [send(own[half_ring - 1], dz=1 - half_ring)]
        return total([v.astype(F32) for v in [own[0]] + late + last])

    def sum_chips(values):
        values = values + send(values, dx=1)
        values = values + send(values, dy=1)
        return total([values] + [send(values, dz=k) for k in range(1, ring)])

    def scatter_rows(delta):
        grid = delta.astype(LOW).reshape(owners, delta.shape[0] // owners, delta.shape[1])
        parts = [
            lax.dynamic_index_in_dim(grid, slot_chip[q], 0, keepdims=False) for q in range(owners)
        ]
        return scatter_chips(parts).astype(LOW)

    def gather_rows(mine, widths=None):
        widths = (mine.shape[1],) if widths is None else widths
        return [
            v.reshape(owners * v.shape[1], v.shape[2])
            for v in assemble(slot_chip, gather_chips(mine), widths)
        ]

    def cut(values, axis):
        size = values.shape[axis] // shards
        return [
            lax.dynamic_slice_in_dim(values, place(s) * size, size, axis) for s in range(shards)
        ]

    def natural(parts, axis):
        pieces = []
        for i in range(shards):
            piece = parts[0]
            for s in range(1, shards):
                piece = jnp.where(place(s) == i, parts[s], piece)
            pieces.append(piece)
        return jnp.concatenate(pieces, axis=axis)

    with jax.named_scope("early_gathers"):
        routes_own = sum_chips(
            jnp.zeros((owners, TOP, rows), jnp.int32).at[chip].set(routes.T)
        )
        token_parts = relative(tokens)
        gains_own = jnp.concatenate([attention_gain, query_gain, latent_gain, feedforward_gain])
        gain_parts = relative(gains_own)
        query_down_parts = relative(query_down)
        latent_down_parts = relative(latent_down)
        query_up_parts = relative(query_up)
        latent_up_parts = relative(latent_up)
        router_parts = relative(router)
        grad_own = lax.all_gather(cotangent, "expert", axis=0)

    hidden_all = shared_gate.shape[1]
    hidden_own = hidden_all // blocks
    hidden_shard = hidden_all // shards

    def shared_columns(weight):
        pieces = [
            lax.dynamic_slice_in_dim(
                weight, place(s) * hidden_shard + chip * hidden_own, hidden_own, 1
            ).T
            for s in range(shards)
        ]
        got = [pieces[0]] + [None] * (shards - 1)
        for s in range(1, shards):
            got[shards - s] = to_core(pieces[s], s)
        return natural(got, 1)

    with jax.named_scope("shared_weights"):
        padded = -(-hidden_own // LANES) * LANES
        pad = ((0, padded - hidden_own), (0, 0))
        pair_w = jnp.concatenate(
            [jnp.pad(shared_columns(shared_gate), pad), jnp.pad(shared_columns(shared_up), pad)]
        )
        down_w = jnp.pad(
            lax.dynamic_slice_in_dim(shared_down, chip * hidden_own, hidden_own, 0), pad
        )
        router_full = natural(router_parts, 0)

    with jax.named_scope("routing"):
        routes_all = jnp.stack(relative(routes_own), axis=2)[slot_chip].reshape(owners, TOP, span)
        expert_ids = jnp.arange(all_experts, dtype=jnp.int32)
        hits = jnp.any(
            routes_all[:, None] == expert_ids[None, :, None, None], axis=2
        )
        first = chip * local_count
        hit = lax.dynamic_slice_in_dim(hits, first, local_count, 1).astype(jnp.int32)
        pos = jnp.where(hit > 0, jnp.cumsum(hit, axis=2) - hit, -1)
        pos_cols = jnp.swapaxes(pos, 1, 2)
        room = shards * capacity
        counts = jnp.sum(hit, axis=2).T
        steps = (counts + ROW_STEP - 1) // ROW_STEP * ROW_STEP
        ends = jnp.cumsum(steps, axis=1)
        totals = ends[:, -1]
        offsets = jnp.concatenate([(ends - steps).reshape(-1), totals])
        counts = counts.reshape(-1)
        hits = hits.astype(F32)
        first_at = first.reshape(1).astype(jnp.int32)

    bounds = [0]
    for size in (part_cols, query_gain.shape[0], latent_gain.shape[0], part_cols):
        bounds.append(bounds[-1] + size)
    attention_gain_parts = [g[bounds[0] : bounds[1]].astype(F32) for g in gain_parts]
    query_gain_full = natural([g[bounds[1] : bounds[2]] for g in gain_parts], 0).astype(F32)
    latent_gain_full = natural([g[bounds[2] : bounds[3]] for g in gain_parts], 0).astype(F32)
    feed_gain_full = natural([g[bounds[3] : bounds[4]] for g in gain_parts], 0).astype(F32)
    gain_rel = jnp.concatenate(attention_gain_parts)

    with jax.named_scope("attention_forward"):
        positions = jnp.concatenate(
            [place(s) * rows + jnp.arange(rows, dtype=jnp.int32) for s in range(shards)]
        )
        cosine_table, sine_table = tables(positions, ROPE)
        length = seq_len[0]
        sequence = jnp.concatenate(token_parts, axis=0)
        source = jnp.concatenate(cut(sequence, 1), axis=1).astype(F32)
        source_scale = inverse_rms(source)
        normed = (source * source_scale * gain_rel).astype(LOW)
        normed, routes_own = lax.optimization_barrier((normed, routes_own))
        normed_parts = jnp.split(normed, shards, axis=1)
        query_latent = total([product(a, w) for a, w in zip(normed_parts, query_down_parts)])
        query_scale = inverse_rms(query_latent)
        query_low = (query_latent * query_scale * query_gain_full).astype(LOW)
        latent = total([product(a, w) for a, w in zip(normed_parts, latent_down_parts)])
        latent_c = latent[:, :KVL]
        latent_scale = inverse_rms(latent_c)
        latent_low = (latent_c * latent_scale * latent_gain_full).astype(LOW)
        key_rope = rotate(latent[:, KVL:], cosine_table, sine_table).astype(LOW)
        query_low_parts = cut(query_low, 1)
        latent_low_parts = cut(latent_low, 1)
        query_raw = total(
            [product(a, cut(w, 1)[0]) for a, w in zip(query_low_parts, query_up_parts)]
        ).reshape(span, own_heads, NOPE + ROPE)
        query_nope = query_raw[..., :NOPE].astype(LOW)
        query_rope = rotate(
            query_raw[..., NOPE:], cosine_table[:, None, :], sine_table[:, None, :]
        ).astype(LOW)
        keys_values = (
            total([product(a, cut(w, 1)[0]) for a, w in zip(latent_low_parts, latent_up_parts)])
            .astype(LOW)
            .reshape(span, own_heads, NOPE + VDIM)
        )
        key_nope = keys_values[..., :NOPE]
        values = keys_values[..., NOPE:]
        score_scale = (NOPE + ROPE) ** (-0.5)
        allowed = (positions[None, :] <= positions[:, None]) & (positions[None, :] < length)
        raw_scores = jnp.einsum("qhd,khd->hqk", query_nope, key_nope, preferred_element_type=F32)
        raw_scores = raw_scores + jnp.einsum(
            "qhr,kr->hqk", query_rope, key_rope, preferred_element_type=F32
        )
        scores = jnp.where(allowed[None], raw_scores * score_scale, NEG)
        row_peak = jnp.max(scores, axis=-1, keepdims=True)
        exp_terms = jnp.exp(scores - row_peak)
        probabilities = exp_terms / jnp.sum(exp_terms, axis=-1, keepdims=True)
        p_low = probabilities.astype(LOW)
        mixed = jnp.einsum("hqk,khv->qhv", p_low, values, preferred_element_type=F32)
        mixed = mixed.astype(LOW).reshape(span, own_heads * VDIM)
        attended = product(mixed, attention_out)
        resid = tokens.astype(F32) + sum_parts(jnp.split(attended, shards, axis=0), F32)
        resid_scale = inverse_rms(resid)
        ffn_low = (resid * resid_scale * feed_gain_full).astype(LOW)

    with jax.named_scope("token_gather"):
        ffn_slots = gather_chips(ffn_low)
        late = 2 * ring + half_ring
        ffn_slots[late], grad_own = lax.optimization_barrier((ffn_slots[late], grad_own))
        ffn_parts = list(zip(*[relative(v) for v in ffn_slots]))
        grad_parts = relative(grad_own)

    with jax.named_scope("dispatch"):
        x_rows, g_rows, row_gates, feats, hiddens, delta_pair, delta_down = dispatch(
            shards, rows, room, offsets, first_at, slot_chip, hits, pos, router_full.T, pair_w,
            down_w, ffn_parts, grad_parts,
        )

    with jax.named_scope("routed_experts"):
        results, grad_rows, low_gate, low_up, weighted, gate_rows = run_experts(
            totals, first_at, x_rows, g_rows, row_gates, jnp.swapaxes(expert_gate, 1, 2),
            jnp.swapaxes(expert_up, 1, 2), expert_down,
        )

    with jax.named_scope("expert_gradients"):
        delta_gate, delta_up, grad_expert_down = run_deltas(
            totals, x_rows, g_rows, low_gate, low_up, weighted
        )
        grad_expert_gate = jnp.swapaxes(delta_gate, 1, 2)
        grad_expert_up = jnp.swapaxes(delta_up, 1, 2)

    with jax.named_scope("shared_gradients"):
        pair = jnp.stack(
            [delta_pair[:hidden_own], delta_pair[padded : padded + hidden_own]]
        )
        pieces = cut(pair, 2)
        got = [pieces[0]] + [None] * (shards - 1)
        for s in range(1, shards):
            got[shards - s] = to_core(pieces[s], s)
        pair = natural([v[None] for v in got], 0)
        pair_all = lax.all_gather(pair, "expert", axis=0)
        down_all = lax.all_gather(delta_down[:hidden_own], "expert", axis=0, tiled=True)

    with jax.named_scope("to_tokens"):
        parts = combine(
            ring, rows, shards, room, True, offsets, counts, slot_chip, grad_rows, gate_rows,
            pos_cols, feats, pair_w,
        )
        gate_grid = parts[-1]
        mine = []
        for col in range(4):
            got = [to_core(parts[4 * s + col], s) for s in range(1, shards)]
            for k in range(ring):
                terms = [parts[col][k].astype(F32)] + [v[k].astype(F32) for v in got]
                mine.append(total(terms).astype(LOW))
        out_parts = combine(
            ring, rows, shards, room, False, offsets, counts, slot_chip, results, None,
            pos_cols, hiddens, down_w,
        )

        def with_deltas(got):
            nonlocal grad_expert_down
            *got, grad_expert_down = lax.optimization_barrier((*got, grad_expert_down))
            return got

        def with_outs(got):
            nonlocal out_parts, pair_all
            *got, first_part, pair_all = lax.optimization_barrier((*got, out_parts[0], pair_all))
            out_parts = [first_part] + list(out_parts[1:])
            return got

        grad_from_experts = scatter_chips(mine, (with_deltas, with_outs))
        gate_grid = lax.dynamic_slice_in_dim(gate_grid, first, local_count, 2)
        gate_grid = gate_grid.reshape(owners, shards, rows, local_count)
        gate_grid = sum_parts([gate_grid[:, s] for s in range(shards)], F32)
        gate_grid = jnp.zeros_like(gate_grid).at[slot_chip].set(gate_grid)
        grad_gates = lax.all_to_all(gate_grid, "expert", split_axis=0, concat_axis=0, tiled=True)
        grad_gates = jnp.swapaxes(grad_gates, 0, 1).reshape(rows, all_experts)
        moe_out = lax.psum_scatter(
            sum_parts(out_parts, LOW).astype(LOW), "expert", scatter_dimension=0
        )
        grad_shared_gate, grad_shared_up = transpose_pair(pair_all)

    with jax.named_scope("feed_backward"):
        grad_out = cotangent.astype(F32)
        hit_own = jnp.any(routes[:, :, None] == expert_ids, axis=1).astype(F32)
        sig = jax.nn.sigmoid(product(ffn_low, router_full))
        chosen = sig * hit_own
        own_sum = jnp.sum(chosen, axis=1, keepdims=True)
        inner = jnp.sum(grad_gates * chosen, axis=1, keepdims=True)
        grad_chosen = ROUTE_SCALE * (grad_gates / own_sum - inner / (own_sum * own_sum))
        grad_logits = (grad_chosen * hit_own * sig * (1.0 - sig)).astype(LOW)
        grad_ffn = back_product(grad_logits, router_full) + grad_from_experts
        grad_resid_part, feed_terms = norm_back(resid, resid_scale, feed_gain_full, grad_ffn)
        grad_resid = grad_out + grad_resid_part
        grad_attended = grad_resid.astype(LOW)
        feed_gain_delta = jnp.sum(feed_terms, axis=0)

    with jax.named_scope("attention_backward"):
        attended_grads = jnp.concatenate(relative(grad_attended), axis=0)
        logit_grads = jnp.concatenate(relative(grad_logits), axis=0)
        mine_out = scatter_rows(outer_sum(mixed, attended_grads))
        ffn_sequence = cut(jnp.concatenate([part[0] for part in ffn_parts]), 1)[0]
        delta_router = outer_sum(logit_grads, ffn_sequence)
        grad_mixed = (
            back_product(attended_grads, attention_out).astype(LOW).reshape(span, own_heads, VDIM)
        )
        grad_probs = jnp.einsum("qhv,khv->hqk", grad_mixed, values, preferred_element_type=F32)
        row_delta = jnp.sum(grad_probs * probabilities, axis=-1, keepdims=True)
        grad_raw = (score_scale * probabilities * (grad_probs - row_delta)).astype(LOW)
        grad_query_nope = jnp.einsum("hqk,khd->qhd", grad_raw, key_nope, preferred_element_type=F32)
        grad_query_rope = jnp.einsum("hqk,kr->qhr", grad_raw, key_rope, preferred_element_type=F32)
        grad_key_nope = jnp.einsum("hqk,qhd->khd", grad_raw, query_nope, preferred_element_type=F32)
        grad_key_rope = jnp.einsum("hqk,qhr->kr", grad_raw, query_rope, preferred_element_type=F32)
        grad_values = jnp.einsum("hqk,qhv->khv", p_low, grad_mixed, preferred_element_type=F32)
        grad_keys = (
            jnp.concatenate([grad_key_nope, grad_values], axis=-1)
            .reshape(span, own_heads * (NOPE + VDIM))
            .astype(LOW)
        )
        grad_query_turned = rotate(
            grad_query_rope, cosine_table[:, None, :], -sine_table[:, None, :]
        )
        grad_queries = (
            jnp.concatenate([grad_query_nope, grad_query_turned], axis=-1)
            .reshape(span, own_heads * (NOPE + ROPE))
            .astype(LOW)
        )

        def reorder(values, s):
            pieces = jnp.split(values, shards, axis=0)
            return jnp.concatenate([pieces[(t - s) % shards] for t in range(shards)], axis=0)

        def every_core(values):
            return [values] + [reorder(from_core(values, s), s) for s in range(1, shards)]

        grad_queries, down_all = lax.optimization_barrier((grad_queries, down_all))
        grad_shared_down = down_all.astype(F32)
        queries_back = natural(every_core(grad_queries), 1)
        keys_back = natural(every_core(grad_keys), 1)
        rope_back = total(every_core(grad_key_rope))
        grad_latent_normed = natural([back_product(keys_back, w) for w in latent_up_parts], 1)
        grad_latent_part, latent_terms = norm_back(
            latent_c, latent_scale, latent_gain_full, grad_latent_normed
        )
        grad_latent = jnp.concatenate(
            [grad_latent_part, rotate(rope_back, cosine_table, -sine_table)], axis=-1
        ).astype(LOW)
        grad_query_normed = natural([back_product(queries_back, w) for w in query_up_parts], 1)
        grad_query_part, query_terms = norm_back(
            query_latent, query_scale, query_gain_full, grad_query_normed
        )
        grad_query_latent = grad_query_part.astype(LOW)
        mine_up = scatter_rows(outer_sum(query_low_parts[0], queries_back))
        mine_latent = scatter_rows(outer_sum(latent_low_parts[0], keys_back))
        mine_down = scatter_rows(
            outer_sum(normed_parts[0], jnp.concatenate([grad_query_latent, grad_latent], axis=1))
        )
        mine_up, moe_out = lax.optimization_barrier((mine_up, moe_out))
        layer_out = (resid + moe_out.astype(F32)).astype(LOW)
        (grad_attention_out,) = gather_rows(mine_out)
        (grad_query_up,) = gather_rows(mine_up)
        (grad_latent_up,) = gather_rows(mine_latent)
        grad_query_down, grad_latent_down = gather_rows(
            mine_down, (grad_query_latent.shape[1], grad_latent.shape[1])
        )
        grad_normed = jnp.concatenate(
            [
                back_product(grad_query_latent[:rows], a) + back_product(grad_latent[:rows], b)
                for a, b in zip(query_down_parts, latent_down_parts)
            ],
            axis=1,
        )
        grad_source, attention_terms = norm_back(
            source[:rows], source_scale[:rows], gain_rel, grad_normed
        )
        grad_tokens = grad_resid + natural(jnp.split(grad_source, shards, axis=1), 1)

    with jax.named_scope("gain_gradients"):
        attention_delta = jnp.split(jnp.sum(attention_terms, axis=0), shards)
        feed_delta = cut(feed_gain_delta, 0)
        both = sum_parts(
            [jnp.concatenate([a, f]) for a, f in zip(attention_delta, feed_delta)], F32
        )
        query_delta = cut(jnp.sum(query_terms, axis=0), 0)[0]
        latent_delta = cut(jnp.sum(latent_terms, axis=0), 0)[0]
        sums = jnp.concatenate([delta_router.reshape(-1), both, query_delta, latent_delta])
        sums = sum_chips(sums.reshape(-1, part_cols)).reshape(-1)
        sizes = [all_experts * part_cols, part_cols, part_cols]
        sizes += [query_gain.shape[0], latent_gain.shape[0]]
        marks = [0]
        for size in sizes:
            marks.append(marks[-1] + size)
        grad_router, grad_attention_gain, grad_feed_gain, grad_query_gain, grad_latent_gain = [
            sums[a:b] for a, b in zip(marks, marks[1:])
        ]
        grad_router = grad_router.reshape(all_experts, part_cols).T

    return (
        layer_out,
        grad_tokens,
        grad_attention_gain,
        grad_query_down,
        grad_query_gain,
        grad_query_up,
        grad_latent_down,
        grad_latent_gain,
        grad_latent_up,
        grad_attention_out,
        grad_feed_gain,
        grad_router,
        grad_shared_gate,
        grad_shared_up,
        grad_shared_down,
        grad_expert_gate,
        grad_expert_up,
        grad_expert_down,
    )


def solution(mesh):
    tokens_spec = P(("expert", "shard"), None)
    rows_spec = P("shard", None)
    gain_spec = P("shard")
    expert_specs = (
        P("expert", None, "shard"),
        P("expert", None, "shard"),
        P("expert", "shard", None),
    )
    weight_specs = (
        gain_spec,
        rows_spec,
        gain_spec,
        rows_spec,
        rows_spec,
        gain_spec,
        rows_spec,
        rows_spec,
        gain_spec,
        rows_spec,
        rows_spec,
        rows_spec,
        rows_spec,
    ) + expert_specs
    return jax.shard_map(
        local,
        mesh=mesh,
        in_specs=(tokens_spec, tokens_spec, P("expert"), tokens_spec) + weight_specs,
        out_specs=(tokens_spec, tokens_spec) + weight_specs,
        check_vma=False,
    )
```

```python
import jax
import jax.numpy as jnp
import functools

from jax import lax
from jax.experimental import pallas as pl
from jax.experimental.pallas import tpu as pltpu
from jax.sharding import PartitionSpec as P

HEADS = 16
NOPE = 128
ROPE = 64
VDIM = 128
KVL = 512
TOP = 6

EPS = 1e-06
ROUTE_SCALE = 2.446
ROPE_BASE = 50000.0
NEG = -1e30

LOW = jnp.bfloat16
F32 = jnp.float32

LANES = 128
ROW_TILE = 512
HALF_TILE = 256
COL_TILE = 512
ROW_STEP = 16
VMEM_BYTES = 58 << 20


def tables(positions, rope_width):
    half_width = rope_width // 2
    frequencies = ROPE_BASE ** (-2.0 * jnp.arange(half_width, dtype=F32) / rope_width)
    angles = positions.astype(F32)[:, None] * frequencies[None, :]
    return (jnp.cos(angles), jnp.sin(angles))


def rotate(values, cosine_table, sine_table):
    half_width = values.shape[-1] // 2
    first_half = values[..., :half_width]
    second_half = values[..., half_width:]
    return jnp.concatenate(
        [
            first_half * cosine_table - second_half * sine_table,
            second_half * cosine_table + first_half * sine_table,
        ],
        axis=-1,
    )


def product(left_side, right_side):
    return jnp.dot(left_side, right_side, preferred_element_type=F32)


def outer_sum(left_side, right_side):
    return lax.dot_general(
        left_side, right_side, (((0,), (0,)), ((), ())), preferred_element_type=F32
    )


def back_product(left_side, right_side):
    return lax.dot_general(
        left_side, right_side, (((1,), (1,)), ((), ())), preferred_element_type=F32
    )


def tie(*arrays):
    return lax.optimization_barrier(arrays)


def total(terms):
    result = terms[0]
    for term in terms[1:]:
        result = result + term
    return result


def inverse_rms(values):
    return lax.rsqrt(jnp.mean(values * values, axis=-1, keepdims=True) + EPS)


def norm_back(values, scale, gain, grad):
    weighted = grad * gain
    inner = jnp.mean(weighted * values, axis=-1, keepdims=True)
    return scale * weighted - values * (scale * scale * scale) * inner, grad * values * scale


def silu_parts(gate_part):
    sig = jax.nn.sigmoid(gate_part)
    return gate_part * sig, sig * (1.0 + gate_part * (1.0 - sig))


def fetch_group(x_parts, g_parts, order, x_buf, g_buf, sems, slot, q, rows):
    for s, array in enumerate(g_parts):
        here = pl.ds(s * rows, rows)
        pltpu.make_async_copy(array.at[order[q]], g_buf.at[slot, here], sems.at[slot, 0, s]).start()
    for number in range(len(x_parts[0])):

        @pl.when(q == number)
        def _(number=number):
            for s, arrays in enumerate(x_parts):
                here = pl.ds(s * rows, rows)
                pltpu.make_async_copy(
                    arrays[number], x_buf.at[slot, here], sems.at[slot, 1, s]
                ).start()


def wait_group(x_parts, x_buf, g_buf, sems, slot, rows):
    for kind, buffer in enumerate((g_buf, x_buf)):
        for s, arrays in enumerate(x_parts):
            here = buffer.at[slot, pl.ds(s * rows, rows)]
            pltpu.make_async_copy(arrays[0], here, sems.at[slot, kind, s]).wait()


def dispatch_kernel(owners, shards, rows, room, offsets, first, order, hits, pos, router_t, pair_w, down_w, *rest):
    x_parts = [rest[owners * s : owners * (s + 1)] for s in range(shards)]
    g_parts = rest[owners * shards : (owners + 1) * shards]
    rest = rest[(owners + 1) * shards :]
    x_rows, g_rows, row_gates, feats, hiddens, delta_pair, delta_down = rest[:7]
    x_buf, g_buf, in_sem, x_stage, g_stage, gate_stage, out_sem, zeros, zero_gates, acc_pair, acc_down = rest[7:]
    q, count = pl.program_id(0), pl.num_programs(0)
    slot = lax.rem(q, 2)
    local_count = pos.shape[1]
    width = down_w.shape[0]

    @pl.when(q == 0)
    def _():
        fetch_group(x_parts, g_parts, order, x_buf, g_buf, in_sem, 0, 0, rows)
        acc_pair[...] = jnp.zeros_like(acc_pair)
        acc_down[...] = jnp.zeros_like(acc_down)
        zeros[...] = jnp.zeros_like(zeros)
        zero_gates[...] = jnp.zeros_like(zero_gates)

    @pl.when(q + 1 < count)
    def _():
        fetch_group(x_parts, g_parts, order, x_buf, g_buf, in_sem, 1 - slot, q + 1, rows)

    wait_group(x_parts, x_buf, g_buf, in_sem, slot, rows)
    x, g = x_buf[slot], g_buf[slot]

    sig = jax.nn.sigmoid(back_product(router_t[...], x))
    chosen = sig * hits[0]
    gates = ROUTE_SCALE * chosen / jnp.sum(chosen, axis=0, keepdims=True)
    numbers = lax.broadcasted_iota(jnp.int32, gates.shape, 0)
    places = lax.broadcasted_iota(jnp.int32, (room, x.shape[0]), 0)
    picks = []
    for e in range(local_count):
        gate = jnp.sum(jnp.where(numbers == first[0] + e, gates, 0.0), axis=0, keepdims=True)
        pick = places == pos[0, e : e + 1]
        row_gate = jnp.sum(jnp.where(pick, gate, 0.0), axis=1, keepdims=True)
        gate_stage[slot, e] = jnp.broadcast_to(row_gate, (room, LANES))
        picks.append(jnp.where(pick, 1.0, 0.0).astype(LOW))
    picks = jnp.concatenate(picks, axis=0)
    x_stage[slot] = product(picks, x).astype(LOW).reshape(local_count, room, -1)
    g_stage[slot] = product(picks, g).astype(LOW).reshape(local_count, room, -1)

    def writes(which, at):
        start = [pl.multiple_of(offsets[e * count + at], ROW_STEP) for e in range(local_count)]
        return [
            pltpu.make_async_copy(
                stage.at[which, e], array.at[e, pl.ds(start[e], room)], out_sem.at[which, k, e]
            )
            for e in range(local_count)
            for k, (stage, array) in enumerate(
                ((x_stage, x_rows), (g_stage, g_rows), (gate_stage, row_gates))
            )
        ]

    @pl.when(q > 0)
    def _():
        for copy in writes(1 - slot, q - 1):
            copy.wait()

    for copy in writes(slot, q):
        copy.start()

    both = back_product(x, pair_w[...])
    gate_part, up_part = both[:, :width], both[:, width:]
    silu_part, slope = silu_parts(gate_part)
    hidden = (silu_part * up_part).astype(LOW)
    back = back_product(g, down_w[...])
    feat = jnp.concatenate(
        [(back * up_part * slope).astype(LOW), (back * silu_part).astype(LOW)], axis=1
    )
    feats[...] = feat
    hiddens[...] = hidden
    acc_pair[...] += outer_sum(feat, x)
    acc_down[...] += outer_sum(hidden, g)

    @pl.when(q == count - 1)
    def _():
        for copy in writes(slot, q):
            copy.wait()
        tails = []
        for e in range(local_count):
            end = pl.multiple_of(offsets[local_count * count + e], ROW_STEP)
            for k, (stage, array) in enumerate(
                ((zeros, x_rows), (zeros, g_rows), (zero_gates, row_gates))
            ):
                tails.append(
                    pltpu.make_async_copy(
                        stage, array.at[e, pl.ds(end, HALF_TILE)], out_sem.at[slot, k, e]
                    )
                )
        for copy in tails:
            copy.start()
        delta_pair[...] = acc_pair[...].astype(LOW)
        delta_down[...] = acc_down[...].astype(LOW)
        for copy in tails:
            copy.wait()


def expert_kernel(totals, first, x, g, row_gate, w_gate, w_up, w_down, grad_row, grad_gate, grad_up, weighted, gate_grad):
    e, t = pl.program_id(0), pl.program_id(1)
    left = totals[e] - t * ROW_TILE

    def work(count):
        here = pl.ds(0, count)
        width = x.shape[2]
        gate = row_gate[0, here][:, :1]
        gate_part = back_product(x[0, here], w_gate[0])
        up_part = back_product(x[0, here], w_up[0])
        silu_part, slope = silu_parts(gate_part)
        hidden = (silu_part * up_part).astype(LOW)
        back = back_product(g[0, here], w_down[0])
        wide = hidden.astype(F32)
        own = jnp.sum(wide * back, axis=1, keepdims=True)
        lanes = lax.broadcasted_iota(jnp.int32, (count, LANES), 1)
        gate_grad[0, here] = jnp.where(lanes == first[0] + e, own, 0.0)
        back = back * gate
        low_gate = (back * up_part * slope).astype(LOW)
        low_up = (back * silu_part).astype(LOW)
        grad_gate[0, here] = low_gate
        grad_up[0, here] = low_up
        weighted[0, here] = (wide * gate).astype(LOW)
        for at in range(0, width, COL_TILE):
            cols = pl.ds(at, COL_TILE)
            grad_row[0, here, cols] = (
                product(low_gate, w_gate[0, :, cols]) + product(low_up, w_up[0, :, cols])
            ).astype(LOW)

    @pl.when(left > HALF_TILE)
    def _():
        work(ROW_TILE)

    @pl.when((left > 0) & (left <= HALF_TILE))
    def _():
        work(HALF_TILE)


def delta_kernel(e, chained, totals, x, g, grad_gate, grad_up, weighted, w_down, *rest):
    delta_gate, delta_up, delta_down, result = rest[chained:]
    t = pl.program_id(0)
    left = totals[e] - t * ROW_TILE

    @pl.when(t == 0)
    def _():
        delta_gate[...] = jnp.zeros_like(delta_gate)
        delta_up[...] = jnp.zeros_like(delta_up)
        delta_down[...] = jnp.zeros_like(delta_down)

    def work(count):
        here = pl.ds(0, count)
        delta_gate[0] += outer_sum(grad_gate[0, here], x[0, here])
        delta_up[0] += outer_sum(grad_up[0, here], x[0, here])
        delta_down[0] += outer_sum(weighted[0, here], g[0, here])
        for at in range(0, x.shape[2], COL_TILE):
            cols = pl.ds(at, COL_TILE)
            result[0, here, cols] = product(weighted[0, here], w_down[0, :, cols]).astype(LOW)

    @pl.when(left > HALF_TILE)
    def _():
        work(ROW_TILE)

    @pl.when((left > 0) & (left <= HALF_TILE))
    def _():
        work(HALF_TILE)


def combine_kernel(base, columns, ring, room, shards, with_gates, offsets, counts, order, rows_all, gates_all, pos, feat, weight, *rest):
    number = max(len(columns), 1) * shards
    outs, rest = rest[:number], rest[number:]
    if with_gates:
        gate_out, rest = rest[0], rest[1:]
    rows_buf, gates_buf, sems = rest
    step, steps = pl.program_id(0), pl.num_programs(0)
    slot = lax.rem(step, 2)
    local_count = rows_all.shape[0]
    count = counts.shape[0] // local_count

    def reads(which, at):
        copies = []
        for e in range(local_count):
            start = pl.multiple_of(offsets[e * count + base + at], ROW_STEP)
            copies.append(
                pltpu.make_async_copy(
                    rows_all.at[e, pl.ds(start, room)], rows_buf.at[which, e], sems.at[which, 0, e]
                )
            )
            if with_gates:
                copies.append(
                    pltpu.make_async_copy(
                        gates_all.at[e, pl.ds(start, room)],
                        gates_buf.at[which, e],
                        sems.at[which, 1, e],
                    )
                )
        return copies

    @pl.when(step == 0)
    def _():
        for copy in reads(0, 0):
            copy.start()

    @pl.when(step + 1 < steps)
    def _():
        for copy in reads(1 - slot, step + 1):
            copy.start()

    for copy in reads(slot, step):
        copy.wait()

    tokens = pos.shape[1]
    places = lax.broadcasted_iota(jnp.int32, (tokens, room), 1)
    row_ids = lax.broadcasted_iota(jnp.int32, (room, 1), 0)
    picks, rows, gate_sum = [], [], None
    for e in range(local_count):
        valid = row_ids < counts[e * count + base + step]
        pick = jnp.where(places == pos[0][:, e : e + 1], 1.0, 0.0)
        picks.append(pick.astype(LOW))
        rows.append(jnp.where(valid, rows_buf[slot, e], jnp.zeros((), LOW)))
        if with_gates:
            gates = jnp.where(valid, gates_buf[slot, e], 0.0)
            for _ in range(3):
                term = gates.astype(LOW)
                gates = gates - term.astype(F32)
                term = product(picks[-1], term)
                gate_sum = term if gate_sum is None else gate_sum + term
    low = (
        product(feat[...], weight[...])
        + product(jnp.concatenate(picks, axis=1), jnp.concatenate(rows, axis=0))
    ).astype(LOW)
    share = tokens // shards
    for s in range(shards):
        mine = low[s * share : (s + 1) * share]
        if columns:
            for n in range(len(columns)):

                @pl.when(step // ring == n)
                def _(n=n, s=s, mine=mine):
                    outs[len(columns) * s + n][0] = mine
        else:
            outs[s][0] = mine
    if with_gates:
        gate_out[0] = gate_sum


def assemble_kernel(owners, widths, order, *refs):
    outs = refs[owners:]
    for q in range(owners):
        at = 0
        for out, width in zip(outs, widths):
            out[order[q]] = refs[q][:, at : at + width].astype(F32)
            at += width


def transpose_kernel(shards, owners, own, every, gate_out, up_out, table):
    which, k = pl.program_id(0), pl.program_id(1)

    @pl.when(k == 0)
    def _():
        for s in range(shards):
            for q in range(owners):
                table[pl.ds((s * owners + q) * own, own)] = every[q, s, 0].astype(F32)

    piece = table[pl.ds(pl.multiple_of(k * LANES, LANES), LANES)].T

    @pl.when(which == 0)
    def _():
        gate_out[...] = piece

    @pl.when(which == 1)
    def _():
        up_out[...] = piece


def params(*semantics):
    return pltpu.CompilerParams(dimension_semantics=semantics, vmem_limit_bytes=VMEM_BYTES)


def assemble(order, arrays, widths):
    owners = len(arrays)
    rows = arrays[0].shape[0]
    whole = lambda *_: (0, 0)
    return pl.pallas_call(
        functools.partial(assemble_kernel, owners, widths),
        grid_spec=pltpu.PrefetchScalarGridSpec(
            num_scalar_prefetch=1,
            grid=(1,),
            in_specs=[pl.BlockSpec(a.shape, whole) for a in arrays],
            out_specs=[pl.BlockSpec((owners, rows, w), lambda *_: (0, 0, 0)) for w in widths],
        ),
        out_shape=[jax.ShapeDtypeStruct((owners, rows, w), F32) for w in widths],
        compiler_params=params("arbitrary"),
        cost_estimate=pl.CostEstimate(
            flops=0, bytes_accessed=owners * rows * sum(widths) * 6, transcendentals=0
        ),
    )(order, *arrays)


def transpose_pair(every):
    owners, shards, unused, own, cols = every.shape
    hidden = owners * shards * own
    tiles = hidden // LANES
    return pl.pallas_call(
        functools.partial(transpose_kernel, shards, owners, own),
        grid=(2, tiles),
        in_specs=[
            pl.BlockSpec((owners, shards, 1, own, cols), lambda w, k: (0, 0, w, 0, 0)),
        ],
        out_specs=[
            pl.BlockSpec((cols, LANES), lambda w, k: (0, jnp.where(w == 0, k, tiles - 1))),
            pl.BlockSpec((cols, LANES), lambda w, k: (0, jnp.where(w == 0, 0, k))),
        ],
        out_shape=[jax.ShapeDtypeStruct((cols, hidden), F32)] * 2,
        scratch_shapes=[pltpu.VMEM((hidden, cols), F32)],
        compiler_params=params("arbitrary", "arbitrary"),
        cost_estimate=pl.CostEstimate(
            flops=0, bytes_accessed=12 * hidden * cols, transcendentals=0
        ),
    )(every)


def dispatch(shards, rows, room, offsets, first, order, hits, pos, router_t, pair_w, down_w, x_parts, g_parts):
    owners, all_experts, span = hits.shape
    local_count = pos.shape[1]
    width = router_t.shape[1]
    hidden = down_w.shape[0]
    capacity = -(-(owners * room + HALF_TILE) // ROW_TILE) * ROW_TILE
    flat = [a for part in x_parts for a in part] + list(g_parts)
    whole = lambda q, *_: (0, 0)
    anywhere = pl.BlockSpec(memory_space=pl.ANY)
    return pl.pallas_call(
        functools.partial(dispatch_kernel, owners, shards, rows, room),
        grid_spec=pltpu.PrefetchScalarGridSpec(
            num_scalar_prefetch=3,
            grid=(owners,),
            in_specs=[
                pl.BlockSpec((1, all_experts, span), lambda q, *_: (q, 0, 0)),
                pl.BlockSpec((1, local_count, span), lambda q, *_: (q, 0, 0)),
                pl.BlockSpec((all_experts, width), whole),
                pl.BlockSpec((2 * hidden, width), whole),
                pl.BlockSpec((hidden, width), whole),
            ]
            + [anywhere] * len(flat),
            out_specs=[
                anywhere,
                anywhere,
                anywhere,
                pl.BlockSpec((span, 2 * hidden), lambda q, *_: (q, 0)),
                pl.BlockSpec((span, hidden), lambda q, *_: (q, 0)),
                pl.BlockSpec((2 * hidden, width), whole),
                pl.BlockSpec((hidden, width), whole),
            ],
            scratch_shapes=[
                pltpu.VMEM((2, span, width), LOW),
                pltpu.VMEM((2, span, width), LOW),
                pltpu.SemaphoreType.DMA((2, 2, shards)),
                pltpu.VMEM((2, local_count, room, width), LOW),
                pltpu.VMEM((2, local_count, room, width), LOW),
                pltpu.VMEM((2, local_count, room, LANES), F32),
                pltpu.SemaphoreType.DMA((2, 3, local_count)),
                pltpu.VMEM((HALF_TILE, width), LOW),
                pltpu.VMEM((HALF_TILE, LANES), F32),
                pltpu.VMEM((2 * hidden, width), F32),
                pltpu.VMEM((hidden, width), F32),
            ],
        ),
        out_shape=[
            jax.ShapeDtypeStruct((local_count, capacity, width), LOW),
            jax.ShapeDtypeStruct((local_count, capacity, width), LOW),
            jax.ShapeDtypeStruct((local_count, capacity, LANES), F32),
            jax.ShapeDtypeStruct((owners * span, 2 * hidden), LOW),
            jax.ShapeDtypeStruct((owners * span, hidden), LOW),
            jax.ShapeDtypeStruct((2 * hidden, width), LOW),
            jax.ShapeDtypeStruct((hidden, width), LOW),
        ],
        compiler_params=params("arbitrary"),
        cost_estimate=pl.CostEstimate(
            flops=14 * owners * span * width * span,
            bytes_accessed=4 * owners * span * width,
            transcendentals=0,
        ),
    )(offsets, first, order, hits, pos, router_t, pair_w, down_w, *flat)


def tile_map(e, t, totals, *_):
    last = jnp.maximum((totals[e] + ROW_TILE - 1) // ROW_TILE - 1, 0)
    return (e, jnp.minimum(t, last), 0)


def expert_map(e, t, *_):
    return (e, 0, 0)


def run_experts(totals, first, x, g, row_gate, w_gate, w_up, w_down):
    local_count, capacity, width = x.shape
    hidden = w_gate.shape[1]
    tiles = capacity // ROW_TILE
    wide = pl.BlockSpec((1, ROW_TILE, width), tile_map)
    slim = pl.BlockSpec((1, ROW_TILE, hidden), tile_map)
    lane = pl.BlockSpec((1, ROW_TILE, LANES), tile_map)
    return pl.pallas_call(
        expert_kernel,
        grid_spec=pltpu.PrefetchScalarGridSpec(
            num_scalar_prefetch=2,
            grid=(local_count, tiles),
            in_specs=[
                wide,
                wide,
                lane,
                pl.BlockSpec((1, hidden, width), expert_map),
                pl.BlockSpec((1, hidden, width), expert_map),
                pl.BlockSpec((1, hidden, width), expert_map),
            ],
            out_specs=[wide, slim, slim, slim, lane],
        ),
        out_shape=[
            jax.ShapeDtypeStruct(x.shape, LOW),
            jax.ShapeDtypeStruct((local_count, capacity, hidden), LOW),
            jax.ShapeDtypeStruct((local_count, capacity, hidden), LOW),
            jax.ShapeDtypeStruct((local_count, capacity, hidden), LOW),
            jax.ShapeDtypeStruct(row_gate.shape, F32),
        ],
        compiler_params=params("arbitrary", "arbitrary"),
        cost_estimate=pl.CostEstimate(
            flops=5 * local_count * capacity * width * hidden,
            bytes_accessed=6 * local_count * width * (capacity + hidden),
            transcendentals=0,
        ),
    )(totals, first, x, g, row_gate, w_gate, w_up, w_down)


def run_deltas(e, before, totals, x, g, grad_gate, grad_up, weighted, w_down):
    local_count, capacity, width = x.shape
    hidden = grad_gate.shape[2]
    tiles = capacity // ROW_TILE

    def rows_at(t, totals):
        return tile_map(e, t, totals)

    def expert_at(t, totals):
        return (e, 0, 0)

    wide = pl.BlockSpec((1, ROW_TILE, width), rows_at)
    slim = pl.BlockSpec((1, ROW_TILE, hidden), rows_at)
    once = pl.BlockSpec((1, hidden, width), expert_at, pipeline_mode=pl.Buffered(1))
    return pl.pallas_call(
        functools.partial(delta_kernel, e, len(before)),
        grid_spec=pltpu.PrefetchScalarGridSpec(
            num_scalar_prefetch=1,
            grid=(tiles,),
            in_specs=[wide, wide, slim, slim, slim, once]
            + [pl.BlockSpec(memory_space=pl.ANY)] * len(before),
            out_specs=[once] * 3 + [wide],
        ),
        out_shape=[jax.ShapeDtypeStruct((local_count, hidden, width), F32)] * 3
        + [jax.ShapeDtypeStruct(x.shape, LOW)],
        input_output_aliases={7 + i: i for i in range(len(before))},
        compiler_params=params("arbitrary"),
        cost_estimate=pl.CostEstimate(
            flops=4 * capacity * width * hidden,
            bytes_accessed=12 * width * hidden,
            transcendentals=0,
        ),
    )(totals, x, g, grad_gate, grad_up, weighted, w_down, *before)


def combine(columns, ring, rows, shards, room, offsets, counts, order, rows_all, gates_all, pos, feat, weight):
    local_count, capacity, width = rows_all.shape
    owners, span = pos.shape[:2]
    with_gates = gates_all is not None
    base = columns[0] * ring if columns else 0
    steps = len(columns) * ring if columns else owners
    if columns:
        out_shape = [jax.ShapeDtypeStruct((ring, rows, width), LOW)] * (len(columns) * shards)
        out_specs = [
            pl.BlockSpec(
                (1, rows, width),
                lambda q, *_, n=n: (jnp.clip(q - n * ring, 0, ring - 1), 0, 0),
            )
            for s in range(shards)
            for n in range(len(columns))
        ]
    else:
        out_shape = [jax.ShapeDtypeStruct((owners, rows, width), LOW)] * shards
        out_specs = [
            pl.BlockSpec((1, rows, width), lambda q, offsets, counts, order: (order[q], 0, 0))
        ] * shards
    if with_gates:
        out_shape = out_shape + [jax.ShapeDtypeStruct((steps, span, LANES), F32)]
        out_specs = out_specs + [pl.BlockSpec((1, span, LANES), lambda q, *_: (q, 0, 0))]
    return pl.pallas_call(
        functools.partial(combine_kernel, base, columns, ring, room, shards, with_gates),
        grid_spec=pltpu.PrefetchScalarGridSpec(
            num_scalar_prefetch=3,
            grid=(steps,),
            in_specs=[
                pl.BlockSpec(memory_space=pl.ANY),
                pl.BlockSpec(memory_space=pl.ANY),
                pl.BlockSpec((1, span, local_count), lambda q, *_: (base + q, 0, 0)),
                pl.BlockSpec((span, feat.shape[1]), lambda q, *_: (base + q, 0)),
                pl.BlockSpec(weight.shape, lambda q, *_: (0, 0)),
            ],
            out_specs=out_specs,
            scratch_shapes=[
                pltpu.VMEM((2, local_count, room, width), LOW),
                pltpu.VMEM((2, local_count, room, LANES), F32),
                pltpu.SemaphoreType.DMA((2, 2, local_count)),
            ],
        ),
        out_shape=out_shape,
        compiler_params=params("arbitrary"),
        cost_estimate=pl.CostEstimate(
            flops=4 * steps * span * width * span,
            bytes_accessed=4 * steps * span * width,
            transcendentals=0,
        ),
    )(offsets, counts, order, rows_all, gates_all if with_gates else rows_all, pos, feat, weight)


def local(
    tokens,
    cotangent,
    seq_len,
    routes,
    attention_gain,
    query_down,
    query_gain,
    query_up,
    latent_down,
    latent_gain,
    latent_up,
    attention_out,
    feedforward_gain,
    router,
    shared_gate,
    shared_up,
    shared_down,
    expert_gate,
    expert_up,
    expert_down,
):
    rows, width = tokens.shape
    shards = lax.axis_size("shard")
    owners = lax.axis_size("expert")
    core = lax.axis_index("shard")
    chip = lax.axis_index("expert")
    local_count = expert_gate.shape[0]
    all_experts = local_count * owners
    capacity = 2 * rows * TOP // all_experts
    span = rows * shards
    blocks = shards * owners
    own_heads = HEADS // shards
    part_cols = width // shards

    def place(s):
        return (core - s) % shards

    def from_core(values, s):
        return lax.ppermute(values, "shard", [(i, (i + s) % shards) for i in range(shards)])

    def to_core(values, s):
        return lax.ppermute(values, "shard", [(i, (i - s) % shards) for i in range(shards)])

    def relative(values):
        return [values] + [from_core(values, s) for s in range(1, shards)]

    def sum_parts(parts, kind):
        got = [to_core(parts[s].astype(kind), s).astype(F32) for s in range(1, shards)]
        return total([parts[0].astype(F32)] + got)

    ring = owners // 4
    z_at, y_at, x_at = chip // 4, chip // 2 % 2, chip % 2

    def send(values, dz=0, dy=0, dx=0):
        pairs = []
        for i in range(owners):
            z, y, x = i // 4, i // 2 % 2, i % 2
            pairs.append((i, (z + dz) % ring * 4 + (y ^ dy) * 2 + (x ^ dx)))
        return lax.ppermute(values, "expert", pairs)

    slot_chip = jnp.stack(
        [
            (z_at - k) % ring * 4 + (y_at ^ (col // 2)) * 2 + (x_at ^ (col % 2))
            for col in range(4)
            for k in range(ring)
        ]
    ).astype(jnp.int32)

    half_ring = ring // 2

    def middle(values):
        return max(values.shape[-1] // 2 // LANES * LANES, 1)

    steps_z = [1, ring - 1] + [k for k in range(2, ring - 1) if k != half_ring] + [half_ring]

    def gather_chips(values, relay=None):
        half = middle(values)
        slots, relayed = {("own", 0): values}, {}
        waiting = [("own", 0)]

        def stage(sends):
            nonlocal waiting
            fresh = {}
            for key in waiting:
                fresh[key] = relay(slots[key]) if relay else []
            flat, marks = [], []
            for key, arrays in list(sends.items()) + [(("core",) + k, v) for k, v in fresh.items()]:
                marks.append((key, len(arrays)))
                flat += arrays
            flat = list(tie(*flat))
            waiting = []
            for key, number in marks:
                arrays, flat = flat[:number], flat[number:]
                if key[0] == "core":
                    relayed[key[1:]] = arrays
                else:
                    slots[key] = arrays[0] if number == 1 else jnp.concatenate(arrays, axis=1)
                    waiting.append(key)

        def along(k):
            source = slots["own", half_ring - 1] if k == half_ring else values
            return {("own", k): [send(source, dz=1 if k == half_ring else k)]}

        def sides(k):
            return {
                ("x", k): [send(slots["own", k], dx=1)],
                ("y", k): [send(slots["own", k], dy=1)],
            }

        def corner(k):
            left = send(slots["y", k][:, :half], dx=1)
            right = send(slots["x", k][:, half:], dy=1)
            return {("both", k): [left, right]}

        def far(k):
            return {("both", k): [send(slots["both", 0], dz=k)]}

        for i, k in enumerate(steps_z):
            group = along(k) | sides(steps_z[i - 1] if i else 0)
            stage(group | corner(0) if i == 1 else group)
        stage(sides(half_ring) | far(steps_z[0]))
        last = corner(half_ring)
        for k in steps_z[1:-1]:
            last = last | far(k)
        stage(last)
        for key in waiting:
            relayed[key] = relay(slots[key]) if relay else []
        keys = [(col, k) for col in ("own", "x", "y", "both") for k in range(ring)]
        if relay:
            return [[slots[key]] + relayed[key] for key in keys]
        return [slots[key] for key in keys]

    def add(a, *terms):
        return total([v.astype(F32) for v in (a,) + terms]).astype(LOW)

    def scatter_chips(parts):
        own, side_x, side_y, both = (list(parts[i * ring : (i + 1) * ring]) for i in range(4))
        half = middle(both[0])

        def from_corner(block):
            return [send(block[:, :half], dx=1), send(block[:, half:], dy=1)]

        def spread(k, for_y, for_x):
            side_y[k] = jnp.concatenate([add(side_y[k][:, :half], for_y), side_y[k][:, half:]], axis=1)
            side_x[k] = jnp.concatenate([side_x[k][:, :half], add(side_x[k][:, half:], for_x)], axis=1)

        def fold(k):
            return [send(side_x[k], dx=1), send(side_y[k], dy=1)]

        others = steps_z[:-1]
        got = yield from_corner(both[half_ring]) + [send(both[1], dz=-1)] + fold(1)
        spread(half_ring, *got[:2])
        both[0] = add(both[0], got[2])
        own[1] = add(own[1], *got[3:])
        got = yield (fold(half_ring) + [send(both[k], dz=-k) for k in others[1:]])
        own[half_ring] = add(own[half_ring], *got[:2])
        both[0] = add(both[0], *got[2:])
        got = from_corner(both[0]) + [send(own[half_ring], dz=-1)]
        for k in others[1:]:
            got = got + fold(k)
        got = yield got
        spread(0, *got[:2])
        own[half_ring - 1] = add(own[half_ring - 1], got[2])
        for n, k in enumerate(others[1:]):
            own[k] = add(own[k], *got[3 + 2 * n : 5 + 2 * n])
        got = yield ([send(own[k], dz=-k) for k in others] + fold(0))
        yield total([v.astype(F32) for v in [own[0]] + list(got)])

    def step(run, got=None, beside=()):
        brought = run.send(got)
        tied = tie(*brought, *beside)
        return tied[: len(brought)], tied[len(brought) :]

    def sum_chips(values):
        values = values + send(values, dx=1)
        values = values + send(values, dy=1)
        return total([values] + [send(values, dz=k) for k in range(1, ring)])

    def scatter_rows(delta):
        grid = delta.astype(LOW).reshape(owners, delta.shape[0] // owners, delta.shape[1])
        parts = [
            lax.dynamic_index_in_dim(grid, slot_chip[q], 0, keepdims=False) for q in range(owners)
        ]
        run, got = scatter_chips(parts), None
        for _ in range(4):
            got, _unused = step(run, got)
        return run.send(got).astype(LOW)

    def gather_rows(mine, widths=None):
        widths = (mine.shape[1],) if widths is None else widths
        return [
            v.reshape(owners * v.shape[1], v.shape[2])
            for v in assemble(slot_chip, gather_chips(mine), widths)
        ]

    def cut(values, axis):
        size = values.shape[axis] // shards
        return [
            lax.dynamic_slice_in_dim(values, place(s) * size, size, axis) for s in range(shards)
        ]

    def natural(parts, axis):
        pieces = []
        for i in range(shards):
            piece = parts[0]
            for s in range(1, shards):
                piece = jnp.where(place(s) == i, parts[s], piece)
            pieces.append(piece)
        return jnp.concatenate(pieces, axis=axis)

    with jax.named_scope("early_gathers"):
        routes_own = sum_chips(
            jnp.zeros((owners, TOP, rows), jnp.int32).at[chip].set(routes.T)
        )
        token_parts = relative(tokens)
        gains_own = jnp.concatenate([attention_gain, query_gain, latent_gain, feedforward_gain])
        gain_parts = relative(gains_own)
        query_down_parts = relative(query_down)
        latent_down_parts = relative(latent_down)
        query_up_parts = relative(query_up)
        latent_up_parts = relative(latent_up)
        router_parts = relative(router)
        grad_own = lax.all_gather(cotangent, "expert", axis=0)

    hidden_all = shared_gate.shape[1]
    hidden_own = hidden_all // blocks
    hidden_shard = hidden_all // shards

    def shared_columns(weight):
        pieces = [
            lax.dynamic_slice_in_dim(
                weight, place(s) * hidden_shard + chip * hidden_own, hidden_own, 1
            ).T
            for s in range(shards)
        ]
        got = [pieces[0]] + [None] * (shards - 1)
        for s in range(1, shards):
            got[shards - s] = to_core(pieces[s], s)
        return natural(got, 1)

    with jax.named_scope("shared_weights"):
        padded = -(-hidden_own // LANES) * LANES
        pad = ((0, padded - hidden_own), (0, 0))
        pair_w = jnp.concatenate(
            [jnp.pad(shared_columns(shared_gate), pad), jnp.pad(shared_columns(shared_up), pad)]
        )
        down_w = jnp.pad(
            lax.dynamic_slice_in_dim(shared_down, chip * hidden_own, hidden_own, 0), pad
        )
        router_full = natural(router_parts, 0)

    with jax.named_scope("routing"):
        routes_all = jnp.stack(relative(routes_own), axis=2)[slot_chip].reshape(owners, TOP, span)
        expert_ids = jnp.arange(all_experts, dtype=jnp.int32)
        hits = jnp.any(
            routes_all[:, None] == expert_ids[None, :, None, None], axis=2
        )
        first = chip * local_count
        hit = lax.dynamic_slice_in_dim(hits, first, local_count, 1).astype(jnp.int32)
        pos = jnp.where(hit > 0, jnp.cumsum(hit, axis=2) - hit, -1)
        pos_cols = jnp.swapaxes(pos, 1, 2)
        room = shards * capacity
        counts = jnp.sum(hit, axis=2).T
        steps = (counts + ROW_STEP - 1) // ROW_STEP * ROW_STEP
        ends = jnp.cumsum(steps, axis=1)
        totals = ends[:, -1]
        offsets = jnp.concatenate([(ends - steps).reshape(-1), totals])
        counts = counts.reshape(-1)
        hits = hits.astype(F32)
        first_at = first.reshape(1).astype(jnp.int32)

    bounds = [0]
    for size in (part_cols, query_gain.shape[0], latent_gain.shape[0], part_cols):
        bounds.append(bounds[-1] + size)
    attention_gain_parts = [g[bounds[0] : bounds[1]].astype(F32) for g in gain_parts]
    query_gain_full = natural([g[bounds[1] : bounds[2]] for g in gain_parts], 0).astype(F32)
    latent_gain_full = natural([g[bounds[2] : bounds[3]] for g in gain_parts], 0).astype(F32)
    feed_gain_full = natural([g[bounds[3] : bounds[4]] for g in gain_parts], 0).astype(F32)
    gain_rel = jnp.concatenate(attention_gain_parts)

    with jax.named_scope("attention_forward"):
        positions = jnp.concatenate(
            [place(s) * rows + jnp.arange(rows, dtype=jnp.int32) for s in range(shards)]
        )
        cosine_table, sine_table = tables(positions, ROPE)
        length = seq_len[0]
        sequence = jnp.concatenate(token_parts, axis=0)
        source = jnp.concatenate(cut(sequence, 1), axis=1).astype(F32)
        source_scale = inverse_rms(source)
        normed = (source * source_scale * gain_rel).astype(LOW)
        normed_parts = jnp.split(normed, shards, axis=1)
        query_latent = total([product(a, w) for a, w in zip(normed_parts, query_down_parts)])
        query_scale = inverse_rms(query_latent)
        query_low = (query_latent * query_scale * query_gain_full).astype(LOW)
        latent = total([product(a, w) for a, w in zip(normed_parts, latent_down_parts)])
        latent_c = latent[:, :KVL]
        latent_scale = inverse_rms(latent_c)
        latent_low = (latent_c * latent_scale * latent_gain_full).astype(LOW)
        key_rope = rotate(latent[:, KVL:], cosine_table, sine_table).astype(LOW)
        query_low_parts = cut(query_low, 1)
        latent_low_parts = cut(latent_low, 1)
        query_raw = total(
            [product(a, cut(w, 1)[0]) for a, w in zip(query_low_parts, query_up_parts)]
        ).reshape(span, own_heads, NOPE + ROPE)
        query_nope = query_raw[..., :NOPE].astype(LOW)
        query_rope = rotate(
            query_raw[..., NOPE:], cosine_table[:, None, :], sine_table[:, None, :]
        ).astype(LOW)
        keys_values = (
            total([product(a, cut(w, 1)[0]) for a, w in zip(latent_low_parts, latent_up_parts)])
            .astype(LOW)
            .reshape(span, own_heads, NOPE + VDIM)
        )
        key_nope = keys_values[..., :NOPE]
        values = keys_values[..., NOPE:]
        score_scale = (NOPE + ROPE) ** (-0.5)
        allowed = (positions[None, :] <= positions[:, None]) & (positions[None, :] < length)
        raw_scores = jnp.einsum("qhd,khd->hqk", query_nope, key_nope, preferred_element_type=F32)
        raw_scores = raw_scores + jnp.einsum(
            "qhr,kr->hqk", query_rope, key_rope, preferred_element_type=F32
        )
        scores = jnp.where(allowed[None], raw_scores * score_scale, NEG)
        row_peak = jnp.max(scores, axis=-1, keepdims=True)
        exp_terms = jnp.exp(scores - row_peak)
        probabilities = exp_terms / jnp.sum(exp_terms, axis=-1, keepdims=True)
        p_low = probabilities.astype(LOW)
        mixed = jnp.einsum("hqk,khv->qhv", p_low, values, preferred_element_type=F32)
        mixed = mixed.astype(LOW).reshape(span, own_heads * VDIM)
        mixed, routes_own = tie(mixed, routes_own)
        attended = product(mixed, attention_out)
        resid = tokens.astype(F32) + sum_parts(jnp.split(attended, shards, axis=0), F32)
        resid_scale = inverse_rms(resid)
        ffn_low = (resid * resid_scale * feed_gain_full).astype(LOW)

    with jax.named_scope("token_gather"):
        ffn_slots = gather_chips(ffn_low, lambda v: relative(v)[1:])
        late = 2 * ring + steps_z[1]
        ffn_slots[late][0], grad_own = tie(ffn_slots[late][0], grad_own)
        ffn_parts = list(zip(*ffn_slots))
        grad_parts = relative(grad_own)

    with jax.named_scope("dispatch"):
        x_rows, g_rows, row_gates, feats, hiddens, delta_pair, delta_down = dispatch(
            shards, rows, room, offsets, first_at, slot_chip, hits, pos, router_full.T, pair_w,
            down_w, ffn_parts, grad_parts,
        )

    with jax.named_scope("routed_experts"):
        grad_rows, low_gate, low_up, weighted, gate_rows = run_experts(
            totals, first_at, x_rows, g_rows, row_gates, jnp.swapaxes(expert_gate, 1, 2),
            jnp.swapaxes(expert_up, 1, 2), expert_down,
        )

    with jax.named_scope("shared_gradients"):
        pair = jnp.stack(
            [delta_pair[:hidden_own], delta_pair[padded : padded + hidden_own]]
        )
        pieces = cut(pair, 2)
        got = [pieces[0]] + [None] * (shards - 1)
        for s in range(1, shards):
            got[shards - s] = to_core(pieces[s], s)
        pair = natural([v[None] for v in got], 0)
        pair_all = lax.all_gather(pair, "expert", axis=0)
        down_all = lax.all_gather(delta_down[:hidden_own], "expert", axis=0, tiled=True)

    with jax.named_scope("to_tokens"):

        def run_combine(columns, rows_all, gates_all, feat, weight):
            return combine(
                columns, ring, rows, shards, room, offsets, counts, slot_chip, rows_all, gates_all,
                pos_cols, feat, weight,
            )

        def over_cores(parts):
            number = len(parts) // shards
            sums = []
            for n in range(number):
                got = [to_core(parts[number * s + n], s) for s in range(1, shards)]
                for k in range(ring):
                    sums.append(add(parts[n][k], *[v[k] for v in got]))
            return sums

        *parts, gates_far = run_combine((3,), grad_rows, gate_rows, feats, pair_w)
        both = over_cores(parts)
        *both, grad_rows = tie(*both, grad_rows)
        *parts, gates_near = run_combine((0, 1, 2), grad_rows, gate_rows, feats, pair_w)
        mine = over_cores(parts)
        mine[-1], weighted = tie(mine[-1], weighted)
        run = scatter_chips(mine + both)
        got, unused = step(run)
        deltas = []
        for e in range(local_count):
            deltas = list(
                run_deltas(
                    e, deltas, totals, x_rows, g_rows, low_gate, low_up, weighted, expert_down
                )
            )
            if e < 2:
                got, (deltas[0], deltas[3]) = step(run, got, (deltas[0], deltas[3]))
        parts = list(run_combine((0, 1, 2, 3), deltas[3], None, hiddens, down_w))
        for _ in range(local_count, 2):
            got, unused = step(run, got)
        got, (parts[0], pair_all) = step(run, got, (parts[0], pair_all))
        grad_from_experts = run.send(got)
        delta_gate, delta_up, grad_expert_down, unused = deltas
        grad_expert_gate = jnp.swapaxes(delta_gate, 1, 2)
        grad_expert_up = jnp.swapaxes(delta_up, 1, 2)
        gate_grid = jnp.concatenate([gates_near, gates_far])
        gate_grid = lax.dynamic_slice_in_dim(gate_grid, first, local_count, 2)
        gate_grid = gate_grid.reshape(owners, shards, rows, local_count)
        gate_grid = sum_parts([gate_grid[:, s] for s in range(shards)], F32)
        gate_grid = jnp.zeros_like(gate_grid).at[slot_chip].set(gate_grid)
        grad_gates = lax.all_to_all(gate_grid, "expert", split_axis=0, concat_axis=0, tiled=True)
        grad_gates = jnp.swapaxes(grad_gates, 0, 1).reshape(rows, all_experts)
        out_run = scatter_chips(over_cores(parts))

    with jax.named_scope("feed_backward"):
        grad_out = cotangent.astype(F32)
        hit_own = jnp.any(routes[:, :, None] == expert_ids, axis=1).astype(F32)
        sig = jax.nn.sigmoid(product(ffn_low, router_full))
        chosen = sig * hit_own
        own_sum = jnp.sum(chosen, axis=1, keepdims=True)
        inner = jnp.sum(grad_gates * chosen, axis=1, keepdims=True)
        grad_chosen = ROUTE_SCALE * (grad_gates / own_sum - inner / (own_sum * own_sum))
        grad_logits = (grad_chosen * hit_own * sig * (1.0 - sig)).astype(LOW)
        grad_ffn = back_product(grad_logits, router_full) + grad_from_experts
        grad_resid_part, feed_terms = norm_back(resid, resid_scale, feed_gain_full, grad_ffn)
        grad_resid = grad_out + grad_resid_part
        grad_attended = grad_resid.astype(LOW)
        feed_gain_delta = jnp.sum(feed_terms, axis=0)

    with jax.named_scope("attention_backward"):
        attended_grads = jnp.concatenate(relative(grad_attended), axis=0)
        logit_grads = jnp.concatenate(relative(grad_logits), axis=0)
        delta_out = outer_sum(mixed, attended_grads).astype(LOW)
        ffn_sequence = cut(jnp.concatenate([part[0] for part in ffn_parts]), 1)[0]
        delta_router = outer_sum(logit_grads, ffn_sequence)
        grad_mixed = (
            back_product(attended_grads, attention_out).astype(LOW).reshape(span, own_heads, VDIM)
        )
        out_got, (grad_mixed,) = step(out_run, None, (grad_mixed,))
        grad_probs = jnp.einsum("qhv,khv->hqk", grad_mixed, values, preferred_element_type=F32)
        row_delta = jnp.sum(grad_probs * probabilities, axis=-1, keepdims=True)
        grad_raw = (score_scale * probabilities * (grad_probs - row_delta)).astype(LOW)
        out_got, (grad_raw,) = step(out_run, out_got, (grad_raw,))
        grad_query_nope = jnp.einsum("hqk,khd->qhd", grad_raw, key_nope, preferred_element_type=F32)
        grad_query_rope = jnp.einsum("hqk,kr->qhr", grad_raw, key_rope, preferred_element_type=F32)
        grad_key_nope = jnp.einsum("hqk,qhd->khd", grad_raw, query_nope, preferred_element_type=F32)
        grad_key_rope = jnp.einsum("hqk,qhr->kr", grad_raw, query_rope, preferred_element_type=F32)
        grad_values = jnp.einsum("hqk,qhv->khv", p_low, grad_mixed, preferred_element_type=F32)
        grad_keys = (
            jnp.concatenate([grad_key_nope, grad_values], axis=-1)
            .reshape(span, own_heads * (NOPE + VDIM))
            .astype(LOW)
        )
        grad_query_turned = rotate(
            grad_query_rope, cosine_table[:, None, :], -sine_table[:, None, :]
        )
        grad_queries = (
            jnp.concatenate([grad_query_nope, grad_query_turned], axis=-1)
            .reshape(span, own_heads * (NOPE + ROPE))
            .astype(LOW)
        )

        def reorder(values, s):
            pieces = jnp.split(values, shards, axis=0)
            return jnp.concatenate([pieces[(t - s) % shards] for t in range(shards)], axis=0)

        def every_core(values):
            return [values] + [reorder(from_core(values, s), s) for s in range(1, shards)]

        out_got, (grad_queries, grad_keys, grad_key_rope, down_all) = step(
            out_run, out_got, (grad_queries, grad_keys, grad_key_rope, down_all)
        )
        queries_back = natural(every_core(grad_queries), 1)
        keys_back = natural(every_core(grad_keys), 1)
        rope_back = total(every_core(grad_key_rope))
        grad_latent_normed = natural([back_product(keys_back, w) for w in latent_up_parts], 1)
        grad_latent_part, latent_terms = norm_back(
            latent_c, latent_scale, latent_gain_full, grad_latent_normed
        )
        grad_latent = jnp.concatenate(
            [grad_latent_part, rotate(rope_back, cosine_table, -sine_table)], axis=-1
        ).astype(LOW)
        grad_query_normed = natural([back_product(queries_back, w) for w in query_up_parts], 1)
        out_got, (grad_query_normed, grad_latent) = step(
            out_run, out_got, (grad_query_normed, grad_latent)
        )
        layer_out = (resid + out_run.send(out_got)).astype(LOW)
        grad_query_part, query_terms = norm_back(
            query_latent, query_scale, query_gain_full, grad_query_normed
        )
        grad_query_latent = grad_query_part.astype(LOW)
        down_delta = outer_sum(
            normed_parts[0], jnp.concatenate([grad_query_latent, grad_latent], axis=1)
        ).astype(LOW)
        up_delta = outer_sum(query_low_parts[0], queries_back).astype(LOW)
        latent_delta = outer_sum(latent_low_parts[0], keys_back).astype(LOW)
        down_delta, up_delta, latent_delta = tie(down_delta, up_delta, latent_delta)
        mine_wide = scatter_rows(jnp.concatenate([delta_out, down_delta], axis=1))
        mine_up = scatter_rows(up_delta)
        mine_latent = scatter_rows(latent_delta)
        mine_wide, pair_all, down_all = tie(mine_wide, pair_all, down_all)
        grad_shared_gate, grad_shared_up = transpose_pair(pair_all)
        grad_shared_down = down_all.astype(F32)
        wide_slots = gather_chips(mine_wide)
        (grad_query_up,) = gather_rows(mine_up)
        (grad_latent_up,) = gather_rows(mine_latent)
        grad_attention_out, grad_query_down, grad_latent_down = [
            v.reshape(owners * v.shape[1], v.shape[2])
            for v in assemble(
                slot_chip,
                wide_slots,
                (delta_out.shape[1], grad_query_latent.shape[1], grad_latent.shape[1]),
            )
        ]
        grad_normed = jnp.concatenate(
            [
                back_product(grad_query_latent[:rows], a) + back_product(grad_latent[:rows], b)
                for a, b in zip(query_down_parts, latent_down_parts)
            ],
            axis=1,
        )
        grad_source, attention_terms = norm_back(
            source[:rows], source_scale[:rows], gain_rel, grad_normed
        )
        grad_tokens = grad_resid + natural(jnp.split(grad_source, shards, axis=1), 1)

    with jax.named_scope("gain_gradients"):
        attention_delta = jnp.split(jnp.sum(attention_terms, axis=0), shards)
        feed_delta = cut(feed_gain_delta, 0)
        both = sum_parts(
            [jnp.concatenate([a, f]) for a, f in zip(attention_delta, feed_delta)], F32
        )
        query_delta = cut(jnp.sum(query_terms, axis=0), 0)[0]
        latent_delta = cut(jnp.sum(latent_terms, axis=0), 0)[0]
        sums = jnp.concatenate([delta_router.reshape(-1), both, query_delta, latent_delta])
        sums = sum_chips(sums.reshape(-1, part_cols)).reshape(-1)
        sizes = [all_experts * part_cols, part_cols, part_cols]
        sizes += [query_gain.shape[0], latent_gain.shape[0]]
        marks = [0]
        for size in sizes:
            marks.append(marks[-1] + size)
        grad_router, grad_attention_gain, grad_feed_gain, grad_query_gain, grad_latent_gain = [
            sums[a:b] for a, b in zip(marks, marks[1:])
        ]
        grad_router = grad_router.reshape(all_experts, part_cols).T

    return (
        layer_out,
        grad_tokens,
        grad_attention_gain,
        grad_query_down,
        grad_query_gain,
        grad_query_up,
        grad_latent_down,
        grad_latent_gain,
        grad_latent_up,
        grad_attention_out,
        grad_feed_gain,
        grad_router,
        grad_shared_gate,
        grad_shared_up,
        grad_shared_down,
        grad_expert_gate,
        grad_expert_up,
        grad_expert_down,
    )


def solution(mesh):
    tokens_spec = P(("expert", "shard"), None)
    rows_spec = P("shard", None)
    gain_spec = P("shard")
    expert_specs = (
        P("expert", None, "shard"),
        P("expert", None, "shard"),
        P("expert", "shard", None),
    )
    weight_specs = (
        gain_spec,
        rows_spec,
        gain_spec,
        rows_spec,
        rows_spec,
        gain_spec,
        rows_spec,
        rows_spec,
        gain_spec,
        rows_spec,
        rows_spec,
        rows_spec,
        rows_spec,
    ) + expert_specs
    return jax.shard_map(
        local,
        mesh=mesh,
        in_specs=(tokens_spec, tokens_spec, P("expert"), tokens_spec) + weight_specs,
        out_specs=(tokens_spec, tokens_spec) + weight_specs,
        check_vma=False,
    )
```

```python
import jax
import jax.numpy as jnp
import functools

from jax import lax
from jax.experimental import pallas as pl
from jax.experimental.pallas import tpu as pltpu
from jax.sharding import PartitionSpec as P

HEADS = 16
NOPE = 128
ROPE = 64
VDIM = 128
KVL = 512
TOP = 6

EPS = 1e-06
ROUTE_SCALE = 2.446
ROPE_BASE = 50000.0
NEG = -1e30

LOW = jnp.bfloat16
F32 = jnp.float32

LANES = 128
ROW_TILE = 512
HALF_TILE = 256
COL_TILE = 512
ROW_STEP = 16
VMEM_BYTES = 58 << 20


def tables(positions, rope_width):
    half_width = rope_width // 2
    frequencies = ROPE_BASE ** (-2.0 * jnp.arange(half_width, dtype=F32) / rope_width)
    angles = positions.astype(F32)[:, None] * frequencies[None, :]
    return (jnp.cos(angles), jnp.sin(angles))


def rotate(values, cosine_table, sine_table):
    half_width = values.shape[-1] // 2
    first_half = values[..., :half_width]
    second_half = values[..., half_width:]
    return jnp.concatenate(
        [
            first_half * cosine_table - second_half * sine_table,
            second_half * cosine_table + first_half * sine_table,
        ],
        axis=-1,
    )


def product(left_side, right_side):
    return jnp.dot(left_side, right_side, preferred_element_type=F32)


def outer_sum(left_side, right_side):
    return lax.dot_general(
        left_side, right_side, (((0,), (0,)), ((), ())), preferred_element_type=F32
    )


def back_product(left_side, right_side):
    return lax.dot_general(
        left_side, right_side, (((1,), (1,)), ((), ())), preferred_element_type=F32
    )


def tie(*arrays):
    return lax.optimization_barrier(arrays)


class Stages:
    def __init__(self, run):
        self.run, self.got, self.result = run, None, None

    def step(self, *beside):
        try:
            brought = self.run.send(self.got)
        except StopIteration as stop:
            self.run, self.result = None, stop.value
            return beside
        tied = tie(*brought, *beside)
        self.got = list(tied[: len(brought)])
        return tied[len(brought) :]

    def finish(self):
        while self.run is not None:
            self.step()
        return self.result


def total(terms):
    result = terms[0]
    for term in terms[1:]:
        result = result + term
    return result


def inverse_rms(values):
    return lax.rsqrt(jnp.mean(values * values, axis=-1, keepdims=True) + EPS)


def norm_back(values, scale, gain, grad):
    weighted = grad * gain
    inner = jnp.mean(weighted * values, axis=-1, keepdims=True)
    return scale * weighted - values * (scale * scale * scale) * inner, grad * values * scale


def silu_parts(gate_part):
    sig = jax.nn.sigmoid(gate_part)
    return gate_part * sig, sig * (1.0 + gate_part * (1.0 - sig))


def fetch_group(x_parts, g_parts, x_buf, g_buf, sems, slot, q, rows):
    for number in range(len(x_parts[0])):

        @pl.when(q == number)
        def _(number=number):
            for kind, (parts, buffer) in enumerate(((g_parts, g_buf), (x_parts, x_buf))):
                for s, arrays in enumerate(parts):
                    here = pl.ds(s * rows, rows)
                    pltpu.make_async_copy(
                        arrays[number], buffer.at[slot, here], sems.at[slot, kind, s]
                    ).start()


def wait_group(x_parts, x_buf, g_buf, sems, slot, rows):
    for kind, buffer in enumerate((g_buf, x_buf)):
        for s, arrays in enumerate(x_parts):
            here = buffer.at[slot, pl.ds(s * rows, rows)]
            pltpu.make_async_copy(arrays[0], here, sems.at[slot, kind, s]).wait()


def dispatch_kernel(owners, shards, rows, room, offsets, first, hits, pos, router_t, pair_w, down_w, *rest):
    x_parts = [rest[owners * s : owners * (s + 1)] for s in range(shards)]
    rest = rest[owners * shards :]
    g_parts = [rest[owners * s : owners * (s + 1)] for s in range(shards)]
    rest = rest[owners * shards :]
    x_rows, g_rows, row_gates, feats, hiddens, delta_pair, delta_down = rest[:7]
    x_buf, g_buf, in_sem, x_stage, g_stage, gate_stage, out_sem, zeros, zero_gates, acc_pair, acc_down = rest[7:]
    q, count = pl.program_id(0), pl.num_programs(0)
    slot = lax.rem(q, 2)
    local_count = pos.shape[1]
    width = down_w.shape[0]

    @pl.when(q == 0)
    def _():
        fetch_group(x_parts, g_parts, x_buf, g_buf, in_sem, 0, 0, rows)
        acc_pair[...] = jnp.zeros_like(acc_pair)
        acc_down[...] = jnp.zeros_like(acc_down)
        zeros[...] = jnp.zeros_like(zeros)
        zero_gates[...] = jnp.zeros_like(zero_gates)

    @pl.when(q + 1 < count)
    def _():
        fetch_group(x_parts, g_parts, x_buf, g_buf, in_sem, 1 - slot, q + 1, rows)

    wait_group(x_parts, x_buf, g_buf, in_sem, slot, rows)
    x, g = x_buf[slot], g_buf[slot]

    sig = jax.nn.sigmoid(back_product(router_t[...], x))
    chosen = sig * hits[0]
    gates = ROUTE_SCALE * chosen / jnp.sum(chosen, axis=0, keepdims=True)
    numbers = lax.broadcasted_iota(jnp.int32, gates.shape, 0)
    places = lax.broadcasted_iota(jnp.int32, (room, x.shape[0]), 0)
    picks = []
    for e in range(local_count):
        gate = jnp.sum(jnp.where(numbers == first[0] + e, gates, 0.0), axis=0, keepdims=True)
        pick = places == pos[0, e : e + 1]
        row_gate = jnp.sum(jnp.where(pick, gate, 0.0), axis=1, keepdims=True)
        gate_stage[slot, e] = jnp.broadcast_to(row_gate, (room, LANES))
        picks.append(jnp.where(pick, 1.0, 0.0).astype(LOW))
    picks = jnp.concatenate(picks, axis=0)
    x_stage[slot] = product(picks, x).astype(LOW).reshape(local_count, room, -1)
    g_stage[slot] = product(picks, g).astype(LOW).reshape(local_count, room, -1)

    def writes(which, at):
        start = [pl.multiple_of(offsets[e * count + at], ROW_STEP) for e in range(local_count)]
        return [
            pltpu.make_async_copy(
                stage.at[which, e], array.at[e, pl.ds(start[e], room)], out_sem.at[which, k, e]
            )
            for e in range(local_count)
            for k, (stage, array) in enumerate(
                ((x_stage, x_rows), (g_stage, g_rows), (gate_stage, row_gates))
            )
        ]

    @pl.when(q > 0)
    def _():
        for copy in writes(1 - slot, q - 1):
            copy.wait()

    for copy in writes(slot, q):
        copy.start()

    both = back_product(x, pair_w[...])
    gate_part, up_part = both[:, :width], both[:, width:]
    silu_part, slope = silu_parts(gate_part)
    hidden = (silu_part * up_part).astype(LOW)
    back = back_product(g, down_w[...])
    feat = jnp.concatenate(
        [(back * up_part * slope).astype(LOW), (back * silu_part).astype(LOW)], axis=1
    )
    feats[...] = feat
    hiddens[...] = hidden
    acc_pair[...] += outer_sum(feat, x)
    acc_down[...] += outer_sum(hidden, g)

    @pl.when(q == count - 1)
    def _():
        for copy in writes(slot, q):
            copy.wait()
        tails = []
        for e in range(local_count):
            end = pl.multiple_of(offsets[local_count * count + e], ROW_STEP)
            for k, (stage, array) in enumerate(
                ((zeros, x_rows), (zeros, g_rows), (zero_gates, row_gates))
            ):
                tails.append(
                    pltpu.make_async_copy(
                        stage, array.at[e, pl.ds(end, HALF_TILE)], out_sem.at[slot, k, e]
                    )
                )
        for copy in tails:
            copy.start()
        delta_pair[...] = acc_pair[...].astype(LOW)
        delta_down[...] = acc_down[...].astype(LOW)
        for copy in tails:
            copy.wait()


def expert_kernel(totals, first, x, g, row_gate, w_gate, w_up, w_down, grad_row, grad_gate, grad_up, weighted, gate_grad):
    e, t = pl.program_id(0), pl.program_id(1)
    left = totals[e] - t * ROW_TILE

    def work(count):
        here = pl.ds(0, count)
        width = x.shape[2]
        gate = row_gate[0, here][:, :1]
        gate_part = back_product(x[0, here], w_gate[0])
        up_part = back_product(x[0, here], w_up[0])
        silu_part, slope = silu_parts(gate_part)
        hidden = (silu_part * up_part).astype(LOW)
        back = back_product(g[0, here], w_down[0])
        wide = hidden.astype(F32)
        own = jnp.sum(wide * back, axis=1, keepdims=True)
        lanes = lax.broadcasted_iota(jnp.int32, (count, LANES), 1)
        gate_grad[0, here] = jnp.where(lanes == first[0] + e, own, 0.0)
        back = back * gate
        low_gate = (back * up_part * slope).astype(LOW)
        low_up = (back * silu_part).astype(LOW)
        grad_gate[0, here] = low_gate
        grad_up[0, here] = low_up
        weighted[0, here] = (wide * gate).astype(LOW)
        for at in range(0, width, COL_TILE):
            cols = pl.ds(at, COL_TILE)
            grad_row[0, here, cols] = (
                product(low_gate, w_gate[0, :, cols]) + product(low_up, w_up[0, :, cols])
            ).astype(LOW)

    @pl.when(left > HALF_TILE)
    def _():
        work(ROW_TILE)

    @pl.when((left > 0) & (left <= HALF_TILE))
    def _():
        work(HALF_TILE)


def delta_kernel(e, chained, totals, x, g, grad_gate, grad_up, weighted, w_down, *rest):
    delta_gate, delta_up, delta_down, result = rest[chained:]
    t = pl.program_id(0)
    left = totals[e] - t * ROW_TILE

    @pl.when(t == 0)
    def _():
        delta_gate[...] = jnp.zeros_like(delta_gate)
        delta_up[...] = jnp.zeros_like(delta_up)
        delta_down[...] = jnp.zeros_like(delta_down)

    def work(count):
        here = pl.ds(0, count)
        delta_gate[0] += outer_sum(grad_gate[0, here], x[0, here])
        delta_up[0] += outer_sum(grad_up[0, here], x[0, here])
        delta_down[0] += outer_sum(weighted[0, here], g[0, here])
        for at in range(0, x.shape[2], COL_TILE):
            cols = pl.ds(at, COL_TILE)
            result[0, here, cols] = product(weighted[0, here], w_down[0, :, cols]).astype(LOW)

    @pl.when(left > HALF_TILE)
    def _():
        work(ROW_TILE)

    @pl.when((left > 0) & (left <= HALF_TILE))
    def _():
        work(HALF_TILE)


def combine_kernel(base, columns, ring, room, shards, with_gates, offsets, counts, order, rows_all, gates_all, pos, feat, weight, *rest):
    number = max(len(columns), 1) * shards
    outs, rest = rest[:number], rest[number:]
    if with_gates:
        gate_out, rest = rest[0], rest[1:]
    rows_buf, gates_buf, sems = rest
    step, steps = pl.program_id(0), pl.num_programs(0)
    slot = lax.rem(step, 2)
    local_count = rows_all.shape[0]
    count = counts.shape[0] // local_count

    def reads(which, at):
        copies = []
        for e in range(local_count):
            start = pl.multiple_of(offsets[e * count + base + at], ROW_STEP)
            copies.append(
                pltpu.make_async_copy(
                    rows_all.at[e, pl.ds(start, room)], rows_buf.at[which, e], sems.at[which, 0, e]
                )
            )
            if with_gates:
                copies.append(
                    pltpu.make_async_copy(
                        gates_all.at[e, pl.ds(start, room)],
                        gates_buf.at[which, e],
                        sems.at[which, 1, e],
                    )
                )
        return copies

    @pl.when(step == 0)
    def _():
        for copy in reads(0, 0):
            copy.start()

    @pl.when(step + 1 < steps)
    def _():
        for copy in reads(1 - slot, step + 1):
            copy.start()

    for copy in reads(slot, step):
        copy.wait()

    tokens = pos.shape[1]
    places = lax.broadcasted_iota(jnp.int32, (tokens, room), 1)
    row_ids = lax.broadcasted_iota(jnp.int32, (room, 1), 0)
    picks, rows, gate_sum = [], [], None
    for e in range(local_count):
        valid = row_ids < counts[e * count + base + step]
        pick = jnp.where(places == pos[0][:, e : e + 1], 1.0, 0.0)
        picks.append(pick.astype(LOW))
        rows.append(jnp.where(valid, rows_buf[slot, e], jnp.zeros((), LOW)))
        if with_gates:
            gates = jnp.where(valid, gates_buf[slot, e], 0.0)
            for _ in range(3):
                term = gates.astype(LOW)
                gates = gates - term.astype(F32)
                term = product(picks[-1], term)
                gate_sum = term if gate_sum is None else gate_sum + term
    low = (
        product(feat[...], weight[...])
        + product(jnp.concatenate(picks, axis=1), jnp.concatenate(rows, axis=0))
    ).astype(LOW)
    share = tokens // shards
    for s in range(shards):
        mine = low[s * share : (s + 1) * share]
        if columns:
            for n in range(len(columns)):

                @pl.when(step // ring == n)
                def _(n=n, s=s, mine=mine):
                    outs[len(columns) * s + n][0] = mine
        else:
            outs[s][0] = mine
    if with_gates:
        gate_out[0] = gate_sum


def assemble_kernel(owners, widths, order, *refs):
    outs = refs[owners:]
    for q in range(owners):
        at = 0
        for out, width in zip(outs, widths):
            out[order[q]] = refs[q][:, at : at + width].astype(F32)
            at += width


def transpose_kernel(shards, owners, own, every, gate_out, up_out, table):
    which, k = pl.program_id(0), pl.program_id(1)

    @pl.when(k == 0)
    def _():
        for s in range(shards):
            for q in range(owners):
                table[pl.ds((s * owners + q) * own, own)] = every[q, s, 0].astype(F32)

    piece = table[pl.ds(pl.multiple_of(k * LANES, LANES), LANES)].T

    @pl.when(which == 0)
    def _():
        gate_out[...] = piece

    @pl.when(which == 1)
    def _():
        up_out[...] = piece


def params(*semantics):
    return pltpu.CompilerParams(dimension_semantics=semantics, vmem_limit_bytes=VMEM_BYTES)


def assemble(order, arrays, widths):
    owners = len(arrays)
    rows = arrays[0].shape[0]
    whole = lambda *_: (0, 0)
    return pl.pallas_call(
        functools.partial(assemble_kernel, owners, widths),
        grid_spec=pltpu.PrefetchScalarGridSpec(
            num_scalar_prefetch=1,
            grid=(1,),
            in_specs=[pl.BlockSpec(a.shape, whole) for a in arrays],
            out_specs=[pl.BlockSpec((owners, rows, w), lambda *_: (0, 0, 0)) for w in widths],
        ),
        out_shape=[jax.ShapeDtypeStruct((owners, rows, w), F32) for w in widths],
        compiler_params=params("arbitrary"),
        cost_estimate=pl.CostEstimate(
            flops=0, bytes_accessed=owners * rows * sum(widths) * 6, transcendentals=0
        ),
    )(order, *arrays)


def transpose_pair(every):
    owners, shards, unused, own, cols = every.shape
    hidden = owners * shards * own
    tiles = hidden // LANES
    return pl.pallas_call(
        functools.partial(transpose_kernel, shards, owners, own),
        grid=(2, tiles),
        in_specs=[
            pl.BlockSpec((owners, shards, 1, own, cols), lambda w, k: (0, 0, w, 0, 0)),
        ],
        out_specs=[
            pl.BlockSpec((cols, LANES), lambda w, k: (0, jnp.where(w == 0, k, tiles - 1))),
            pl.BlockSpec((cols, LANES), lambda w, k: (0, jnp.where(w == 0, 0, k))),
        ],
        out_shape=[jax.ShapeDtypeStruct((cols, hidden), F32)] * 2,
        scratch_shapes=[pltpu.VMEM((hidden, cols), F32)],
        compiler_params=params("arbitrary", "arbitrary"),
        cost_estimate=pl.CostEstimate(
            flops=0, bytes_accessed=12 * hidden * cols, transcendentals=0
        ),
    )(every)


def dispatch(shards, rows, room, offsets, first, hits, pos, router_t, pair_w, down_w, x_parts, g_parts):
    owners, all_experts, span = hits.shape
    local_count = pos.shape[1]
    width = router_t.shape[1]
    hidden = down_w.shape[0]
    capacity = -(-(owners * room + HALF_TILE) // ROW_TILE) * ROW_TILE
    flat = [a for part in x_parts for a in part] + [a for part in g_parts for a in part]
    whole = lambda q, *_: (0, 0)
    anywhere = pl.BlockSpec(memory_space=pl.ANY)
    return pl.pallas_call(
        functools.partial(dispatch_kernel, owners, shards, rows, room),
        grid_spec=pltpu.PrefetchScalarGridSpec(
            num_scalar_prefetch=2,
            grid=(owners,),
            in_specs=[
                pl.BlockSpec((1, all_experts, span), lambda q, *_: (q, 0, 0)),
                pl.BlockSpec((1, local_count, span), lambda q, *_: (q, 0, 0)),
                pl.BlockSpec((all_experts, width), whole),
                pl.BlockSpec((2 * hidden, width), whole),
                pl.BlockSpec((hidden, width), whole),
            ]
            + [anywhere] * len(flat),
            out_specs=[
                anywhere,
                anywhere,
                anywhere,
                pl.BlockSpec((span, 2 * hidden), lambda q, *_: (q, 0)),
                pl.BlockSpec((span, hidden), lambda q, *_: (q, 0)),
                pl.BlockSpec((2 * hidden, width), whole),
                pl.BlockSpec((hidden, width), whole),
            ],
            scratch_shapes=[
                pltpu.VMEM((2, span, width), LOW),
                pltpu.VMEM((2, span, width), LOW),
                pltpu.SemaphoreType.DMA((2, 2, shards)),
                pltpu.VMEM((2, local_count, room, width), LOW),
                pltpu.VMEM((2, local_count, room, width), LOW),
                pltpu.VMEM((2, local_count, room, LANES), F32),
                pltpu.SemaphoreType.DMA((2, 3, local_count)),
                pltpu.VMEM((HALF_TILE, width), LOW),
                pltpu.VMEM((HALF_TILE, LANES), F32),
                pltpu.VMEM((2 * hidden, width), F32),
                pltpu.VMEM((hidden, width), F32),
            ],
        ),
        out_shape=[
            jax.ShapeDtypeStruct((local_count, capacity, width), LOW),
            jax.ShapeDtypeStruct((local_count, capacity, width), LOW),
            jax.ShapeDtypeStruct((local_count, capacity, LANES), F32),
            jax.ShapeDtypeStruct((owners * span, 2 * hidden), LOW),
            jax.ShapeDtypeStruct((owners * span, hidden), LOW),
            jax.ShapeDtypeStruct((2 * hidden, width), LOW),
            jax.ShapeDtypeStruct((hidden, width), LOW),
        ],
        compiler_params=params("arbitrary"),
        cost_estimate=pl.CostEstimate(
            flops=14 * owners * span * width * span,
            bytes_accessed=4 * owners * span * width,
            transcendentals=0,
        ),
    )(offsets, first, hits, pos, router_t, pair_w, down_w, *flat)


def tile_map(e, t, totals, *_):
    last = jnp.maximum((totals[e] + ROW_TILE - 1) // ROW_TILE - 1, 0)
    return (e, jnp.minimum(t, last), 0)


def expert_map(e, t, *_):
    return (e, 0, 0)


def run_experts(totals, first, x, g, row_gate, w_gate, w_up, w_down):
    local_count, capacity, width = x.shape
    hidden = w_gate.shape[1]
    tiles = capacity // ROW_TILE
    wide = pl.BlockSpec((1, ROW_TILE, width), tile_map)
    slim = pl.BlockSpec((1, ROW_TILE, hidden), tile_map)
    lane = pl.BlockSpec((1, ROW_TILE, LANES), tile_map)
    return pl.pallas_call(
        expert_kernel,
        grid_spec=pltpu.PrefetchScalarGridSpec(
            num_scalar_prefetch=2,
            grid=(local_count, tiles),
            in_specs=[
                wide,
                wide,
                lane,
                pl.BlockSpec((1, hidden, width), expert_map),
                pl.BlockSpec((1, hidden, width), expert_map),
                pl.BlockSpec((1, hidden, width), expert_map),
            ],
            out_specs=[wide, slim, slim, slim, lane],
        ),
        out_shape=[
            jax.ShapeDtypeStruct(x.shape, LOW),
            jax.ShapeDtypeStruct((local_count, capacity, hidden), LOW),
            jax.ShapeDtypeStruct((local_count, capacity, hidden), LOW),
            jax.ShapeDtypeStruct((local_count, capacity, hidden), LOW),
            jax.ShapeDtypeStruct(row_gate.shape, F32),
        ],
        compiler_params=params("arbitrary", "arbitrary"),
        cost_estimate=pl.CostEstimate(
            flops=5 * local_count * capacity * width * hidden,
            bytes_accessed=6 * local_count * width * (capacity + hidden),
            transcendentals=0,
        ),
    )(totals, first, x, g, row_gate, w_gate, w_up, w_down)


def run_deltas(e, before, totals, x, g, grad_gate, grad_up, weighted, w_down):
    local_count, capacity, width = x.shape
    hidden = grad_gate.shape[2]
    tiles = capacity // ROW_TILE

    def rows_at(t, totals):
        return tile_map(e, t, totals)

    def expert_at(t, totals):
        return (e, 0, 0)

    wide = pl.BlockSpec((1, ROW_TILE, width), rows_at)
    slim = pl.BlockSpec((1, ROW_TILE, hidden), rows_at)
    once = pl.BlockSpec((1, hidden, width), expert_at, pipeline_mode=pl.Buffered(1))
    return pl.pallas_call(
        functools.partial(delta_kernel, e, len(before)),
        grid_spec=pltpu.PrefetchScalarGridSpec(
            num_scalar_prefetch=1,
            grid=(tiles,),
            in_specs=[wide, wide, slim, slim, slim, once]
            + [pl.BlockSpec(memory_space=pl.ANY)] * len(before),
            out_specs=[once] * 3 + [wide],
        ),
        out_shape=[jax.ShapeDtypeStruct((local_count, hidden, width), F32)] * 3
        + [jax.ShapeDtypeStruct(x.shape, LOW)],
        input_output_aliases={7 + i: i + 4 - len(before) for i in range(len(before))},
        compiler_params=params("arbitrary"),
        cost_estimate=pl.CostEstimate(
            flops=4 * capacity * width * hidden,
            bytes_accessed=12 * width * hidden,
            transcendentals=0,
        ),
    )(totals, x, g, grad_gate, grad_up, weighted, w_down, *before)


def combine(columns, ring, rows, shards, room, offsets, counts, order, rows_all, gates_all, pos, feat, weight):
    local_count, capacity, width = rows_all.shape
    owners, span = pos.shape[:2]
    with_gates = gates_all is not None
    base = columns[0] * ring if columns else 0
    steps = len(columns) * ring if columns else owners
    if columns:
        out_shape = [jax.ShapeDtypeStruct((ring, rows, width), LOW)] * (len(columns) * shards)
        out_specs = [
            pl.BlockSpec(
                (1, rows, width),
                lambda q, *_, n=n: (jnp.clip(q - n * ring, 0, ring - 1), 0, 0),
            )
            for s in range(shards)
            for n in range(len(columns))
        ]
    else:
        out_shape = [jax.ShapeDtypeStruct((owners, rows, width), LOW)] * shards
        out_specs = [
            pl.BlockSpec((1, rows, width), lambda q, offsets, counts, order: (order[q], 0, 0))
        ] * shards
    if with_gates:
        out_shape = out_shape + [jax.ShapeDtypeStruct((steps, span, LANES), F32)]
        out_specs = out_specs + [pl.BlockSpec((1, span, LANES), lambda q, *_: (q, 0, 0))]
    return pl.pallas_call(
        functools.partial(combine_kernel, base, columns, ring, room, shards, with_gates),
        grid_spec=pltpu.PrefetchScalarGridSpec(
            num_scalar_prefetch=3,
            grid=(steps,),
            in_specs=[
                pl.BlockSpec(memory_space=pl.ANY),
                pl.BlockSpec(memory_space=pl.ANY),
                pl.BlockSpec((1, span, local_count), lambda q, *_: (base + q, 0, 0)),
                pl.BlockSpec((span, feat.shape[1]), lambda q, *_: (base + q, 0)),
                pl.BlockSpec(weight.shape, lambda q, *_: (0, 0)),
            ],
            out_specs=out_specs,
            scratch_shapes=[
                pltpu.VMEM((2, local_count, room, width), LOW),
                pltpu.VMEM((2, local_count, room, LANES), F32),
                pltpu.SemaphoreType.DMA((2, 2, local_count)),
            ],
        ),
        out_shape=out_shape,
        compiler_params=params("arbitrary"),
        cost_estimate=pl.CostEstimate(
            flops=4 * steps * span * width * span,
            bytes_accessed=4 * steps * span * width,
            transcendentals=0,
        ),
    )(offsets, counts, order, rows_all, gates_all if with_gates else rows_all, pos, feat, weight)


def local(
    tokens,
    cotangent,
    seq_len,
    routes,
    attention_gain,
    query_down,
    query_gain,
    query_up,
    latent_down,
    latent_gain,
    latent_up,
    attention_out,
    feedforward_gain,
    router,
    shared_gate,
    shared_up,
    shared_down,
    expert_gate,
    expert_up,
    expert_down,
):
    rows, width = tokens.shape
    shards = lax.axis_size("shard")
    owners = lax.axis_size("expert")
    core = lax.axis_index("shard")
    chip = lax.axis_index("expert")
    local_count = expert_gate.shape[0]
    all_experts = local_count * owners
    capacity = 2 * rows * TOP // all_experts
    span = rows * shards
    blocks = shards * owners
    own_heads = HEADS // shards
    part_cols = width // shards

    def place(s):
        return (core - s) % shards

    def from_core(values, s):
        return lax.ppermute(values, "shard", [(i, (i + s) % shards) for i in range(shards)])

    def to_core(values, s):
        return lax.ppermute(values, "shard", [(i, (i - s) % shards) for i in range(shards)])

    def relative(values):
        return [values] + [from_core(values, s) for s in range(1, shards)]

    def sum_parts(parts, kind):
        got = [to_core(parts[s].astype(kind), s).astype(F32) for s in range(1, shards)]
        return total([parts[0].astype(F32)] + got)

    ring = owners // 4
    z_at, y_at, x_at = chip // 4, chip // 2 % 2, chip % 2

    def send(values, dz=0, dy=0, dx=0):
        pairs = []
        for i in range(owners):
            z, y, x = i // 4, i // 2 % 2, i % 2
            pairs.append((i, (z + dz) % ring * 4 + (y ^ dy) * 2 + (x ^ dx)))
        return lax.ppermute(values, "expert", pairs)

    slot_chip = jnp.stack(
        [
            (z_at - k) % ring * 4 + (y_at ^ (col // 2)) * 2 + (x_at ^ (col % 2))
            for col in range(4)
            for k in range(ring)
        ]
    ).astype(jnp.int32)

    half_ring = ring // 2

    def middle(values):
        return max(values.shape[-1] // 2 // LANES * LANES, 1)

    steps_z = [1, ring - 1] + [k for k in range(2, ring - 1) if k != half_ring] + [half_ring]

    def gather_chips(values, relay=None):
        half = middle(values)
        slots, relayed = {("own", 0): values}, {}
        waiting = [("own", 0)]

        def stage(sends):
            nonlocal waiting
            fresh = {}
            for key in waiting:
                fresh[key] = relay(slots[key]) if relay else []
            flat, marks = [], []
            for key, arrays in list(sends.items()) + [(("core",) + k, v) for k, v in fresh.items()]:
                marks.append((key, len(arrays)))
                flat += arrays
            flat = list((yield flat))
            waiting = []
            for key, number in marks:
                arrays, flat = flat[:number], flat[number:]
                if key[0] == "core":
                    relayed[key[1:]] = arrays
                else:
                    slots[key] = arrays[0] if number == 1 else jnp.concatenate(arrays, axis=1)
                    waiting.append(key)

        def along(k):
            source = slots["own", half_ring - 1] if k == half_ring else values
            return {("own", k): [send(source, dz=1 if k == half_ring else k)]}

        def sides(k):
            return {
                ("x", k): [send(slots["own", k], dx=1)],
                ("y", k): [send(slots["own", k], dy=1)],
            }

        def corner(k):
            left = send(slots["y", k][:, :half], dx=1)
            right = send(slots["x", k][:, half:], dy=1)
            return {("both", k): [left, right]}

        def far(k):
            return {("both", k): [send(slots["both", 0], dz=k)]}

        for i, k in enumerate(steps_z):
            group = along(k) | sides(steps_z[i - 1] if i else 0)
            yield from stage(group | corner(0) if i == 1 else group)
        yield from stage(sides(half_ring) | far(steps_z[0]))
        last = corner(half_ring)
        for k in steps_z[1:-1]:
            last = last | far(k)
        yield from stage(last)
        for key in waiting:
            relayed[key] = relay(slots[key]) if relay else []
        keys = [(col, k) for col in ("own", "x", "y", "both") for k in range(ring)]
        if relay:
            return [[slots[key]] + relayed[key] for key in keys]
        return [slots[key] for key in keys]

    def add(a, *terms):
        return total([v.astype(F32) for v in (a,) + terms]).astype(LOW)

    def scatter_chips(parts):
        own, side_x, side_y, both = (list(parts[i * ring : (i + 1) * ring]) for i in range(4))
        half = middle(both[0])

        def from_corner(block):
            return [send(block[:, :half], dx=1), send(block[:, half:], dy=1)]

        def spread(k, for_y, for_x):
            side_y[k] = jnp.concatenate([add(side_y[k][:, :half], for_y), side_y[k][:, half:]], axis=1)
            side_x[k] = jnp.concatenate([side_x[k][:, :half], add(side_x[k][:, half:], for_x)], axis=1)

        def fold(k):
            return [send(side_x[k], dx=1), send(side_y[k], dy=1)]

        others = steps_z[:-1]
        got = yield from_corner(both[half_ring]) + [send(both[1], dz=-1)] + fold(1)
        spread(half_ring, *got[:2])
        both[0] = add(both[0], got[2])
        own[1] = add(own[1], *got[3:])
        got = yield (fold(half_ring) + [send(both[k], dz=-k) for k in others[1:]])
        own[half_ring] = add(own[half_ring], *got[:2])
        both[0] = add(both[0], *got[2:])
        got = from_corner(both[0]) + [send(own[half_ring], dz=-1)]
        for k in others[1:]:
            got = got + fold(k)
        got = yield got
        spread(0, *got[:2])
        own[half_ring - 1] = add(own[half_ring - 1], got[2])
        for n, k in enumerate(others[1:]):
            own[k] = add(own[k], *got[3 + 2 * n : 5 + 2 * n])
        got = yield ([send(own[k], dz=-k) for k in others] + fold(0))
        return total([v.astype(F32) for v in [own[0]] + list(got)])

    def sum_chips(values):
        values = values + send(values, dx=1)
        values = values + send(values, dy=1)
        return total([values] + [send(values, dz=k) for k in range(1, ring)])

    def scatter_rows(*deltas):
        def share(q):
            pieces = []
            for delta in deltas:
                height = delta.shape[0] // owners
                pieces.append(lax.dynamic_slice_in_dim(delta, slot_chip[q] * height, height, 0))
            return jnp.concatenate(pieces, axis=1)

        return Stages(scatter_chips([share(q) for q in range(owners)])).finish().astype(LOW)

    def gather_rows(mine, widths=None):
        widths = (mine.shape[1],) if widths is None else widths
        return [
            v.reshape(owners * v.shape[1], v.shape[2])
            for v in assemble(slot_chip, Stages(gather_chips(mine)).finish(), widths)
        ]

    def cut(values, axis):
        size = values.shape[axis] // shards
        return [
            lax.dynamic_slice_in_dim(values, place(s) * size, size, axis) for s in range(shards)
        ]

    def natural(parts, axis):
        pieces = []
        for i in range(shards):
            piece = parts[0]
            for s in range(1, shards):
                piece = jnp.where(place(s) == i, parts[s], piece)
            pieces.append(piece)
        return jnp.concatenate(pieces, axis=axis)

    with jax.named_scope("early_gathers"):
        routes_own = lax.all_gather(routes.T, "expert", axis=0)
        token_parts = relative(tokens)
        gains_own = jnp.concatenate([attention_gain, query_gain, latent_gain, feedforward_gain])
        gain_parts = relative(gains_own)
        query_down_parts = relative(query_down)
        latent_down_parts = relative(latent_down)
        query_up_parts = relative(query_up)
        latent_up_parts = relative(latent_up)
        router_parts = relative(router)
        relay = lambda v: relative(v)[1:]
        grad_run = Stages(gather_chips(cotangent, relay))

    hidden_all = shared_gate.shape[1]
    hidden_own = hidden_all // blocks
    hidden_shard = hidden_all // shards

    def shared_columns(weight):
        pieces = [
            lax.dynamic_slice_in_dim(
                weight, place(s) * hidden_shard + chip * hidden_own, hidden_own, 1
            ).T
            for s in range(shards)
        ]
        got = [pieces[0]] + [None] * (shards - 1)
        for s in range(1, shards):
            got[shards - s] = to_core(pieces[s], s)
        return natural(got, 1)

    with jax.named_scope("shared_weights"):
        padded = -(-hidden_own // LANES) * LANES
        pad = ((0, padded - hidden_own), (0, 0))
        pair_w = jnp.concatenate(
            [jnp.pad(shared_columns(shared_gate), pad), jnp.pad(shared_columns(shared_up), pad)]
        )
        down_w = jnp.pad(
            lax.dynamic_slice_in_dim(shared_down, chip * hidden_own, hidden_own, 0), pad
        )
        router_full = natural(router_parts, 0)

    with jax.named_scope("routing"):
        routes_all = jnp.stack(relative(routes_own), axis=2)[slot_chip].reshape(owners, TOP, span)
        expert_ids = jnp.arange(all_experts, dtype=jnp.int32)
        hits = jnp.any(
            routes_all[:, None] == expert_ids[None, :, None, None], axis=2
        )
        first = chip * local_count
        hit = lax.dynamic_slice_in_dim(hits, first, local_count, 1).astype(jnp.int32)
        pos = jnp.where(hit > 0, jnp.cumsum(hit, axis=2) - hit, -1)
        pos_cols = jnp.swapaxes(pos, 1, 2)
        room = shards * capacity
        counts = jnp.sum(hit, axis=2).T
        steps = (counts + ROW_STEP - 1) // ROW_STEP * ROW_STEP
        ends = jnp.cumsum(steps, axis=1)
        totals = ends[:, -1]
        offsets = jnp.concatenate([(ends - steps).reshape(-1), totals])
        counts = counts.reshape(-1)
        hits = hits.astype(F32)
        first_at = first.reshape(1).astype(jnp.int32)

    bounds = [0]
    for size in (part_cols, query_gain.shape[0], latent_gain.shape[0], part_cols):
        bounds.append(bounds[-1] + size)
    attention_gain_parts = [g[bounds[0] : bounds[1]].astype(F32) for g in gain_parts]
    query_gain_full = natural([g[bounds[1] : bounds[2]] for g in gain_parts], 0).astype(F32)
    latent_gain_full = natural([g[bounds[2] : bounds[3]] for g in gain_parts], 0).astype(F32)
    feed_gain_full = natural([g[bounds[3] : bounds[4]] for g in gain_parts], 0).astype(F32)
    gain_rel = jnp.concatenate(attention_gain_parts)

    with jax.named_scope("attention_forward"):
        positions = jnp.concatenate(
            [place(s) * rows + jnp.arange(rows, dtype=jnp.int32) for s in range(shards)]
        )
        cosine_table, sine_table = tables(positions, ROPE)
        length = seq_len[0]
        sequence = jnp.concatenate(token_parts, axis=0)
        source = jnp.concatenate(cut(sequence, 1), axis=1).astype(F32)
        source_scale = inverse_rms(source)
        normed = (source * source_scale * gain_rel).astype(LOW)
        normed_parts = jnp.split(normed, shards, axis=1)
        query_latent = total([product(a, w) for a, w in zip(normed_parts, query_down_parts)])
        query_scale = inverse_rms(query_latent)
        query_low = (query_latent * query_scale * query_gain_full).astype(LOW)
        (query_low,) = grad_run.step(query_low)
        latent = total([product(a, w) for a, w in zip(normed_parts, latent_down_parts)])
        latent_c = latent[:, :KVL]
        latent_scale = inverse_rms(latent_c)
        latent_low = (latent_c * latent_scale * latent_gain_full).astype(LOW)
        key_rope = rotate(latent[:, KVL:], cosine_table, sine_table).astype(LOW)
        query_low_parts = cut(query_low, 1)
        latent_low_parts = cut(latent_low, 1)
        query_raw = total(
            [product(a, cut(w, 1)[0]) for a, w in zip(query_low_parts, query_up_parts)]
        ).reshape(span, own_heads, NOPE + ROPE)
        query_nope = query_raw[..., :NOPE].astype(LOW)
        query_rope = rotate(
            query_raw[..., NOPE:], cosine_table[:, None, :], sine_table[:, None, :]
        ).astype(LOW)
        keys_values = (
            total([product(a, cut(w, 1)[0]) for a, w in zip(latent_low_parts, latent_up_parts)])
            .astype(LOW)
            .reshape(span, own_heads, NOPE + VDIM)
        )
        query_nope, keys_values = grad_run.step(query_nope, keys_values)
        key_nope = keys_values[..., :NOPE]
        values = keys_values[..., NOPE:]
        score_scale = (NOPE + ROPE) ** (-0.5)
        allowed = (positions[None, :] <= positions[:, None]) & (positions[None, :] < length)
        raw_scores = jnp.einsum("qhd,khd->hqk", query_nope, key_nope, preferred_element_type=F32)
        raw_scores = raw_scores + jnp.einsum(
            "qhr,kr->hqk", query_rope, key_rope, preferred_element_type=F32
        )
        scores = jnp.where(allowed[None], raw_scores * score_scale, NEG)
        row_peak = jnp.max(scores, axis=-1, keepdims=True)
        exp_terms = jnp.exp(scores - row_peak)
        probabilities = exp_terms / jnp.sum(exp_terms, axis=-1, keepdims=True)
        (probabilities,) = grad_run.step(probabilities)
        p_low = probabilities.astype(LOW)
        mixed = jnp.einsum("hqk,khv->qhv", p_low, values, preferred_element_type=F32)
        mixed = mixed.astype(LOW).reshape(span, own_heads * VDIM)
        (mixed,) = grad_run.step(mixed)
        attended = product(mixed, attention_out)
        resid = tokens.astype(F32) + sum_parts(jnp.split(attended, shards, axis=0), F32)
        resid_scale = inverse_rms(resid)
        ffn_low = (resid * resid_scale * feed_gain_full).astype(LOW)

    with jax.named_scope("token_gather"):
        ffn_run = Stages(gather_chips(ffn_low, relay))
        ffn_run.step()
        grad_parts = list(zip(*grad_run.finish()))
        ffn_parts = list(zip(*ffn_run.finish()))

    with jax.named_scope("dispatch"):
        x_rows, g_rows, row_gates, feats, hiddens, delta_pair, delta_down = dispatch(
            shards, rows, room, offsets, first_at, hits, pos, router_full.T, pair_w,
            down_w, ffn_parts, grad_parts,
        )

    with jax.named_scope("routed_experts"):
        grad_rows, low_gate, low_up, weighted, gate_rows = run_experts(
            totals, first_at, x_rows, g_rows, row_gates, jnp.swapaxes(expert_gate, 1, 2),
            jnp.swapaxes(expert_up, 1, 2), expert_down,
        )

    with jax.named_scope("shared_gradients"):
        pair = jnp.stack(
            [delta_pair[:hidden_own], delta_pair[padded : padded + hidden_own]]
        )
        pieces = cut(pair, 2)
        got = [pieces[0]] + [None] * (shards - 1)
        for s in range(1, shards):
            got[shards - s] = to_core(pieces[s], s)
        pair = natural([v[None] for v in got], 0)
        pair_all = lax.all_gather(pair, "expert", axis=0)
        down_all = lax.all_gather(delta_down[:hidden_own], "expert", axis=0, tiled=True)

    with jax.named_scope("to_tokens"):

        def run_combine(columns, rows_all, gates_all, feat, weight):
            return combine(
                columns, ring, rows, shards, room, offsets, counts, slot_chip, rows_all, gates_all,
                pos_cols, feat, weight,
            )

        def over_cores(parts):
            number = len(parts) // shards
            sums = []
            for n in range(number):
                got = [to_core(parts[number * s + n], s) for s in range(1, shards)]
                for k in range(ring):
                    sums.append(add(parts[n][k], *[v[k] for v in got]))
            return sums

        *parts, gates_far = run_combine((3,), grad_rows, gate_rows, feats, pair_w)
        both = over_cores(parts)
        *both, grad_rows = tie(*both, grad_rows)
        *parts, gates_near = run_combine((0, 1, 2), grad_rows, gate_rows, feats, pair_w)
        mine = over_cores(parts)
        mine[-1], weighted = tie(mine[-1], weighted)
        back_run = Stages(scatter_chips(mine + both))
        back_run.step()
        deltas = [grad_rows]
        for e in range(local_count):
            deltas = list(
                run_deltas(
                    e, deltas, totals, x_rows, g_rows, low_gate, low_up, weighted, expert_down
                )
            )
            if e == 0:
                deltas[0], deltas[3], pair_all = back_run.step(deltas[0], deltas[3], pair_all)
            if e == 1:
                deltas[0], deltas[3] = back_run.step(deltas[0], deltas[3])
        parts = list(run_combine((0, 1, 2, 3), deltas[3], None, hiddens, down_w))
        parts = list(back_run.step(*parts))
        grad_from_experts = back_run.finish()
        delta_gate, delta_up, grad_expert_down, unused = deltas
        grad_expert_gate = jnp.swapaxes(delta_gate, 1, 2)
        grad_expert_up = jnp.swapaxes(delta_up, 1, 2)
        gate_grid = jnp.concatenate([gates_near, gates_far])
        gate_grid = lax.dynamic_slice_in_dim(gate_grid, first, local_count, 2)
        gate_grid = gate_grid.reshape(owners, shards, rows, local_count)
        gate_grid = sum_parts([gate_grid[:, s] for s in range(shards)], F32)
        gate_grid = jnp.zeros_like(gate_grid).at[slot_chip].set(gate_grid)
        grad_gates = lax.all_to_all(gate_grid, "expert", split_axis=0, concat_axis=0, tiled=True)
        grad_gates = jnp.swapaxes(grad_gates, 0, 1).reshape(rows, all_experts)
        out_run = Stages(scatter_chips(over_cores(parts)))

    with jax.named_scope("feed_backward"):
        grad_out = cotangent.astype(F32)
        hit_own = jnp.any(routes[:, :, None] == expert_ids, axis=1).astype(F32)
        sig = jax.nn.sigmoid(product(ffn_low, router_full))
        chosen = sig * hit_own
        own_sum = jnp.sum(chosen, axis=1, keepdims=True)
        inner = jnp.sum(grad_gates * chosen, axis=1, keepdims=True)
        grad_chosen = ROUTE_SCALE * (grad_gates / own_sum - inner / (own_sum * own_sum))
        grad_logits = (grad_chosen * hit_own * sig * (1.0 - sig)).astype(LOW)
        grad_ffn = back_product(grad_logits, router_full) + grad_from_experts
        grad_resid_part, feed_terms = norm_back(resid, resid_scale, feed_gain_full, grad_ffn)
        grad_resid = grad_out + grad_resid_part
        grad_attended = grad_resid.astype(LOW)
        feed_gain_delta = jnp.sum(feed_terms, axis=0)

    with jax.named_scope("attention_backward"):
        attended_grads = jnp.concatenate(relative(grad_attended), axis=0)
        logit_grads = jnp.concatenate(relative(grad_logits), axis=0)
        delta_out = outer_sum(mixed, attended_grads).astype(LOW)
        ffn_sequence = cut(jnp.concatenate([part[0] for part in ffn_parts]), 1)[0]
        delta_router = outer_sum(logit_grads, ffn_sequence)
        grad_mixed = (
            back_product(attended_grads, attention_out).astype(LOW).reshape(span, own_heads, VDIM)
        )
        (grad_mixed,) = out_run.step(grad_mixed)
        grad_probs = jnp.einsum("qhv,khv->hqk", grad_mixed, values, preferred_element_type=F32)
        row_delta = jnp.sum(grad_probs * probabilities, axis=-1, keepdims=True)
        grad_raw = (score_scale * probabilities * (grad_probs - row_delta)).astype(LOW)
        (grad_raw,) = out_run.step(grad_raw)
        grad_query_nope = jnp.einsum("hqk,khd->qhd", grad_raw, key_nope, preferred_element_type=F32)
        grad_query_rope = jnp.einsum("hqk,kr->qhr", grad_raw, key_rope, preferred_element_type=F32)
        grad_key_nope = jnp.einsum("hqk,qhd->khd", grad_raw, query_nope, preferred_element_type=F32)
        grad_key_rope = jnp.einsum("hqk,qhr->kr", grad_raw, query_rope, preferred_element_type=F32)
        grad_values = jnp.einsum("hqk,qhv->khv", p_low, grad_mixed, preferred_element_type=F32)
        grad_keys = (
            jnp.concatenate([grad_key_nope, grad_values], axis=-1)
            .reshape(span, own_heads * (NOPE + VDIM))
            .astype(LOW)
        )
        grad_query_turned = rotate(
            grad_query_rope, cosine_table[:, None, :], -sine_table[:, None, :]
        )
        grad_queries = (
            jnp.concatenate([grad_query_nope, grad_query_turned], axis=-1)
            .reshape(span, own_heads * (NOPE + ROPE))
            .astype(LOW)
        )

        def reorder(values, s):
            pieces = jnp.split(values, shards, axis=0)
            return jnp.concatenate([pieces[(t - s) % shards] for t in range(shards)], axis=0)

        def every_core(values):
            return [values] + [reorder(from_core(values, s), s) for s in range(1, shards)]

        grad_queries, grad_keys, grad_key_rope, down_all = out_run.step(
            grad_queries, grad_keys, grad_key_rope, down_all
        )
        grad_shared_down = down_all.astype(F32)
        queries_back = natural(every_core(grad_queries), 1)
        keys_back = natural(every_core(grad_keys), 1)
        rope_back = total(every_core(grad_key_rope))
        grad_latent_normed = natural([back_product(keys_back, w) for w in latent_up_parts], 1)
        grad_latent_part, latent_terms = norm_back(
            latent_c, latent_scale, latent_gain_full, grad_latent_normed
        )
        grad_latent = jnp.concatenate(
            [grad_latent_part, rotate(rope_back, cosine_table, -sine_table)], axis=-1
        ).astype(LOW)
        grad_query_normed = natural([back_product(queries_back, w) for w in query_up_parts], 1)
        grad_query_normed, grad_latent, grad_shared_down = out_run.step(
            grad_query_normed, grad_latent, grad_shared_down
        )
        layer_out = (resid + out_run.finish()).astype(LOW)
        grad_query_part, query_terms = norm_back(
            query_latent, query_scale, query_gain_full, grad_query_normed
        )
        grad_query_latent = grad_query_part.astype(LOW)
        down_delta = outer_sum(
            normed_parts[0], jnp.concatenate([grad_query_latent, grad_latent], axis=1)
        ).astype(LOW)
        up_delta = outer_sum(query_low_parts[0], queries_back).astype(LOW)
        latent_delta = outer_sum(latent_low_parts[0], keys_back).astype(LOW)
        down_delta, up_delta, latent_delta, pair_all = tie(
            down_delta, up_delta, latent_delta, pair_all
        )
        grad_shared_gate, grad_shared_up = transpose_pair(pair_all)
        mine_wide = scatter_rows(delta_out, down_delta)
        mine_up = scatter_rows(up_delta)
        mine_latent = scatter_rows(latent_delta)
        mine_up, grad_shared_gate = tie(mine_up, grad_shared_gate)
        wide_slots = Stages(gather_chips(mine_wide)).finish()
        (grad_query_up,) = gather_rows(mine_up)
        (grad_latent_up,) = gather_rows(mine_latent)
        grad_attention_out, grad_query_down, grad_latent_down = [
            v.reshape(owners * v.shape[1], v.shape[2])
            for v in assemble(
                slot_chip,
                wide_slots,
                (delta_out.shape[1], grad_query_latent.shape[1], grad_latent.shape[1]),
            )
        ]
        grad_normed = jnp.concatenate(
            [
                back_product(grad_query_latent[:rows], a) + back_product(grad_latent[:rows], b)
                for a, b in zip(query_down_parts, latent_down_parts)
            ],
            axis=1,
        )
        grad_source, attention_terms = norm_back(
            source[:rows], source_scale[:rows], gain_rel, grad_normed
        )
        grad_tokens = grad_resid + natural(jnp.split(grad_source, shards, axis=1), 1)

    with jax.named_scope("gain_gradients"):
        attention_delta = jnp.split(jnp.sum(attention_terms, axis=0), shards)
        feed_delta = cut(feed_gain_delta, 0)
        both = sum_parts(
            [jnp.concatenate([a, f]) for a, f in zip(attention_delta, feed_delta)], F32
        )
        query_delta = cut(jnp.sum(query_terms, axis=0), 0)[0]
        latent_delta = cut(jnp.sum(latent_terms, axis=0), 0)[0]
        sums = jnp.concatenate([delta_router.reshape(-1), both, query_delta, latent_delta])
        sums = sum_chips(sums.reshape(-1, part_cols)).reshape(-1)
        sizes = [all_experts * part_cols, part_cols, part_cols]
        sizes += [query_gain.shape[0], latent_gain.shape[0]]
        marks = [0]
        for size in sizes:
            marks.append(marks[-1] + size)
        grad_router, grad_attention_gain, grad_feed_gain, grad_query_gain, grad_latent_gain = [
            sums[a:b] for a, b in zip(marks, marks[1:])
        ]
        grad_router = grad_router.reshape(all_experts, part_cols).T

    return (
        layer_out,
        grad_tokens,
        grad_attention_gain,
        grad_query_down,
        grad_query_gain,
        grad_query_up,
        grad_latent_down,
        grad_latent_gain,
        grad_latent_up,
        grad_attention_out,
        grad_feed_gain,
        grad_router,
        grad_shared_gate,
        grad_shared_up,
        grad_shared_down,
        grad_expert_gate,
        grad_expert_up,
        grad_expert_down,
    )


def solution(mesh):
    tokens_spec = P(("expert", "shard"), None)
    rows_spec = P("shard", None)
    gain_spec = P("shard")
    expert_specs = (
        P("expert", None, "shard"),
        P("expert", None, "shard"),
        P("expert", "shard", None),
    )
    weight_specs = (
        gain_spec,
        rows_spec,
        gain_spec,
        rows_spec,
        rows_spec,
        gain_spec,
        rows_spec,
        rows_spec,
        gain_spec,
        rows_spec,
        rows_spec,
        rows_spec,
        rows_spec,
    ) + expert_specs
    return jax.shard_map(
        local,
        mesh=mesh,
        in_specs=(tokens_spec, tokens_spec, P("expert"), tokens_spec) + weight_specs,
        out_specs=(tokens_spec, tokens_spec) + weight_specs,
        check_vma=False,
    )
```

```python
import jax
import jax.numpy as jnp
import functools

from jax import lax
from jax.experimental import pallas as pl
from jax.experimental.pallas import tpu as pltpu
from jax.sharding import PartitionSpec as P

HEADS = 16
NOPE = 128
ROPE = 64
VDIM = 128
KVL = 512
TOP = 6

EPS = 1e-06
ROUTE_SCALE = 2.446
ROPE_BASE = 50000.0
NEG = -1e30

LOW = jnp.bfloat16
F32 = jnp.float32

LANES = 128
ROW_TILE = 512
HALF_TILE = 256
COL_TILE = 512
ROW_STEP = 16
VMEM_BYTES = 58 << 20


def tables(positions, rope_width):
    half_width = rope_width // 2
    frequencies = ROPE_BASE ** (-2.0 * jnp.arange(half_width, dtype=F32) / rope_width)
    angles = positions.astype(F32)[:, None] * frequencies[None, :]
    return (jnp.cos(angles), jnp.sin(angles))


def rotate(values, cosine_table, sine_table):
    half_width = values.shape[-1] // 2
    first_half = values[..., :half_width]
    second_half = values[..., half_width:]
    return jnp.concatenate(
        [
            first_half * cosine_table - second_half * sine_table,
            second_half * cosine_table + first_half * sine_table,
        ],
        axis=-1,
    )


def product(left_side, right_side):
    return jnp.dot(left_side, right_side, preferred_element_type=F32)


def outer_sum(left_side, right_side):
    return lax.dot_general(
        left_side, right_side, (((0,), (0,)), ((), ())), preferred_element_type=F32
    )


def back_product(left_side, right_side):
    return lax.dot_general(
        left_side, right_side, (((1,), (1,)), ((), ())), preferred_element_type=F32
    )


def tie(*arrays):
    return lax.optimization_barrier(arrays)


class Stages:
    def __init__(self, run):
        self.run, self.got, self.result = run, None, None

    def step(self, *beside):
        try:
            brought = self.run.send(self.got)
        except StopIteration as stop:
            self.run, self.result = None, stop.value
            return beside
        tied = tie(*brought, *beside)
        self.got = list(tied[: len(brought)])
        return tied[len(brought) :]

    def finish(self):
        while self.run is not None:
            self.step()
        return self.result


def total(terms):
    result = terms[0]
    for term in terms[1:]:
        result = result + term
    return result


def inverse_rms(values):
    return lax.rsqrt(jnp.mean(values * values, axis=-1, keepdims=True) + EPS)


def norm_back(values, scale, gain, grad):
    weighted = grad * gain
    inner = jnp.mean(weighted * values, axis=-1, keepdims=True)
    return scale * weighted - values * (scale * scale * scale) * inner, grad * values * scale


def silu_parts(gate_part):
    sig = jax.nn.sigmoid(gate_part)
    return gate_part * sig, sig * (1.0 + gate_part * (1.0 - sig))


def fetch_group(x_parts, g_parts, order, x_buf, g_buf, sems, slot, q, rows):
    cols = pl.ds(0, g_buf.shape[2])
    for s, array in enumerate(g_parts):
        here = g_buf.at[slot, pl.ds(s * rows, rows)]
        pltpu.make_async_copy(array.at[order[q], :, cols], here, sems.at[slot, 0, s]).start()
    for number in range(len(x_parts[0])):

        @pl.when(q == number)
        def _(number=number):
            for s, arrays in enumerate(x_parts):
                here = pl.ds(s * rows, rows)
                pltpu.make_async_copy(
                    arrays[number], x_buf.at[slot, here], sems.at[slot, 1, s]
                ).start()


def wait_group(x_parts, x_buf, g_buf, sems, slot, rows):
    for kind, buffer in enumerate((g_buf, x_buf)):
        for s, arrays in enumerate(x_parts):
            here = buffer.at[slot, pl.ds(s * rows, rows)]
            pltpu.make_async_copy(arrays[0], here, sems.at[slot, kind, s]).wait()


def dispatch_kernel(owners, shards, rows, room, offsets, first, order, hits, pos, router_t, pair_w, down_w, *rest):
    x_parts = [rest[owners * s : owners * (s + 1)] for s in range(shards)]
    g_parts = rest[owners * shards : (owners + 1) * shards]
    rest = rest[(owners + 1) * shards :]
    x_rows, g_rows, row_gates, feats, hiddens, delta_pair, delta_down = rest[:7]
    x_buf, g_buf, in_sem, x_stage, g_stage, gate_stage, out_sem, zeros, zero_gates, acc_pair, acc_down = rest[7:]
    q, count = pl.program_id(0), pl.num_programs(0)
    slot = lax.rem(q, 2)
    local_count = pos.shape[1]
    width = down_w.shape[0]

    @pl.when(q == 0)
    def _():
        fetch_group(x_parts, g_parts, order, x_buf, g_buf, in_sem, 0, 0, rows)
        acc_pair[...] = jnp.zeros_like(acc_pair)
        acc_down[...] = jnp.zeros_like(acc_down)
        zeros[...] = jnp.zeros_like(zeros)
        zero_gates[...] = jnp.zeros_like(zero_gates)

    @pl.when(q + 1 < count)
    def _():
        fetch_group(x_parts, g_parts, order, x_buf, g_buf, in_sem, 1 - slot, q + 1, rows)

    wait_group(x_parts, x_buf, g_buf, in_sem, slot, rows)
    x, g = x_buf[slot], g_buf[slot]

    sig = jax.nn.sigmoid(back_product(router_t[...], x))
    chosen = sig * hits[0]
    gates = ROUTE_SCALE * chosen / jnp.sum(chosen, axis=0, keepdims=True)
    numbers = lax.broadcasted_iota(jnp.int32, gates.shape, 0)
    places = lax.broadcasted_iota(jnp.int32, (room, x.shape[0]), 0)
    picks = []
    for e in range(local_count):
        gate = jnp.sum(jnp.where(numbers == first[0] + e, gates, 0.0), axis=0, keepdims=True)
        pick = places == pos[0, e : e + 1]
        row_gate = jnp.sum(jnp.where(pick, gate, 0.0), axis=1, keepdims=True)
        gate_stage[slot, e] = jnp.broadcast_to(row_gate, (room, LANES))
        picks.append(jnp.where(pick, 1.0, 0.0).astype(LOW))
    picks = jnp.concatenate(picks, axis=0)
    x_stage[slot] = product(picks, x).astype(LOW).reshape(local_count, room, -1)
    g_stage[slot] = product(picks, g).astype(LOW).reshape(local_count, room, -1)

    def writes(which, at):
        start = [pl.multiple_of(offsets[e * count + at], ROW_STEP) for e in range(local_count)]
        return [
            pltpu.make_async_copy(
                stage.at[which, e], array.at[e, pl.ds(start[e], room)], out_sem.at[which, k, e]
            )
            for e in range(local_count)
            for k, (stage, array) in enumerate(
                ((x_stage, x_rows), (g_stage, g_rows), (gate_stage, row_gates))
            )
        ]

    @pl.when(q > 0)
    def _():
        for copy in writes(1 - slot, q - 1):
            copy.wait()

    for copy in writes(slot, q):
        copy.start()

    both = back_product(x, pair_w[...])
    gate_part, up_part = both[:, :width], both[:, width:]
    silu_part, slope = silu_parts(gate_part)
    hidden = (silu_part * up_part).astype(LOW)
    back = back_product(g, down_w[...])
    feat = jnp.concatenate(
        [(back * up_part * slope).astype(LOW), (back * silu_part).astype(LOW)], axis=1
    )
    feats[...] = feat
    hiddens[...] = hidden
    acc_pair[...] += outer_sum(feat, x)
    acc_down[...] += outer_sum(hidden, g)

    @pl.when(q == count - 1)
    def _():
        for copy in writes(slot, q):
            copy.wait()
        tails = []
        for e in range(local_count):
            end = pl.multiple_of(offsets[local_count * count + e], ROW_STEP)
            for k, (stage, array) in enumerate(
                ((zeros, x_rows), (zeros, g_rows), (zero_gates, row_gates))
            ):
                tails.append(
                    pltpu.make_async_copy(
                        stage, array.at[e, pl.ds(end, HALF_TILE)], out_sem.at[slot, k, e]
                    )
                )
        for copy in tails:
            copy.start()
        delta_pair[...] = acc_pair[...].astype(LOW)
        delta_down[...] = acc_down[...].astype(LOW)
        for copy in tails:
            copy.wait()


def expert_kernel(totals, first, x, g, row_gate, w_gate, w_up, w_down, grad_row, grad_gate, grad_up, weighted, gate_grad):
    e, t = pl.program_id(0), pl.program_id(1)
    left = totals[e] - t * ROW_TILE

    def work(count):
        here = pl.ds(0, count)
        width = x.shape[2]
        gate = row_gate[0, here][:, :1]
        gate_part = back_product(x[0, here], w_gate[0])
        up_part = back_product(x[0, here], w_up[0])
        silu_part, slope = silu_parts(gate_part)
        hidden = (silu_part * up_part).astype(LOW)
        back = back_product(g[0, here], w_down[0])
        wide = hidden.astype(F32)
        own = jnp.sum(wide * back, axis=1, keepdims=True)
        lanes = lax.broadcasted_iota(jnp.int32, (count, LANES), 1)
        gate_grad[0, here] = jnp.where(lanes == first[0] + e, own, 0.0)
        back = back * gate
        low_gate = (back * up_part * slope).astype(LOW)
        low_up = (back * silu_part).astype(LOW)
        grad_gate[0, here] = low_gate
        grad_up[0, here] = low_up
        weighted[0, here] = (wide * gate).astype(LOW)
        for at in range(0, width, COL_TILE):
            cols = pl.ds(at, COL_TILE)
            grad_row[0, here, cols] = (
                product(low_gate, w_gate[0, :, cols]) + product(low_up, w_up[0, :, cols])
            ).astype(LOW)

    @pl.when(left > HALF_TILE)
    def _():
        work(ROW_TILE)

    @pl.when((left > 0) & (left <= HALF_TILE))
    def _():
        work(HALF_TILE)


def delta_kernel(e, chained, totals, x, g, grad_gate, grad_up, weighted, w_down, *rest):
    delta_gate, delta_up, delta_down, result = rest[chained:]
    t = pl.program_id(0)
    left = totals[e] - t * ROW_TILE

    @pl.when(t == 0)
    def _():
        delta_gate[...] = jnp.zeros_like(delta_gate)
        delta_up[...] = jnp.zeros_like(delta_up)
        delta_down[...] = jnp.zeros_like(delta_down)

    def work(count):
        here = pl.ds(0, count)
        delta_gate[0] += outer_sum(grad_gate[0, here], x[0, here])
        delta_up[0] += outer_sum(grad_up[0, here], x[0, here])
        delta_down[0] += outer_sum(weighted[0, here], g[0, here])
        for at in range(0, x.shape[2], COL_TILE):
            cols = pl.ds(at, COL_TILE)
            result[0, here, cols] = product(weighted[0, here], w_down[0, :, cols]).astype(LOW)

    @pl.when(left > HALF_TILE)
    def _():
        work(ROW_TILE)

    @pl.when((left > 0) & (left <= HALF_TILE))
    def _():
        work(HALF_TILE)


def combine_kernel(base, columns, ring, room, shards, with_gates, offsets, counts, order, rows_all, gates_all, pos, feat, weight, *rest):
    number = max(len(columns), 1) * shards
    outs, rest = rest[:number], rest[number:]
    if with_gates:
        gate_out, rest = rest[0], rest[1:]
    rows_buf, gates_buf, sems = rest
    step, steps = pl.program_id(0), pl.num_programs(0)
    slot = lax.rem(step, 2)
    local_count = rows_all.shape[0]
    count = counts.shape[0] // local_count

    def reads(which, at):
        copies = []
        for e in range(local_count):
            start = pl.multiple_of(offsets[e * count + base + at], ROW_STEP)
            copies.append(
                pltpu.make_async_copy(
                    rows_all.at[e, pl.ds(start, room)], rows_buf.at[which, e], sems.at[which, 0, e]
                )
            )
            if with_gates:
                copies.append(
                    pltpu.make_async_copy(
                        gates_all.at[e, pl.ds(start, room)],
                        gates_buf.at[which, e],
                        sems.at[which, 1, e],
                    )
                )
        return copies

    @pl.when(step == 0)
    def _():
        for copy in reads(0, 0):
            copy.start()

    @pl.when(step + 1 < steps)
    def _():
        for copy in reads(1 - slot, step + 1):
            copy.start()

    for copy in reads(slot, step):
        copy.wait()

    tokens = pos.shape[1]
    places = lax.broadcasted_iota(jnp.int32, (tokens, room), 1)
    row_ids = lax.broadcasted_iota(jnp.int32, (room, 1), 0)
    picks, rows, gate_sum = [], [], None
    for e in range(local_count):
        valid = row_ids < counts[e * count + base + step]
        pick = jnp.where(places == pos[0][:, e : e + 1], 1.0, 0.0)
        picks.append(pick.astype(LOW))
        rows.append(jnp.where(valid, rows_buf[slot, e], jnp.zeros((), LOW)))
        if with_gates:
            gates = jnp.where(valid, gates_buf[slot, e], 0.0)
            for _ in range(3):
                term = gates.astype(LOW)
                gates = gates - term.astype(F32)
                term = product(picks[-1], term)
                gate_sum = term if gate_sum is None else gate_sum + term
    low = (
        product(feat[...], weight[...])
        + product(jnp.concatenate(picks, axis=1), jnp.concatenate(rows, axis=0))
    ).astype(LOW)
    share = tokens // shards
    for s in range(shards):
        mine = low[s * share : (s + 1) * share]
        if columns:
            for n in range(len(columns)):

                @pl.when(step // ring == n)
                def _(n=n, s=s, mine=mine):
                    outs[len(columns) * s + n][0] = mine
        else:
            outs[s][0] = mine
    if with_gates:
        gate_out[0] = gate_sum


def assemble_kernel(owners, widths, order, *refs):
    outs = refs[owners:]
    for q in range(owners):
        at = 0
        for out, width in zip(outs, widths):
            out[order[q]] = refs[q][:, at : at + width].astype(F32)
            at += width


def transpose_kernel(shards, owners, own, every, gate_out, up_out, table):
    which, k = pl.program_id(0), pl.program_id(1)

    @pl.when(k == 0)
    def _():
        for s in range(shards):
            for q in range(owners):
                table[pl.ds((s * owners + q) * own, own)] = every[q, s, 0].astype(F32)

    piece = table[pl.ds(pl.multiple_of(k * LANES, LANES), LANES)].T

    @pl.when(which == 0)
    def _():
        gate_out[...] = piece

    @pl.when(which == 1)
    def _():
        up_out[...] = piece


def params(*semantics):
    return pltpu.CompilerParams(dimension_semantics=semantics, vmem_limit_bytes=VMEM_BYTES)


def assemble(order, arrays, widths):
    owners = len(arrays)
    rows = arrays[0].shape[0]
    whole = lambda *_: (0, 0)
    return pl.pallas_call(
        functools.partial(assemble_kernel, owners, widths),
        grid_spec=pltpu.PrefetchScalarGridSpec(
            num_scalar_prefetch=1,
            grid=(1,),
            in_specs=[pl.BlockSpec(a.shape, whole) for a in arrays],
            out_specs=[pl.BlockSpec((owners, rows, w), lambda *_: (0, 0, 0)) for w in widths],
        ),
        out_shape=[jax.ShapeDtypeStruct((owners, rows, w), F32) for w in widths],
        compiler_params=params("arbitrary"),
        cost_estimate=pl.CostEstimate(
            flops=0, bytes_accessed=owners * rows * sum(widths) * 6, transcendentals=0
        ),
    )(order, *arrays)


def transpose_pair(every):
    owners, shards, unused, own, cols = every.shape
    hidden = owners * shards * own
    tiles = hidden // LANES
    return pl.pallas_call(
        functools.partial(transpose_kernel, shards, owners, own),
        grid=(2, tiles),
        in_specs=[
            pl.BlockSpec((owners, shards, 1, own, cols), lambda w, k: (0, 0, w, 0, 0)),
        ],
        out_specs=[
            pl.BlockSpec((cols, LANES), lambda w, k: (0, jnp.where(w == 0, k, tiles - 1))),
            pl.BlockSpec((cols, LANES), lambda w, k: (0, jnp.where(w == 0, 0, k))),
        ],
        out_shape=[jax.ShapeDtypeStruct((cols, hidden), F32)] * 2,
        scratch_shapes=[pltpu.VMEM((hidden, cols), F32)],
        compiler_params=params("arbitrary", "arbitrary"),
        cost_estimate=pl.CostEstimate(
            flops=0, bytes_accessed=12 * hidden * cols, transcendentals=0
        ),
    )(every)


def dispatch(shards, rows, room, offsets, first, order, hits, pos, router_t, pair_w, down_w, x_parts, g_parts):
    owners, all_experts, span = hits.shape
    local_count = pos.shape[1]
    width = router_t.shape[1]
    hidden = down_w.shape[0]
    capacity = -(-(owners * room + HALF_TILE) // ROW_TILE) * ROW_TILE
    flat = [a for part in x_parts for a in part] + list(g_parts)
    whole = lambda q, *_: (0, 0)
    anywhere = pl.BlockSpec(memory_space=pl.ANY)
    return pl.pallas_call(
        functools.partial(dispatch_kernel, owners, shards, rows, room),
        grid_spec=pltpu.PrefetchScalarGridSpec(
            num_scalar_prefetch=3,
            grid=(owners,),
            in_specs=[
                pl.BlockSpec((1, all_experts, span), lambda q, *_: (q, 0, 0)),
                pl.BlockSpec((1, local_count, span), lambda q, *_: (q, 0, 0)),
                pl.BlockSpec((all_experts, width), whole),
                pl.BlockSpec((2 * hidden, width), whole),
                pl.BlockSpec((hidden, width), whole),
            ]
            + [anywhere] * len(flat),
            out_specs=[
                anywhere,
                anywhere,
                anywhere,
                pl.BlockSpec((span, 2 * hidden), lambda q, *_: (q, 0)),
                pl.BlockSpec((span, hidden), lambda q, *_: (q, 0)),
                pl.BlockSpec((2 * hidden, width), whole),
                pl.BlockSpec((hidden, width), whole),
            ],
            scratch_shapes=[
                pltpu.VMEM((2, span, width), LOW),
                pltpu.VMEM((2, span, width), LOW),
                pltpu.SemaphoreType.DMA((2, 2, shards)),
                pltpu.VMEM((2, local_count, room, width), LOW),
                pltpu.VMEM((2, local_count, room, width), LOW),
                pltpu.VMEM((2, local_count, room, LANES), F32),
                pltpu.SemaphoreType.DMA((2, 3, local_count)),
                pltpu.VMEM((HALF_TILE, width), LOW),
                pltpu.VMEM((HALF_TILE, LANES), F32),
                pltpu.VMEM((2 * hidden, width), F32),
                pltpu.VMEM((hidden, width), F32),
            ],
        ),
        out_shape=[
            jax.ShapeDtypeStruct((local_count, capacity, width), LOW),
            jax.ShapeDtypeStruct((local_count, capacity, width), LOW),
            jax.ShapeDtypeStruct((local_count, capacity, LANES), F32),
            jax.ShapeDtypeStruct((owners * span, 2 * hidden), LOW),
            jax.ShapeDtypeStruct((owners * span, hidden), LOW),
            jax.ShapeDtypeStruct((2 * hidden, width), LOW),
            jax.ShapeDtypeStruct((hidden, width), LOW),
        ],
        compiler_params=params("arbitrary"),
        cost_estimate=pl.CostEstimate(
            flops=14 * owners * span * width * span,
            bytes_accessed=4 * owners * span * width,
            transcendentals=0,
        ),
    )(offsets, first, order, hits, pos, router_t, pair_w, down_w, *flat)


def tile_map(e, t, totals, *_):
    last = jnp.maximum((totals[e] + ROW_TILE - 1) // ROW_TILE - 1, 0)
    return (e, jnp.minimum(t, last), 0)


def expert_map(e, t, *_):
    return (e, 0, 0)


def run_experts(totals, first, x, g, row_gate, w_gate, w_up, w_down):
    local_count, capacity, width = x.shape
    hidden = w_gate.shape[1]
    tiles = capacity // ROW_TILE
    wide = pl.BlockSpec((1, ROW_TILE, width), tile_map)
    slim = pl.BlockSpec((1, ROW_TILE, hidden), tile_map)
    lane = pl.BlockSpec((1, ROW_TILE, LANES), tile_map)
    return pl.pallas_call(
        expert_kernel,
        grid_spec=pltpu.PrefetchScalarGridSpec(
            num_scalar_prefetch=2,
            grid=(local_count, tiles),
            in_specs=[
                wide,
                wide,
                lane,
                pl.BlockSpec((1, hidden, width), expert_map),
                pl.BlockSpec((1, hidden, width), expert_map),
                pl.BlockSpec((1, hidden, width), expert_map),
            ],
            out_specs=[wide, slim, slim, slim, lane],
        ),
        out_shape=[
            jax.ShapeDtypeStruct(x.shape, LOW),
            jax.ShapeDtypeStruct((local_count, capacity, hidden), LOW),
            jax.ShapeDtypeStruct((local_count, capacity, hidden), LOW),
            jax.ShapeDtypeStruct((local_count, capacity, hidden), LOW),
            jax.ShapeDtypeStruct(row_gate.shape, F32),
        ],
        compiler_params=params("arbitrary", "arbitrary"),
        cost_estimate=pl.CostEstimate(
            flops=5 * local_count * capacity * width * hidden,
            bytes_accessed=6 * local_count * width * (capacity + hidden),
            transcendentals=0,
        ),
    )(totals, first, x, g, row_gate, w_gate, w_up, w_down)


def run_deltas(e, before, totals, x, g, grad_gate, grad_up, weighted, w_down):
    local_count, capacity, width = x.shape
    hidden = grad_gate.shape[2]
    tiles = capacity // ROW_TILE

    def rows_at(t, totals):
        return tile_map(e, t, totals)

    def expert_at(t, totals):
        return (e, 0, 0)

    wide = pl.BlockSpec((1, ROW_TILE, width), rows_at)
    slim = pl.BlockSpec((1, ROW_TILE, hidden), rows_at)
    once = pl.BlockSpec((1, hidden, width), expert_at, pipeline_mode=pl.Buffered(1))
    return pl.pallas_call(
        functools.partial(delta_kernel, e, len(before)),
        grid_spec=pltpu.PrefetchScalarGridSpec(
            num_scalar_prefetch=1,
            grid=(tiles,),
            in_specs=[wide, wide, slim, slim, slim, once]
            + [pl.BlockSpec(memory_space=pl.ANY)] * len(before),
            out_specs=[once] * 3 + [wide],
        ),
        out_shape=[jax.ShapeDtypeStruct((local_count, hidden, width), F32)] * 3
        + [jax.ShapeDtypeStruct(x.shape, LOW)],
        input_output_aliases={7 + i: i + 4 - len(before) for i in range(len(before))},
        compiler_params=params("arbitrary"),
        cost_estimate=pl.CostEstimate(
            flops=4 * capacity * width * hidden,
            bytes_accessed=12 * width * hidden,
            transcendentals=0,
        ),
    )(totals, x, g, grad_gate, grad_up, weighted, w_down, *before)


def combine(columns, ring, rows, shards, room, offsets, counts, order, rows_all, gates_all, pos, feat, weight):
    local_count, capacity, width = rows_all.shape
    owners, span = pos.shape[:2]
    with_gates = gates_all is not None
    base = columns[0] * ring if columns else 0
    steps = len(columns) * ring if columns else owners
    if columns:
        out_shape = [jax.ShapeDtypeStruct((ring, rows, width), LOW)] * (len(columns) * shards)
        out_specs = [
            pl.BlockSpec(
                (1, rows, width),
                lambda q, *_, n=n: (jnp.clip(q - n * ring, 0, ring - 1), 0, 0),
            )
            for s in range(shards)
            for n in range(len(columns))
        ]
    else:
        out_shape = [jax.ShapeDtypeStruct((owners, rows, width), LOW)] * shards
        out_specs = [
            pl.BlockSpec((1, rows, width), lambda q, offsets, counts, order: (order[q], 0, 0))
        ] * shards
    if with_gates:
        out_shape = out_shape + [jax.ShapeDtypeStruct((steps, span, LANES), F32)]
        out_specs = out_specs + [pl.BlockSpec((1, span, LANES), lambda q, *_: (q, 0, 0))]
    return pl.pallas_call(
        functools.partial(combine_kernel, base, columns, ring, room, shards, with_gates),
        grid_spec=pltpu.PrefetchScalarGridSpec(
            num_scalar_prefetch=3,
            grid=(steps,),
            in_specs=[
                pl.BlockSpec(memory_space=pl.ANY),
                pl.BlockSpec(memory_space=pl.ANY),
                pl.BlockSpec((1, span, local_count), lambda q, *_: (base + q, 0, 0)),
                pl.BlockSpec((span, feat.shape[1]), lambda q, *_: (base + q, 0)),
                pl.BlockSpec(weight.shape, lambda q, *_: (0, 0)),
            ],
            out_specs=out_specs,
            scratch_shapes=[
                pltpu.VMEM((2, local_count, room, width), LOW),
                pltpu.VMEM((2, local_count, room, LANES), F32),
                pltpu.SemaphoreType.DMA((2, 2, local_count)),
            ],
        ),
        out_shape=out_shape,
        compiler_params=params("arbitrary"),
        cost_estimate=pl.CostEstimate(
            flops=4 * steps * span * width * span,
            bytes_accessed=4 * steps * span * width,
            transcendentals=0,
        ),
    )(offsets, counts, order, rows_all, gates_all if with_gates else rows_all, pos, feat, weight)


def local(
    tokens,
    cotangent,
    seq_len,
    routes,
    attention_gain,
    query_down,
    query_gain,
    query_up,
    latent_down,
    latent_gain,
    latent_up,
    attention_out,
    feedforward_gain,
    router,
    shared_gate,
    shared_up,
    shared_down,
    expert_gate,
    expert_up,
    expert_down,
):
    rows, width = tokens.shape
    shards = lax.axis_size("shard")
    owners = lax.axis_size("expert")
    core = lax.axis_index("shard")
    chip = lax.axis_index("expert")
    local_count = expert_gate.shape[0]
    all_experts = local_count * owners
    capacity = 2 * rows * TOP // all_experts
    span = rows * shards
    blocks = shards * owners
    own_heads = HEADS // shards
    part_cols = width // shards

    def place(s):
        return (core - s) % shards

    def from_core(values, s):
        return lax.ppermute(values, "shard", [(i, (i + s) % shards) for i in range(shards)])

    def to_core(values, s):
        return lax.ppermute(values, "shard", [(i, (i - s) % shards) for i in range(shards)])

    def relative(values):
        return [values] + [from_core(values, s) for s in range(1, shards)]

    def sum_parts(parts, kind):
        got = [to_core(parts[s].astype(kind), s).astype(F32) for s in range(1, shards)]
        return total([parts[0].astype(F32)] + got)

    ring = owners // 4
    z_at, y_at, x_at = chip // 4, chip // 2 % 2, chip % 2

    def send(values, dz=0, dy=0, dx=0):
        pairs = []
        for i in range(owners):
            z, y, x = i // 4, i // 2 % 2, i % 2
            pairs.append((i, (z + dz) % ring * 4 + (y ^ dy) * 2 + (x ^ dx)))
        return lax.ppermute(values, "expert", pairs)

    slot_chip = jnp.stack(
        [
            (z_at - k) % ring * 4 + (y_at ^ (col // 2)) * 2 + (x_at ^ (col % 2))
            for col in range(4)
            for k in range(ring)
        ]
    ).astype(jnp.int32)

    half_ring = ring // 2

    def middle(values):
        return max(values.shape[-1] // 2 // LANES * LANES, 1)

    steps_z = [1, ring - 1] + [k for k in range(2, ring - 1) if k != half_ring] + [half_ring]

    def gather_chips(values, relay=None):
        half = middle(values)
        slots, relayed = {("own", 0): values}, {}
        waiting = [("own", 0)]

        def stage(sends):
            nonlocal waiting
            fresh = {}
            for key in waiting:
                fresh[key] = relay(slots[key]) if relay else []
            flat, marks = [], []
            for key, arrays in list(sends.items()) + [(("core",) + k, v) for k, v in fresh.items()]:
                marks.append((key, len(arrays)))
                flat += arrays
            flat = list((yield flat))
            waiting = []
            for key, number in marks:
                arrays, flat = flat[:number], flat[number:]
                if key[0] == "core":
                    relayed[key[1:]] = arrays
                else:
                    slots[key] = arrays[0] if number == 1 else jnp.concatenate(arrays, axis=1)
                    waiting.append(key)

        def along(k):
            source = slots["own", half_ring - 1] if k == half_ring else values
            return {("own", k): [send(source, dz=1 if k == half_ring else k)]}

        def sides(k):
            return {
                ("x", k): [send(slots["own", k], dx=1)],
                ("y", k): [send(slots["own", k], dy=1)],
            }

        def corner(k):
            left = send(slots["y", k][:, :half], dx=1)
            right = send(slots["x", k][:, half:], dy=1)
            return {("both", k): [left, right]}

        def far(k):
            return {("both", k): [send(slots["both", 0], dz=k)]}

        for i, k in enumerate(steps_z):
            group = along(k) | sides(steps_z[i - 1] if i else 0)
            yield from stage(group | corner(0) if i == 1 else group)
        yield from stage(sides(half_ring) | far(steps_z[0]))
        last = corner(half_ring)
        for k in steps_z[1:-1]:
            last = last | far(k)
        yield from stage(last)
        for key in waiting:
            relayed[key] = relay(slots[key]) if relay else []
        keys = [(col, k) for col in ("own", "x", "y", "both") for k in range(ring)]
        if relay:
            return [[slots[key]] + relayed[key] for key in keys]
        return [slots[key] for key in keys]

    def add(a, *terms):
        return total([v.astype(F32) for v in (a,) + terms]).astype(LOW)

    def scatter_chips(parts):
        own, side_x, side_y, both = (list(parts[i * ring : (i + 1) * ring]) for i in range(4))
        half = middle(both[0])

        def from_corner(block):
            return [send(block[:, :half], dx=1), send(block[:, half:], dy=1)]

        def spread(k, for_y, for_x):
            side_y[k] = jnp.concatenate([add(side_y[k][:, :half], for_y), side_y[k][:, half:]], axis=1)
            side_x[k] = jnp.concatenate([side_x[k][:, :half], add(side_x[k][:, half:], for_x)], axis=1)

        def fold(k):
            return [send(side_x[k], dx=1), send(side_y[k], dy=1)]

        others = steps_z[:-1]
        got = yield from_corner(both[half_ring]) + [send(both[1], dz=-1)] + fold(1)
        spread(half_ring, *got[:2])
        both[0] = add(both[0], got[2])
        own[1] = add(own[1], *got[3:])
        got = yield (fold(half_ring) + [send(both[k], dz=-k) for k in others[1:]])
        own[half_ring] = add(own[half_ring], *got[:2])
        both[0] = add(both[0], *got[2:])
        got = from_corner(both[0]) + [send(own[half_ring], dz=-1)]
        for k in others[1:]:
            got = got + fold(k)
        got = yield got
        spread(0, *got[:2])
        own[half_ring - 1] = add(own[half_ring - 1], got[2])
        for n, k in enumerate(others[1:]):
            own[k] = add(own[k], *got[3 + 2 * n : 5 + 2 * n])
        got = yield ([send(own[k], dz=-k) for k in others] + fold(0))
        return total([v.astype(F32) for v in [own[0]] + list(got)])

    def sum_chips(values):
        values = values + send(values, dx=1)
        values = values + send(values, dy=1)
        return total([values] + [send(values, dz=k) for k in range(1, ring)])

    def shares(delta):
        height = delta.shape[0] // owners
        return [
            lax.dynamic_slice_in_dim(delta, slot_chip[q] * height, height, 0)
            for q in range(owners)
        ]

    def in_rows(slots):
        return [
            v.reshape(owners * v.shape[1], v.shape[2])
            for v in assemble(slot_chip, slots, (slots[0].shape[1],))
        ]

    def cut(values, axis):
        size = values.shape[axis] // shards
        return [
            lax.dynamic_slice_in_dim(values, place(s) * size, size, axis) for s in range(shards)
        ]

    def natural(parts, axis):
        pieces = []
        for i in range(shards):
            piece = parts[0]
            for s in range(1, shards):
                piece = jnp.where(place(s) == i, parts[s], piece)
            pieces.append(piece)
        return jnp.concatenate(pieces, axis=axis)

    with jax.named_scope("early_gathers"):
        token_parts = relative(tokens)
        gains_own = jnp.concatenate([attention_gain, query_gain, latent_gain, feedforward_gain])
        gain_parts = relative(gains_own)
        query_down_parts = relative(query_down)
        latent_down_parts = relative(latent_down)
        query_up_parts = relative(query_up)
        latent_up_parts = relative(latent_up)
        router_parts = relative(router)
        relay = lambda v: relative(v)[1:]
        expert_ids = jnp.arange(all_experts, dtype=jnp.int32)
        hit_own = jnp.any(routes[:, :, None] == expert_ids, axis=1).astype(F32)
        marks_own = jnp.pad(hit_own.astype(LOW), ((0, 0), (0, -all_experts % LANES)))
        grad_own = lax.all_gather(jnp.concatenate([cotangent, marks_own], axis=1), "expert", axis=0)

    hidden_all = shared_gate.shape[1]
    hidden_own = hidden_all // blocks
    hidden_shard = hidden_all // shards

    def shared_columns(weight):
        pieces = [
            lax.dynamic_slice_in_dim(
                weight, place(s) * hidden_shard + chip * hidden_own, hidden_own, 1
            ).T
            for s in range(shards)
        ]
        got = [pieces[0]] + [None] * (shards - 1)
        for s in range(1, shards):
            got[shards - s] = to_core(pieces[s], s)
        return natural(got, 1)

    with jax.named_scope("shared_weights"):
        padded = -(-hidden_own // LANES) * LANES
        pad = ((0, padded - hidden_own), (0, 0))
        pair_w = jnp.concatenate(
            [jnp.pad(shared_columns(shared_gate), pad), jnp.pad(shared_columns(shared_up), pad)]
        )
        down_w = jnp.pad(
            lax.dynamic_slice_in_dim(shared_down, chip * hidden_own, hidden_own, 0), pad
        )
        router_full = natural(router_parts, 0)

    bounds = [0]
    for size in (part_cols, query_gain.shape[0], latent_gain.shape[0], part_cols):
        bounds.append(bounds[-1] + size)
    attention_gain_parts = [g[bounds[0] : bounds[1]].astype(F32) for g in gain_parts]
    query_gain_full = natural([g[bounds[1] : bounds[2]] for g in gain_parts], 0).astype(F32)
    latent_gain_full = natural([g[bounds[2] : bounds[3]] for g in gain_parts], 0).astype(F32)
    feed_gain_full = natural([g[bounds[3] : bounds[4]] for g in gain_parts], 0).astype(F32)
    gain_rel = jnp.concatenate(attention_gain_parts)

    with jax.named_scope("attention_forward"):
        positions = jnp.concatenate(
            [place(s) * rows + jnp.arange(rows, dtype=jnp.int32) for s in range(shards)]
        )
        cosine_table, sine_table = tables(positions, ROPE)
        length = seq_len[0]
        sequence = jnp.concatenate(token_parts, axis=0)
        source = jnp.concatenate(cut(sequence, 1), axis=1).astype(F32)
        source_scale = inverse_rms(source)
        normed = (source * source_scale * gain_rel).astype(LOW)
        normed_parts = jnp.split(normed, shards, axis=1)
        query_latent = total([product(a, w) for a, w in zip(normed_parts, query_down_parts)])
        query_scale = inverse_rms(query_latent)
        query_low = (query_latent * query_scale * query_gain_full).astype(LOW)
        latent = total([product(a, w) for a, w in zip(normed_parts, latent_down_parts)])
        latent_c = latent[:, :KVL]
        latent_scale = inverse_rms(latent_c)
        latent_low = (latent_c * latent_scale * latent_gain_full).astype(LOW)
        key_rope = rotate(latent[:, KVL:], cosine_table, sine_table).astype(LOW)
        query_low_parts = cut(query_low, 1)
        latent_low_parts = cut(latent_low, 1)
        query_raw = total(
            [product(a, cut(w, 1)[0]) for a, w in zip(query_low_parts, query_up_parts)]
        ).reshape(span, own_heads, NOPE + ROPE)
        query_nope = query_raw[..., :NOPE].astype(LOW)
        query_rope = rotate(
            query_raw[..., NOPE:], cosine_table[:, None, :], sine_table[:, None, :]
        ).astype(LOW)
        keys_values = (
            total([product(a, cut(w, 1)[0]) for a, w in zip(latent_low_parts, latent_up_parts)])
            .astype(LOW)
            .reshape(span, own_heads, NOPE + VDIM)
        )
        key_nope = keys_values[..., :NOPE]
        values = keys_values[..., NOPE:]
        score_scale = (NOPE + ROPE) ** (-0.5)
        allowed = (positions[None, :] <= positions[:, None]) & (positions[None, :] < length)
        raw_scores = jnp.einsum("qhd,khd->hqk", query_nope, key_nope, preferred_element_type=F32)
        raw_scores = raw_scores + jnp.einsum(
            "qhr,kr->hqk", query_rope, key_rope, preferred_element_type=F32
        )
        scores = jnp.where(allowed[None], raw_scores * score_scale, NEG)
        row_peak = jnp.max(scores, axis=-1, keepdims=True)
        exp_terms = jnp.exp(scores - row_peak)
        probabilities = exp_terms / jnp.sum(exp_terms, axis=-1, keepdims=True)
        p_low = probabilities.astype(LOW)
        mixed = jnp.einsum("hqk,khv->qhv", p_low, values, preferred_element_type=F32)
        mixed = mixed.astype(LOW).reshape(span, own_heads * VDIM)
        attended = product(mixed, attention_out)
        resid = tokens.astype(F32) + sum_parts(jnp.split(attended, shards, axis=0), F32)
        resid_scale = inverse_rms(resid)
        ffn_low = (resid * resid_scale * feed_gain_full).astype(LOW)

    with jax.named_scope("token_gather"):
        ffn_slots = Stages(gather_chips(ffn_low, relay)).finish()
        late = 2 * ring + steps_z[1]
        ffn_slots[late][0], grad_own = tie(ffn_slots[late][0], grad_own)
        ffn_parts = list(zip(*ffn_slots))
        grad_parts = relative(grad_own)

    with jax.named_scope("routing"):
        marks = jnp.concatenate(relative(grad_own[:, :, width : width + all_experts]), axis=1)
        hits = jnp.swapaxes(marks[slot_chip], 1, 2) > 0
        first = chip * local_count
        hit = lax.dynamic_slice_in_dim(hits, first, local_count, 1).astype(jnp.int32)
        pos = jnp.where(hit > 0, jnp.cumsum(hit, axis=2) - hit, -1)
        pos_cols = jnp.swapaxes(pos, 1, 2)
        room = shards * capacity
        counts = jnp.sum(hit, axis=2).T
        steps = (counts + ROW_STEP - 1) // ROW_STEP * ROW_STEP
        ends = jnp.cumsum(steps, axis=1)
        totals = ends[:, -1]
        offsets = jnp.concatenate([(ends - steps).reshape(-1), totals])
        counts = counts.reshape(-1)
        hits = hits.astype(F32)
        first_at = first.reshape(1).astype(jnp.int32)

    with jax.named_scope("dispatch"):
        x_rows, g_rows, row_gates, feats, hiddens, delta_pair, delta_down = dispatch(
            shards, rows, room, offsets, first_at, slot_chip, hits, pos, router_full.T, pair_w,
            down_w, ffn_parts, grad_parts,
        )

    with jax.named_scope("routed_experts"):
        grad_rows, low_gate, low_up, weighted, gate_rows = run_experts(
            totals, first_at, x_rows, g_rows, row_gates, jnp.swapaxes(expert_gate, 1, 2),
            jnp.swapaxes(expert_up, 1, 2), expert_down,
        )

    with jax.named_scope("shared_gradients"):
        pair = jnp.stack(
            [delta_pair[:hidden_own], delta_pair[padded : padded + hidden_own]]
        )
        pieces = cut(pair, 2)
        got = [pieces[0]] + [None] * (shards - 1)
        for s in range(1, shards):
            got[shards - s] = to_core(pieces[s], s)
        pair = natural([v[None] for v in got], 0)
        pair_all = lax.all_gather(pair, "expert", axis=0)
        down_all = lax.all_gather(delta_down[:hidden_own], "expert", axis=0, tiled=True)

    with jax.named_scope("to_tokens"):

        def run_combine(columns, rows_all, gates_all, feat, weight):
            return combine(
                columns, ring, rows, shards, room, offsets, counts, slot_chip, rows_all, gates_all,
                pos_cols, feat, weight,
            )

        def over_cores(parts):
            number = len(parts) // shards
            sums = []
            for n in range(number):
                got = [to_core(parts[number * s + n], s) for s in range(1, shards)]
                for k in range(ring):
                    sums.append(add(parts[n][k], *[v[k] for v in got]))
            return sums

        *parts, gates_far = run_combine((3,), grad_rows, gate_rows, feats, pair_w)
        both = over_cores(parts)
        *both, grad_rows = tie(*both, grad_rows)
        *parts, gates_near = run_combine((0, 1, 2), grad_rows, gate_rows, feats, pair_w)
        mine = over_cores(parts)
        mine[-1], weighted = tie(mine[-1], weighted)
        back_run = Stages(scatter_chips(mine + both))
        back_run.step()
        deltas = [grad_rows]
        for e in range(local_count):
            deltas = list(
                run_deltas(
                    e, deltas, totals, x_rows, g_rows, low_gate, low_up, weighted, expert_down
                )
            )
            if e == 0:
                deltas[0], deltas[3], pair_all = back_run.step(deltas[0], deltas[3], pair_all)
            if e == 1:
                deltas[0], deltas[3] = back_run.step(deltas[0], deltas[3])
        parts = list(run_combine((0, 1, 2, 3), deltas[3], None, hiddens, down_w))
        parts = list(back_run.step(*parts))
        grad_from_experts = back_run.finish()
        delta_gate, delta_up, grad_expert_down, unused = deltas
        grad_expert_gate = jnp.swapaxes(delta_gate, 1, 2)
        grad_expert_up = jnp.swapaxes(delta_up, 1, 2)
        gate_grid = jnp.concatenate([gates_near, gates_far])
        gate_grid = lax.dynamic_slice_in_dim(gate_grid, first, local_count, 2)
        gate_grid = gate_grid.reshape(owners, shards, rows, local_count)
        gate_grid = sum_parts([gate_grid[:, s] for s in range(shards)], F32)
        gate_grid = jnp.zeros_like(gate_grid).at[slot_chip].set(gate_grid)
        grad_gates = lax.all_to_all(gate_grid, "expert", split_axis=0, concat_axis=0, tiled=True)
        grad_gates = jnp.swapaxes(grad_gates, 0, 1).reshape(rows, all_experts)
        out_run = Stages(scatter_chips(over_cores(parts)))

    with jax.named_scope("feed_backward"):
        grad_out = cotangent.astype(F32)
        sig = jax.nn.sigmoid(product(ffn_low, router_full))
        chosen = sig * hit_own
        own_sum = jnp.sum(chosen, axis=1, keepdims=True)
        inner = jnp.sum(grad_gates * chosen, axis=1, keepdims=True)
        grad_chosen = ROUTE_SCALE * (grad_gates / own_sum - inner / (own_sum * own_sum))
        grad_logits = (grad_chosen * hit_own * sig * (1.0 - sig)).astype(LOW)
        grad_ffn = back_product(grad_logits, router_full) + grad_from_experts
        grad_resid_part, feed_terms = norm_back(resid, resid_scale, feed_gain_full, grad_ffn)
        grad_resid = grad_out + grad_resid_part
        grad_attended = grad_resid.astype(LOW)
        feed_gain_delta = jnp.sum(feed_terms, axis=0)

    with jax.named_scope("attention_backward"):
        attended_grads = jnp.concatenate(relative(grad_attended), axis=0)
        logit_grads = jnp.concatenate(relative(grad_logits), axis=0)
        delta_out = outer_sum(mixed, attended_grads).astype(LOW)
        ffn_sequence = cut(jnp.concatenate([part[0] for part in ffn_parts]), 1)[0]
        delta_router = outer_sum(logit_grads, ffn_sequence)
        grad_mixed = (
            back_product(attended_grads, attention_out).astype(LOW).reshape(span, own_heads, VDIM)
        )
        grad_mixed, delta_out = out_run.step(grad_mixed, delta_out)
        sum_out = lax.psum(delta_out, "expert")
        grad_probs = jnp.einsum("qhv,khv->hqk", grad_mixed, values, preferred_element_type=F32)
        row_delta = jnp.sum(grad_probs * probabilities, axis=-1, keepdims=True)
        grad_raw = (score_scale * probabilities * (grad_probs - row_delta)).astype(LOW)
        (grad_raw,) = out_run.step(grad_raw)
        grad_query_nope = jnp.einsum("hqk,khd->qhd", grad_raw, key_nope, preferred_element_type=F32)
        grad_query_rope = jnp.einsum("hqk,kr->qhr", grad_raw, key_rope, preferred_element_type=F32)
        grad_key_nope = jnp.einsum("hqk,qhd->khd", grad_raw, query_nope, preferred_element_type=F32)
        grad_key_rope = jnp.einsum("hqk,qhr->kr", grad_raw, query_rope, preferred_element_type=F32)
        grad_values = jnp.einsum("hqk,qhv->khv", p_low, grad_mixed, preferred_element_type=F32)
        grad_keys = (
            jnp.concatenate([grad_key_nope, grad_values], axis=-1)
            .reshape(span, own_heads * (NOPE + VDIM))
            .astype(LOW)
        )
        grad_query_turned = rotate(
            grad_query_rope, cosine_table[:, None, :], -sine_table[:, None, :]
        )
        grad_queries = (
            jnp.concatenate([grad_query_nope, grad_query_turned], axis=-1)
            .reshape(span, own_heads * (NOPE + ROPE))
            .astype(LOW)
        )

        def reorder(values, s):
            pieces = jnp.split(values, shards, axis=0)
            return jnp.concatenate([pieces[(t - s) % shards] for t in range(shards)], axis=0)

        def every_core(values):
            return [values] + [reorder(from_core(values, s), s) for s in range(1, shards)]

        grad_queries, grad_keys, grad_key_rope, down_all = out_run.step(
            grad_queries, grad_keys, grad_key_rope, down_all
        )
        grad_shared_down = down_all.astype(F32)
        queries_back = natural(every_core(grad_queries), 1)
        keys_back = natural(every_core(grad_keys), 1)
        rope_back = total(every_core(grad_key_rope))
        grad_latent_normed = natural([back_product(keys_back, w) for w in latent_up_parts], 1)
        grad_latent_part, latent_terms = norm_back(
            latent_c, latent_scale, latent_gain_full, grad_latent_normed
        )
        grad_latent = jnp.concatenate(
            [grad_latent_part, rotate(rope_back, cosine_table, -sine_table)], axis=-1
        ).astype(LOW)
        grad_query_normed = natural([back_product(queries_back, w) for w in query_up_parts], 1)
        grad_query_normed, grad_latent, grad_shared_down = out_run.step(
            grad_query_normed, grad_latent, grad_shared_down
        )
        layer_out = (resid + out_run.finish()).astype(LOW)
        grad_query_part, query_terms = norm_back(
            query_latent, query_scale, query_gain_full, grad_query_normed
        )
        grad_query_latent = grad_query_part.astype(LOW)
        down_delta = outer_sum(
            normed_parts[0], jnp.concatenate([grad_query_latent, grad_latent], axis=1)
        ).astype(LOW)
        up_delta = outer_sum(query_low_parts[0], queries_back).astype(LOW)
        latent_delta = outer_sum(latent_low_parts[0], keys_back).astype(LOW)
        down_run = Stages(scatter_chips(shares(down_delta)))
        down_run.step()
        up_delta, latent_delta, pair_all = down_run.step(up_delta, latent_delta, pair_all)
        down_sum = lax.all_gather(down_run.finish().astype(LOW), "expert", axis=0, tiled=True)
        mine_up = Stages(scatter_chips(shares(up_delta))).finish().astype(LOW)
        mine_latent = Stages(scatter_chips(shares(latent_delta))).finish().astype(LOW)
        grad_shared_gate, grad_shared_up = transpose_pair(pair_all)
        up_run = Stages(gather_chips(mine_up))
        up_run.step()
        up_run.step()
        (grad_shared_gate,) = up_run.step(grad_shared_gate)
        (sum_out,) = up_run.step(sum_out)
        (grad_query_up,) = in_rows(up_run.finish())
        (grad_latent_up,) = in_rows(Stages(gather_chips(mine_latent)).finish())
        grad_attention_out = sum_out.astype(F32)
        grad_query_down, grad_latent_down = jnp.split(
            down_sum.astype(F32), [grad_query_latent.shape[1]], axis=1
        )
        grad_normed = jnp.concatenate(
            [
                back_product(grad_query_latent[:rows], a) + back_product(grad_latent[:rows], b)
                for a, b in zip(query_down_parts, latent_down_parts)
            ],
            axis=1,
        )
        grad_source, attention_terms = norm_back(
            source[:rows], source_scale[:rows], gain_rel, grad_normed
        )
        grad_tokens = grad_resid + natural(jnp.split(grad_source, shards, axis=1), 1)

    with jax.named_scope("gain_gradients"):
        attention_delta = jnp.split(jnp.sum(attention_terms, axis=0), shards)
        feed_delta = cut(feed_gain_delta, 0)
        both = sum_parts(
            [jnp.concatenate([a, f]) for a, f in zip(attention_delta, feed_delta)], F32
        )
        query_delta = cut(jnp.sum(query_terms, axis=0), 0)[0]
        latent_delta = cut(jnp.sum(latent_terms, axis=0), 0)[0]
        sums = jnp.concatenate([delta_router.reshape(-1), both, query_delta, latent_delta])
        sums = sum_chips(sums.reshape(-1, part_cols)).reshape(-1)
        sizes = [all_experts * part_cols, part_cols, part_cols]
        sizes += [query_gain.shape[0], latent_gain.shape[0]]
        marks = [0]
        for size in sizes:
            marks.append(marks[-1] + size)
        grad_router, grad_attention_gain, grad_feed_gain, grad_query_gain, grad_latent_gain = [
            sums[a:b] for a, b in zip(marks, marks[1:])
        ]
        grad_router = grad_router.reshape(all_experts, part_cols).T

    return (
        layer_out,
        grad_tokens,
        grad_attention_gain,
        grad_query_down,
        grad_query_gain,
        grad_query_up,
        grad_latent_down,
        grad_latent_gain,
        grad_latent_up,
        grad_attention_out,
        grad_feed_gain,
        grad_router,
        grad_shared_gate,
        grad_shared_up,
        grad_shared_down,
        grad_expert_gate,
        grad_expert_up,
        grad_expert_down,
    )


def solution(mesh):
    tokens_spec = P(("expert", "shard"), None)
    rows_spec = P("shard", None)
    gain_spec = P("shard")
    expert_specs = (
        P("expert", None, "shard"),
        P("expert", None, "shard"),
        P("expert", "shard", None),
    )
    weight_specs = (
        gain_spec,
        rows_spec,
        gain_spec,
        rows_spec,
        rows_spec,
        gain_spec,
        rows_spec,
        rows_spec,
        gain_spec,
        rows_spec,
        rows_spec,
        rows_spec,
        rows_spec,
    ) + expert_specs
    return jax.shard_map(
        local,
        mesh=mesh,
        in_specs=(tokens_spec, tokens_spec, P("expert"), tokens_spec) + weight_specs,
        out_specs=(tokens_spec, tokens_spec) + weight_specs,
        check_vma=False,
    )
```

```python
import jax
import jax.numpy as jnp
import functools

from jax import lax
from jax.experimental import pallas as pl
from jax.experimental.pallas import tpu as pltpu
from jax.sharding import PartitionSpec as P

HEADS = 16
NOPE = 128
ROPE = 64
VDIM = 128
KVL = 512
TOP = 6

EPS = 1e-06
ROUTE_SCALE = 2.446
ROPE_BASE = 50000.0
NEG = -1e30

LOW = jnp.bfloat16
F32 = jnp.float32

LANES = 128
ROW_TILE = 512
HALF_TILE = 256
COL_TILE = 512
ROW_STEP = 16
VMEM_BYTES = 58 << 20


def tables(positions, rope_width):
    half_width = rope_width // 2
    frequencies = ROPE_BASE ** (-2.0 * jnp.arange(half_width, dtype=F32) / rope_width)
    angles = positions.astype(F32)[:, None] * frequencies[None, :]
    return (jnp.cos(angles), jnp.sin(angles))


def rotate(values, cosine_table, sine_table):
    half_width = values.shape[-1] // 2
    first_half = values[..., :half_width]
    second_half = values[..., half_width:]
    return jnp.concatenate(
        [
            first_half * cosine_table - second_half * sine_table,
            second_half * cosine_table + first_half * sine_table,
        ],
        axis=-1,
    )


def product(left_side, right_side):
    return jnp.dot(left_side, right_side, preferred_element_type=F32)


def outer_sum(left_side, right_side):
    return lax.dot_general(
        left_side, right_side, (((0,), (0,)), ((), ())), preferred_element_type=F32
    )


def back_product(left_side, right_side):
    return lax.dot_general(
        left_side, right_side, (((1,), (1,)), ((), ())), preferred_element_type=F32
    )


def tie(*arrays):
    return lax.optimization_barrier(arrays)


class Stages:
    def __init__(self, run):
        self.run, self.got, self.result = run, None, None

    def step(self, *beside):
        try:
            brought = self.run.send(self.got)
        except StopIteration as stop:
            self.run, self.result = None, stop.value
            return beside
        tied = tie(*brought, *beside)
        self.got = list(tied[: len(brought)])
        return tied[len(brought) :]

    def finish(self):
        while self.run is not None:
            self.step()
        return self.result


def total(terms):
    result = terms[0]
    for term in terms[1:]:
        result = result + term
    return result


def inverse_rms(values):
    return lax.rsqrt(jnp.mean(values * values, axis=-1, keepdims=True) + EPS)


def norm_back(values, scale, gain, grad):
    weighted = grad * gain
    inner = jnp.mean(weighted * values, axis=-1, keepdims=True)
    return scale * weighted - values * (scale * scale * scale) * inner, grad * values * scale


def silu_parts(gate_part):
    sig = jax.nn.sigmoid(gate_part)
    return gate_part * sig, sig * (1.0 + gate_part * (1.0 - sig))


def fetch_group(x_parts, g_parts, order, x_buf, g_buf, sems, slot, q, rows):
    cols = pl.ds(0, g_buf.shape[2])
    for s, array in enumerate(g_parts):
        here = g_buf.at[slot, pl.ds(s * rows, rows)]
        pltpu.make_async_copy(array.at[order[q], :, cols], here, sems.at[slot, 0, s]).start()
    for number in range(len(x_parts[0])):

        @pl.when(q == number)
        def _(number=number):
            for s, arrays in enumerate(x_parts):
                here = pl.ds(s * rows, rows)
                pltpu.make_async_copy(
                    arrays[number], x_buf.at[slot, here], sems.at[slot, 1, s]
                ).start()


def wait_group(x_parts, x_buf, g_buf, sems, slot, rows):
    for kind, buffer in enumerate((g_buf, x_buf)):
        for s, arrays in enumerate(x_parts):
            here = buffer.at[slot, pl.ds(s * rows, rows)]
            pltpu.make_async_copy(arrays[0], here, sems.at[slot, kind, s]).wait()


def dispatch_kernel(owners, shards, rows, room, offsets, first, order, hits, pos, router_t, pair_w, down_w, *rest):
    x_parts = [rest[owners * s : owners * (s + 1)] for s in range(shards)]
    g_parts = rest[owners * shards : (owners + 1) * shards]
    rest = rest[(owners + 1) * shards :]
    x_rows, g_rows, row_gates, feats, hiddens, delta_pair, delta_down = rest[:7]
    x_buf, g_buf, in_sem, x_stage, g_stage, gate_stage, out_sem, zeros, zero_gates, acc_pair, acc_down = rest[7:]
    q, count = pl.program_id(0), pl.num_programs(0)
    slot = lax.rem(q, 2)
    local_count = pos.shape[1]
    width = down_w.shape[0]

    @pl.when(q == 0)
    def _():
        fetch_group(x_parts, g_parts, order, x_buf, g_buf, in_sem, 0, 0, rows)
        acc_pair[...] = jnp.zeros_like(acc_pair)
        acc_down[...] = jnp.zeros_like(acc_down)
        zeros[...] = jnp.zeros_like(zeros)
        zero_gates[...] = jnp.zeros_like(zero_gates)

    @pl.when(q + 1 < count)
    def _():
        fetch_group(x_parts, g_parts, order, x_buf, g_buf, in_sem, 1 - slot, q + 1, rows)

    wait_group(x_parts, x_buf, g_buf, in_sem, slot, rows)
    x, g = x_buf[slot], g_buf[slot]

    sig = jax.nn.sigmoid(back_product(router_t[...], x))
    chosen = sig * hits[0]
    gates = ROUTE_SCALE * chosen / jnp.sum(chosen, axis=0, keepdims=True)
    numbers = lax.broadcasted_iota(jnp.int32, gates.shape, 0)
    places = lax.broadcasted_iota(jnp.int32, (room, x.shape[0]), 0)
    picks = []
    for e in range(local_count):
        gate = jnp.sum(jnp.where(numbers == first[0] + e, gates, 0.0), axis=0, keepdims=True)
        pick = places == pos[0, e : e + 1]
        row_gate = jnp.sum(jnp.where(pick, gate, 0.0), axis=1, keepdims=True)
        gate_stage[slot, e] = jnp.broadcast_to(row_gate, (room, LANES))
        picks.append(jnp.where(pick, 1.0, 0.0).astype(LOW))
    picks = jnp.concatenate(picks, axis=0)
    x_stage[slot] = product(picks, x).astype(LOW).reshape(local_count, room, -1)
    g_stage[slot] = product(picks, g).astype(LOW).reshape(local_count, room, -1)

    def writes(which, at):
        start = [pl.multiple_of(offsets[e * count + at], ROW_STEP) for e in range(local_count)]
        return [
            pltpu.make_async_copy(
                stage.at[which, e], array.at[e, pl.ds(start[e], room)], out_sem.at[which, k, e]
            )
            for e in range(local_count)
            for k, (stage, array) in enumerate(
                ((x_stage, x_rows), (g_stage, g_rows), (gate_stage, row_gates))
            )
        ]

    @pl.when(q > 0)
    def _():
        for copy in writes(1 - slot, q - 1):
            copy.wait()

    for copy in writes(slot, q):
        copy.start()

    both = back_product(x, pair_w[...])
    gate_part, up_part = both[:, :width], both[:, width:]
    silu_part, slope = silu_parts(gate_part)
    hidden = (silu_part * up_part).astype(LOW)
    back = back_product(g, down_w[...])
    feat = jnp.concatenate(
        [(back * up_part * slope).astype(LOW), (back * silu_part).astype(LOW)], axis=1
    )
    feats[...] = feat
    hiddens[...] = hidden
    acc_pair[...] += outer_sum(feat, x)
    acc_down[...] += outer_sum(hidden, g)

    @pl.when(q == count - 1)
    def _():
        for copy in writes(slot, q):
            copy.wait()
        tails = []
        for e in range(local_count):
            end = pl.multiple_of(offsets[local_count * count + e], ROW_STEP)
            for k, (stage, array) in enumerate(
                ((zeros, x_rows), (zeros, g_rows), (zero_gates, row_gates))
            ):
                tails.append(
                    pltpu.make_async_copy(
                        stage, array.at[e, pl.ds(end, HALF_TILE)], out_sem.at[slot, k, e]
                    )
                )
        for copy in tails:
            copy.start()
        delta_pair[...] = acc_pair[...].astype(LOW)
        delta_down[...] = acc_down[...].astype(LOW)
        for copy in tails:
            copy.wait()


def expert_kernel(totals, first, x, g, row_gate, w_gate, w_up, w_down, grad_row, grad_gate, grad_up, weighted, gate_grad):
    e, t = pl.program_id(0), pl.program_id(1)
    left = totals[e] - t * ROW_TILE

    def work(count):
        here = pl.ds(0, count)
        width = x.shape[2]
        gate = row_gate[0, here][:, :1]
        gate_part = back_product(x[0, here], w_gate[0])
        up_part = back_product(x[0, here], w_up[0])
        silu_part, slope = silu_parts(gate_part)
        hidden = (silu_part * up_part).astype(LOW)
        back = back_product(g[0, here], w_down[0])
        wide = hidden.astype(F32)
        own = jnp.sum(wide * back, axis=1, keepdims=True)
        lanes = lax.broadcasted_iota(jnp.int32, (count, LANES), 1)
        gate_grad[0, here] = jnp.where(lanes == first[0] + e, own, 0.0)
        back = back * gate
        low_gate = (back * up_part * slope).astype(LOW)
        low_up = (back * silu_part).astype(LOW)
        grad_gate[0, here] = low_gate
        grad_up[0, here] = low_up
        weighted[0, here] = (wide * gate).astype(LOW)
        for at in range(0, width, COL_TILE):
            cols = pl.ds(at, COL_TILE)
            grad_row[0, here, cols] = (
                product(low_gate, w_gate[0, :, cols]) + product(low_up, w_up[0, :, cols])
            ).astype(LOW)

    @pl.when(left > HALF_TILE)
    def _():
        work(ROW_TILE)

    @pl.when((left > 0) & (left <= HALF_TILE))
    def _():
        work(HALF_TILE)


def delta_kernel(e, chained, totals, x, g, grad_gate, grad_up, weighted, w_down, *rest):
    delta_gate, delta_up, delta_down, result = rest[chained:]
    t = pl.program_id(0)
    left = totals[e] - t * ROW_TILE

    @pl.when(t == 0)
    def _():
        delta_gate[...] = jnp.zeros_like(delta_gate)
        delta_up[...] = jnp.zeros_like(delta_up)
        delta_down[...] = jnp.zeros_like(delta_down)

    def work(count):
        here = pl.ds(0, count)
        delta_gate[0] += outer_sum(grad_gate[0, here], x[0, here])
        delta_up[0] += outer_sum(grad_up[0, here], x[0, here])
        delta_down[0] += outer_sum(weighted[0, here], g[0, here])
        for at in range(0, x.shape[2], COL_TILE):
            cols = pl.ds(at, COL_TILE)
            result[0, here, cols] = product(weighted[0, here], w_down[0, :, cols]).astype(LOW)

    @pl.when(left > HALF_TILE)
    def _():
        work(ROW_TILE)

    @pl.when((left > 0) & (left <= HALF_TILE))
    def _():
        work(HALF_TILE)


def combine_kernel(base, columns, ring, room, shards, with_gates, offsets, counts, order, rows_all, gates_all, pos, feat, weight, *rest):
    number = max(len(columns), 1) * shards
    outs, rest = rest[:number], rest[number:]
    if with_gates:
        gate_out, rest = rest[0], rest[1:]
    rows_buf, gates_buf, sems = rest
    step, steps = pl.program_id(0), pl.num_programs(0)
    slot = lax.rem(step, 2)
    local_count = rows_all.shape[0]
    count = counts.shape[0] // local_count

    def reads(which, at):
        copies = []
        for e in range(local_count):
            start = pl.multiple_of(offsets[e * count + base + at], ROW_STEP)
            copies.append(
                pltpu.make_async_copy(
                    rows_all.at[e, pl.ds(start, room)], rows_buf.at[which, e], sems.at[which, 0, e]
                )
            )
            if with_gates:
                copies.append(
                    pltpu.make_async_copy(
                        gates_all.at[e, pl.ds(start, room)],
                        gates_buf.at[which, e],
                        sems.at[which, 1, e],
                    )
                )
        return copies

    @pl.when(step == 0)
    def _():
        for copy in reads(0, 0):
            copy.start()

    @pl.when(step + 1 < steps)
    def _():
        for copy in reads(1 - slot, step + 1):
            copy.start()

    for copy in reads(slot, step):
        copy.wait()

    tokens = pos.shape[1]
    places = lax.broadcasted_iota(jnp.int32, (tokens, room), 1)
    row_ids = lax.broadcasted_iota(jnp.int32, (room, 1), 0)
    picks, rows, gate_sum = [], [], None
    for e in range(local_count):
        valid = row_ids < counts[e * count + base + step]
        pick = jnp.where(places == pos[0][:, e : e + 1], 1.0, 0.0)
        picks.append(pick.astype(LOW))
        rows.append(jnp.where(valid, rows_buf[slot, e], jnp.zeros((), LOW)))
        if with_gates:
            gates = jnp.where(valid, gates_buf[slot, e], 0.0)
            for _ in range(3):
                term = gates.astype(LOW)
                gates = gates - term.astype(F32)
                term = product(picks[-1], term)
                gate_sum = term if gate_sum is None else gate_sum + term
    low = (
        product(feat[...], weight[...])
        + product(jnp.concatenate(picks, axis=1), jnp.concatenate(rows, axis=0))
    ).astype(LOW)
    share = tokens // shards
    for s in range(shards):
        mine = low[s * share : (s + 1) * share]
        if columns:
            for n in range(len(columns)):

                @pl.when(step // ring == n)
                def _(n=n, s=s, mine=mine):
                    outs[len(columns) * s + n][0] = mine
        else:
            outs[s][0] = mine
    if with_gates:
        gate_out[0] = gate_sum


def assemble_kernel(owners, widths, order, *refs):
    outs = refs[owners:]
    for q in range(owners):
        at = 0
        for out, width in zip(outs, widths):
            out[order[q]] = refs[q][:, at : at + width].astype(F32)
            at += width


def transpose_kernel(shards, owners, own, every, out, table):
    k = pl.program_id(0)

    @pl.when(k == 0)
    def _():
        for s in range(shards):
            for q in range(owners):
                table[pl.ds((s * owners + q) * own, own)] = every[q, s, 0].astype(F32)

    out[...] = table[pl.ds(pl.multiple_of(k * LANES, LANES), LANES)].T


def params(*semantics):
    return pltpu.CompilerParams(dimension_semantics=semantics, vmem_limit_bytes=VMEM_BYTES)


def assemble(order, arrays, widths):
    owners = len(arrays)
    rows = arrays[0].shape[0]
    whole = lambda *_: (0, 0)
    return pl.pallas_call(
        functools.partial(assemble_kernel, owners, widths),
        grid_spec=pltpu.PrefetchScalarGridSpec(
            num_scalar_prefetch=1,
            grid=(1,),
            in_specs=[pl.BlockSpec(a.shape, whole) for a in arrays],
            out_specs=[pl.BlockSpec((owners, rows, w), lambda *_: (0, 0, 0)) for w in widths],
        ),
        out_shape=[jax.ShapeDtypeStruct((owners, rows, w), F32) for w in widths],
        compiler_params=params("arbitrary"),
        cost_estimate=pl.CostEstimate(
            flops=0, bytes_accessed=owners * rows * sum(widths) * 6, transcendentals=0
        ),
    )(order, *arrays)


def transpose(which, every):
    owners, shards, unused, own, cols = every.shape
    hidden = owners * shards * own
    return pl.pallas_call(
        functools.partial(transpose_kernel, shards, owners, own),
        grid=(hidden // LANES,),
        in_specs=[
            pl.BlockSpec((owners, shards, 1, own, cols), lambda k: (0, 0, which, 0, 0)),
        ],
        out_specs=pl.BlockSpec((cols, LANES), lambda k: (0, k)),
        out_shape=jax.ShapeDtypeStruct((cols, hidden), F32),
        scratch_shapes=[pltpu.VMEM((hidden, cols), F32)],
        compiler_params=params("arbitrary"),
        cost_estimate=pl.CostEstimate(
            flops=0, bytes_accessed=6 * hidden * cols, transcendentals=0
        ),
    )(every)


def dispatch(shards, rows, room, offsets, first, order, hits, pos, router_t, pair_w, down_w, x_parts, g_parts):
    owners, all_experts, span = hits.shape
    local_count = pos.shape[1]
    width = router_t.shape[1]
    hidden = down_w.shape[0]
    capacity = -(-(owners * room + HALF_TILE) // ROW_TILE) * ROW_TILE
    flat = [a for part in x_parts for a in part] + list(g_parts)
    whole = lambda q, *_: (0, 0)
    anywhere = pl.BlockSpec(memory_space=pl.ANY)
    return pl.pallas_call(
        functools.partial(dispatch_kernel, owners, shards, rows, room),
        grid_spec=pltpu.PrefetchScalarGridSpec(
            num_scalar_prefetch=3,
            grid=(owners,),
            in_specs=[
                pl.BlockSpec((1, all_experts, span), lambda q, *_: (q, 0, 0)),
                pl.BlockSpec((1, local_count, span), lambda q, *_: (q, 0, 0)),
                pl.BlockSpec((all_experts, width), whole),
                pl.BlockSpec((2 * hidden, width), whole),
                pl.BlockSpec((hidden, width), whole),
            ]
            + [anywhere] * len(flat),
            out_specs=[
                anywhere,
                anywhere,
                anywhere,
                pl.BlockSpec((span, 2 * hidden), lambda q, *_: (q, 0)),
                pl.BlockSpec((span, hidden), lambda q, *_: (q, 0)),
                pl.BlockSpec((2 * hidden, width), whole),
                pl.BlockSpec((hidden, width), whole),
            ],
            scratch_shapes=[
                pltpu.VMEM((2, span, width), LOW),
                pltpu.VMEM((2, span, width), LOW),
                pltpu.SemaphoreType.DMA((2, 2, shards)),
                pltpu.VMEM((2, local_count, room, width), LOW),
                pltpu.VMEM((2, local_count, room, width), LOW),
                pltpu.VMEM((2, local_count, room, LANES), F32),
                pltpu.SemaphoreType.DMA((2, 3, local_count)),
                pltpu.VMEM((HALF_TILE, width), LOW),
                pltpu.VMEM((HALF_TILE, LANES), F32),
                pltpu.VMEM((2 * hidden, width), F32),
                pltpu.VMEM((hidden, width), F32),
            ],
        ),
        out_shape=[
            jax.ShapeDtypeStruct((local_count, capacity, width), LOW),
            jax.ShapeDtypeStruct((local_count, capacity, width), LOW),
            jax.ShapeDtypeStruct((local_count, capacity, LANES), F32),
            jax.ShapeDtypeStruct((owners * span, 2 * hidden), LOW),
            jax.ShapeDtypeStruct((owners * span, hidden), LOW),
            jax.ShapeDtypeStruct((2 * hidden, width), LOW),
            jax.ShapeDtypeStruct((hidden, width), LOW),
        ],
        compiler_params=params("arbitrary"),
        cost_estimate=pl.CostEstimate(
            flops=14 * owners * span * width * span,
            bytes_accessed=4 * owners * span * width,
            transcendentals=0,
        ),
    )(offsets, first, order, hits, pos, router_t, pair_w, down_w, *flat)


def tile_map(e, t, totals, *_):
    last = jnp.maximum((totals[e] + ROW_TILE - 1) // ROW_TILE - 1, 0)
    return (e, jnp.minimum(t, last), 0)


def expert_map(e, t, *_):
    return (e, 0, 0)


def run_experts(totals, first, x, g, row_gate, w_gate, w_up, w_down):
    local_count, capacity, width = x.shape
    hidden = w_gate.shape[1]
    tiles = capacity // ROW_TILE
    wide = pl.BlockSpec((1, ROW_TILE, width), tile_map)
    slim = pl.BlockSpec((1, ROW_TILE, hidden), tile_map)
    lane = pl.BlockSpec((1, ROW_TILE, LANES), tile_map)
    return pl.pallas_call(
        expert_kernel,
        grid_spec=pltpu.PrefetchScalarGridSpec(
            num_scalar_prefetch=2,
            grid=(local_count, tiles),
            in_specs=[
                wide,
                wide,
                lane,
                pl.BlockSpec((1, hidden, width), expert_map),
                pl.BlockSpec((1, hidden, width), expert_map),
                pl.BlockSpec((1, hidden, width), expert_map),
            ],
            out_specs=[wide, slim, slim, slim, lane],
        ),
        out_shape=[
            jax.ShapeDtypeStruct(x.shape, LOW),
            jax.ShapeDtypeStruct((local_count, capacity, hidden), LOW),
            jax.ShapeDtypeStruct((local_count, capacity, hidden), LOW),
            jax.ShapeDtypeStruct((local_count, capacity, hidden), LOW),
            jax.ShapeDtypeStruct(row_gate.shape, F32),
        ],
        compiler_params=params("arbitrary", "arbitrary"),
        cost_estimate=pl.CostEstimate(
            flops=5 * local_count * capacity * width * hidden,
            bytes_accessed=6 * local_count * width * (capacity + hidden),
            transcendentals=0,
        ),
    )(totals, first, x, g, row_gate, w_gate, w_up, w_down)


def run_deltas(e, before, totals, x, g, grad_gate, grad_up, weighted, w_down):
    local_count, capacity, width = x.shape
    hidden = grad_gate.shape[2]
    tiles = capacity // ROW_TILE

    def rows_at(t, totals):
        return tile_map(e, t, totals)

    def expert_at(t, totals):
        return (e, 0, 0)

    wide = pl.BlockSpec((1, ROW_TILE, width), rows_at)
    slim = pl.BlockSpec((1, ROW_TILE, hidden), rows_at)
    once = pl.BlockSpec((1, hidden, width), expert_at, pipeline_mode=pl.Buffered(1))
    return pl.pallas_call(
        functools.partial(delta_kernel, e, len(before)),
        grid_spec=pltpu.PrefetchScalarGridSpec(
            num_scalar_prefetch=1,
            grid=(tiles,),
            in_specs=[wide, wide, slim, slim, slim, once]
            + [pl.BlockSpec(memory_space=pl.ANY)] * len(before),
            out_specs=[once] * 3 + [wide],
        ),
        out_shape=[jax.ShapeDtypeStruct((local_count, hidden, width), F32)] * 3
        + [jax.ShapeDtypeStruct(x.shape, LOW)],
        input_output_aliases={7 + i: i + 4 - len(before) for i in range(len(before))},
        compiler_params=params("arbitrary"),
        cost_estimate=pl.CostEstimate(
            flops=4 * capacity * width * hidden,
            bytes_accessed=12 * width * hidden,
            transcendentals=0,
        ),
    )(totals, x, g, grad_gate, grad_up, weighted, w_down, *before)


def combine(columns, ring, rows, shards, room, offsets, counts, order, rows_all, gates_all, pos, feat, weight):
    local_count, capacity, width = rows_all.shape
    owners, span = pos.shape[:2]
    with_gates = gates_all is not None
    base = columns[0] * ring if columns else 0
    steps = len(columns) * ring if columns else owners
    if columns:
        out_shape = [jax.ShapeDtypeStruct((ring, rows, width), LOW)] * (len(columns) * shards)
        out_specs = [
            pl.BlockSpec(
                (1, rows, width),
                lambda q, *_, n=n: (jnp.clip(q - n * ring, 0, ring - 1), 0, 0),
            )
            for s in range(shards)
            for n in range(len(columns))
        ]
    else:
        out_shape = [jax.ShapeDtypeStruct((owners, rows, width), LOW)] * shards
        out_specs = [
            pl.BlockSpec((1, rows, width), lambda q, offsets, counts, order: (order[q], 0, 0))
        ] * shards
    if with_gates:
        out_shape = out_shape + [jax.ShapeDtypeStruct((steps, span, LANES), F32)]
        out_specs = out_specs + [pl.BlockSpec((1, span, LANES), lambda q, *_: (q, 0, 0))]
    return pl.pallas_call(
        functools.partial(combine_kernel, base, columns, ring, room, shards, with_gates),
        grid_spec=pltpu.PrefetchScalarGridSpec(
            num_scalar_prefetch=3,
            grid=(steps,),
            in_specs=[
                pl.BlockSpec(memory_space=pl.ANY),
                pl.BlockSpec(memory_space=pl.ANY),
                pl.BlockSpec((1, span, local_count), lambda q, *_: (base + q, 0, 0)),
                pl.BlockSpec((span, feat.shape[1]), lambda q, *_: (base + q, 0)),
                pl.BlockSpec(weight.shape, lambda q, *_: (0, 0)),
            ],
            out_specs=out_specs,
            scratch_shapes=[
                pltpu.VMEM((2, local_count, room, width), LOW),
                pltpu.VMEM((2, local_count, room, LANES), F32),
                pltpu.SemaphoreType.DMA((2, 2, local_count)),
            ],
        ),
        out_shape=out_shape,
        compiler_params=params("arbitrary"),
        cost_estimate=pl.CostEstimate(
            flops=4 * steps * span * width * span,
            bytes_accessed=4 * steps * span * width,
            transcendentals=0,
        ),
    )(offsets, counts, order, rows_all, gates_all if with_gates else rows_all, pos, feat, weight)


def local(
    tokens,
    cotangent,
    seq_len,
    routes,
    attention_gain,
    query_down,
    query_gain,
    query_up,
    latent_down,
    latent_gain,
    latent_up,
    attention_out,
    feedforward_gain,
    router,
    shared_gate,
    shared_up,
    shared_down,
    expert_gate,
    expert_up,
    expert_down,
):
    rows, width = tokens.shape
    shards = lax.axis_size("shard")
    owners = lax.axis_size("expert")
    core = lax.axis_index("shard")
    chip = lax.axis_index("expert")
    local_count = expert_gate.shape[0]
    all_experts = local_count * owners
    capacity = 2 * rows * TOP // all_experts
    span = rows * shards
    blocks = shards * owners
    own_heads = HEADS // shards
    part_cols = width // shards

    def place(s):
        return (core - s) % shards

    def from_core(values, s):
        return lax.ppermute(values, "shard", [(i, (i + s) % shards) for i in range(shards)])

    def to_core(values, s):
        return lax.ppermute(values, "shard", [(i, (i - s) % shards) for i in range(shards)])

    def relative(values):
        return [values] + [from_core(values, s) for s in range(1, shards)]

    def sum_parts(parts, kind):
        got = [to_core(parts[s].astype(kind), s).astype(F32) for s in range(1, shards)]
        return total([parts[0].astype(F32)] + got)

    ring = owners // 4
    z_at, y_at, x_at = chip // 4, chip // 2 % 2, chip % 2

    def send(values, dz=0, dy=0, dx=0):
        pairs = []
        for i in range(owners):
            z, y, x = i // 4, i // 2 % 2, i % 2
            pairs.append((i, (z + dz) % ring * 4 + (y ^ dy) * 2 + (x ^ dx)))
        return lax.ppermute(values, "expert", pairs)

    slot_chip = jnp.stack(
        [
            (z_at - k) % ring * 4 + (y_at ^ (col // 2)) * 2 + (x_at ^ (col % 2))
            for col in range(4)
            for k in range(ring)
        ]
    ).astype(jnp.int32)

    half_ring = ring // 2

    def middle(values):
        return max(values.shape[-1] // 2 // LANES * LANES, 1)

    steps_z = [1, ring - 1] + [k for k in range(2, ring - 1) if k != half_ring] + [half_ring]

    def gather_chips(values, relay=None):
        half = middle(values)
        slots, relayed = {("own", 0): values}, {}
        waiting = [("own", 0)]

        def stage(sends):
            nonlocal waiting
            fresh = {}
            for key in waiting:
                fresh[key] = relay(slots[key]) if relay else []
            flat, marks = [], []
            for key, arrays in list(sends.items()) + [(("core",) + k, v) for k, v in fresh.items()]:
                marks.append((key, len(arrays)))
                flat += arrays
            flat = list((yield flat))
            waiting = []
            for key, number in marks:
                arrays, flat = flat[:number], flat[number:]
                if key[0] == "core":
                    relayed[key[1:]] = arrays
                else:
                    slots[key] = arrays[0] if number == 1 else jnp.concatenate(arrays, axis=1)
                    waiting.append(key)

        def along(k):
            source = slots["own", half_ring - 1] if k == half_ring else values
            return {("own", k): [send(source, dz=1 if k == half_ring else k)]}

        def sides(k):
            return {
                ("x", k): [send(slots["own", k], dx=1)],
                ("y", k): [send(slots["own", k], dy=1)],
            }

        def corner(k):
            left = send(slots["y", k][:, :half], dx=1)
            right = send(slots["x", k][:, half:], dy=1)
            return {("both", k): [left, right]}

        def far(k):
            return {("both", k): [send(slots["both", 0], dz=k)]}

        for i, k in enumerate(steps_z):
            group = along(k) | sides(steps_z[i - 1] if i else 0)
            yield from stage(group | corner(0) if i == 1 else group)
        yield from stage(sides(half_ring) | far(steps_z[0]))
        last = corner(half_ring)
        for k in steps_z[1:-1]:
            last = last | far(k)
        yield from stage(last)
        for key in waiting:
            relayed[key] = relay(slots[key]) if relay else []
        keys = [(col, k) for col in ("own", "x", "y", "both") for k in range(ring)]
        if relay:
            return [[slots[key]] + relayed[key] for key in keys]
        return [slots[key] for key in keys]

    def add(a, *terms):
        return total([v.astype(F32) for v in (a,) + terms]).astype(LOW)

    def scatter_chips(parts):
        own, side_x, side_y, both = (list(parts[i * ring : (i + 1) * ring]) for i in range(4))
        half = middle(both[0])

        def from_corner(block):
            return [send(block[:, :half], dx=1), send(block[:, half:], dy=1)]

        def spread(k, for_y, for_x):
            side_y[k] = jnp.concatenate([add(side_y[k][:, :half], for_y), side_y[k][:, half:]], axis=1)
            side_x[k] = jnp.concatenate([side_x[k][:, :half], add(side_x[k][:, half:], for_x)], axis=1)

        def fold(k):
            return [send(side_x[k], dx=1), send(side_y[k], dy=1)]

        others = steps_z[:-1]
        got = yield from_corner(both[half_ring]) + [send(both[1], dz=-1)] + fold(1)
        spread(half_ring, *got[:2])
        both[0] = add(both[0], got[2])
        own[1] = add(own[1], *got[3:])
        got = yield (fold(half_ring) + [send(both[k], dz=-k) for k in others[1:]])
        own[half_ring] = add(own[half_ring], *got[:2])
        both[0] = add(both[0], *got[2:])
        got = from_corner(both[0]) + [send(own[half_ring], dz=-1)]
        for k in others[1:]:
            got = got + fold(k)
        got = yield got
        spread(0, *got[:2])
        own[half_ring - 1] = add(own[half_ring - 1], got[2])
        for n, k in enumerate(others[1:]):
            own[k] = add(own[k], *got[3 + 2 * n : 5 + 2 * n])
        got = yield ([send(own[k], dz=-k) for k in others] + fold(0))
        return total([v.astype(F32) for v in [own[0]] + list(got)])

    def shares(delta):
        height = delta.shape[0] // owners
        return [
            lax.dynamic_slice_in_dim(delta, slot_chip[q] * height, height, 0)
            for q in range(owners)
        ]

    def in_rows(slots, widths=None):
        widths = (slots[0].shape[1],) if widths is None else widths
        return [
            v.reshape(owners * v.shape[1], v.shape[2]) for v in assemble(slot_chip, slots, widths)
        ]

    def cut(values, axis):
        size = values.shape[axis] // shards
        return [
            lax.dynamic_slice_in_dim(values, place(s) * size, size, axis) for s in range(shards)
        ]

    def natural(parts, axis):
        pieces = []
        for i in range(shards):
            piece = parts[0]
            for s in range(1, shards):
                piece = jnp.where(place(s) == i, parts[s], piece)
            pieces.append(piece)
        return jnp.concatenate(pieces, axis=axis)

    with jax.named_scope("early_gathers"):
        token_parts = relative(tokens)
        gains_own = jnp.concatenate([attention_gain, query_gain, latent_gain, feedforward_gain])
        gain_parts = relative(gains_own)
        query_down_parts = relative(query_down)
        latent_down_parts = relative(latent_down)
        query_up_parts = relative(query_up)
        latent_up_parts = relative(latent_up)
        router_parts = relative(router)
        relay = lambda v: relative(v)[1:]
        expert_ids = jnp.arange(all_experts, dtype=jnp.int32)
        hit_own = jnp.any(routes[:, :, None] == expert_ids, axis=1).astype(F32)
        marks_own = jnp.pad(hit_own.astype(LOW), ((0, 0), (0, -all_experts % LANES)))
        grad_own = lax.all_gather(jnp.concatenate([cotangent, marks_own], axis=1), "expert", axis=0)

    hidden_all = shared_gate.shape[1]
    hidden_own = hidden_all // blocks
    hidden_shard = hidden_all // shards

    def shared_columns(weight):
        pieces = [
            lax.dynamic_slice_in_dim(
                weight, place(s) * hidden_shard + chip * hidden_own, hidden_own, 1
            ).T
            for s in range(shards)
        ]
        got = [pieces[0]] + [None] * (shards - 1)
        for s in range(1, shards):
            got[shards - s] = to_core(pieces[s], s)
        return natural(got, 1)

    with jax.named_scope("shared_weights"):
        padded = -(-hidden_own // LANES) * LANES
        pad = ((0, padded - hidden_own), (0, 0))
        pair_w = jnp.concatenate(
            [jnp.pad(shared_columns(shared_gate), pad), jnp.pad(shared_columns(shared_up), pad)]
        )
        down_w = jnp.pad(
            lax.dynamic_slice_in_dim(shared_down, chip * hidden_own, hidden_own, 0), pad
        )
        router_full = natural(router_parts, 0)

    bounds = [0]
    for size in (part_cols, query_gain.shape[0], latent_gain.shape[0], part_cols):
        bounds.append(bounds[-1] + size)
    attention_gain_parts = [g[bounds[0] : bounds[1]].astype(F32) for g in gain_parts]
    query_gain_full = natural([g[bounds[1] : bounds[2]] for g in gain_parts], 0).astype(F32)
    latent_gain_full = natural([g[bounds[2] : bounds[3]] for g in gain_parts], 0).astype(F32)
    feed_gain_full = natural([g[bounds[3] : bounds[4]] for g in gain_parts], 0).astype(F32)
    gain_rel = jnp.concatenate(attention_gain_parts)

    with jax.named_scope("attention_forward"):
        positions = jnp.concatenate(
            [place(s) * rows + jnp.arange(rows, dtype=jnp.int32) for s in range(shards)]
        )
        cosine_table, sine_table = tables(positions, ROPE)
        length = seq_len[0]
        sequence = jnp.concatenate(token_parts, axis=0)
        source = jnp.concatenate(cut(sequence, 1), axis=1).astype(F32)
        source_scale = inverse_rms(source)
        normed = (source * source_scale * gain_rel).astype(LOW)
        normed_parts = jnp.split(normed, shards, axis=1)
        query_latent = total([product(a, w) for a, w in zip(normed_parts, query_down_parts)])
        query_scale = inverse_rms(query_latent)
        query_low = (query_latent * query_scale * query_gain_full).astype(LOW)
        latent = total([product(a, w) for a, w in zip(normed_parts, latent_down_parts)])
        latent_c = latent[:, :KVL]
        latent_scale = inverse_rms(latent_c)
        latent_low = (latent_c * latent_scale * latent_gain_full).astype(LOW)
        key_rope = rotate(latent[:, KVL:], cosine_table, sine_table).astype(LOW)
        query_low_parts = cut(query_low, 1)
        latent_low_parts = cut(latent_low, 1)
        query_raw = total(
            [product(a, cut(w, 1)[0]) for a, w in zip(query_low_parts, query_up_parts)]
        ).reshape(span, own_heads, NOPE + ROPE)
        query_nope = query_raw[..., :NOPE].astype(LOW)
        query_rope = rotate(
            query_raw[..., NOPE:], cosine_table[:, None, :], sine_table[:, None, :]
        ).astype(LOW)
        keys_values = (
            total([product(a, cut(w, 1)[0]) for a, w in zip(latent_low_parts, latent_up_parts)])
            .astype(LOW)
            .reshape(span, own_heads, NOPE + VDIM)
        )
        key_nope = keys_values[..., :NOPE]
        values = keys_values[..., NOPE:]
        score_scale = (NOPE + ROPE) ** (-0.5)
        allowed = (positions[None, :] <= positions[:, None]) & (positions[None, :] < length)
        raw_scores = jnp.einsum("qhd,khd->hqk", query_nope, key_nope, preferred_element_type=F32)
        raw_scores = raw_scores + jnp.einsum(
            "qhr,kr->hqk", query_rope, key_rope, preferred_element_type=F32
        )
        scores = jnp.where(allowed[None], raw_scores * score_scale, NEG)
        row_peak = jnp.max(scores, axis=-1, keepdims=True)
        exp_terms = jnp.exp(scores - row_peak)
        probabilities = exp_terms / jnp.sum(exp_terms, axis=-1, keepdims=True)
        p_low = probabilities.astype(LOW)
        mixed = jnp.einsum("hqk,khv->qhv", p_low, values, preferred_element_type=F32)
        mixed = mixed.astype(LOW).reshape(span, own_heads * VDIM)
        attended = product(mixed, attention_out)
        resid = tokens.astype(F32) + sum_parts(jnp.split(attended, shards, axis=0), F32)
        resid_scale = inverse_rms(resid)
        ffn_low = (resid * resid_scale * feed_gain_full).astype(LOW)

    with jax.named_scope("token_gather"):
        ffn_slots = Stages(gather_chips(ffn_low, relay)).finish()
        late = 2 * ring + half_ring
        ffn_slots[late][0], grad_own = tie(ffn_slots[late][0], grad_own)
        ffn_parts = list(zip(*ffn_slots))
        grad_parts = relative(grad_own)

    with jax.named_scope("routing"):
        marks = jnp.concatenate(relative(grad_own[:, :, width : width + all_experts]), axis=1)
        hits = jnp.swapaxes(marks[slot_chip], 1, 2) > 0
        first = chip * local_count
        hit = lax.dynamic_slice_in_dim(hits, first, local_count, 1).astype(jnp.int32)
        pos = jnp.where(hit > 0, jnp.cumsum(hit, axis=2) - hit, -1)
        pos_cols = jnp.swapaxes(pos, 1, 2)
        room = shards * capacity
        counts = jnp.sum(hit, axis=2).T
        steps = (counts + ROW_STEP - 1) // ROW_STEP * ROW_STEP
        ends = jnp.cumsum(steps, axis=1)
        totals = ends[:, -1]
        offsets = jnp.concatenate([(ends - steps).reshape(-1), totals])
        counts = counts.reshape(-1)
        hits = hits.astype(F32)
        first_at = first.reshape(1).astype(jnp.int32)

    with jax.named_scope("dispatch"):
        x_rows, g_rows, row_gates, feats, hiddens, delta_pair, delta_down = dispatch(
            shards, rows, room, offsets, first_at, slot_chip, hits, pos, router_full.T, pair_w,
            down_w, ffn_parts, grad_parts,
        )

    with jax.named_scope("routed_experts"):
        grad_rows, low_gate, low_up, weighted, gate_rows = run_experts(
            totals, first_at, x_rows, g_rows, row_gates, jnp.swapaxes(expert_gate, 1, 2),
            jnp.swapaxes(expert_up, 1, 2), expert_down,
        )

    with jax.named_scope("shared_gradients"):
        pair = jnp.stack(
            [delta_pair[:hidden_own], delta_pair[padded : padded + hidden_own]]
        )
        pieces = cut(pair, 2)
        got = [pieces[0]] + [None] * (shards - 1)
        for s in range(1, shards):
            got[shards - s] = to_core(pieces[s], s)
        pair = natural([v[None] for v in got], 0)
        pair_all = lax.all_gather(pair, "expert", axis=0)
        down_all = lax.all_gather(delta_down[:hidden_own], "expert", axis=0, tiled=True)

    with jax.named_scope("to_tokens"):

        def run_combine(columns, rows_all, gates_all, feat, weight):
            return combine(
                columns, ring, rows, shards, room, offsets, counts, slot_chip, rows_all, gates_all,
                pos_cols, feat, weight,
            )

        def over_cores(parts):
            number = len(parts) // shards
            sums = []
            for n in range(number):
                got = [to_core(parts[number * s + n], s) for s in range(1, shards)]
                for k in range(ring):
                    sums.append(add(parts[n][k], *[v[k] for v in got]))
            return sums

        *parts, gates_far = run_combine((3,), grad_rows, gate_rows, feats, pair_w)
        both = over_cores(parts)
        *both, grad_rows = tie(*both, grad_rows)
        *parts, gates_near = run_combine((0, 1, 2), grad_rows, gate_rows, feats, pair_w)
        mine = over_cores(parts)
        mine[-1], weighted = tie(mine[-1], weighted)
        gate_grid = jnp.concatenate([gates_near, gates_far])
        gate_grid = lax.dynamic_slice_in_dim(gate_grid, first, local_count, 2)
        gate_grid = gate_grid.reshape(owners, shards, rows, local_count)
        gate_grid = sum_parts([gate_grid[:, s] for s in range(shards)], F32)
        gate_grid = jnp.zeros_like(gate_grid).at[slot_chip].set(gate_grid)
        grad_gates = lax.all_to_all(gate_grid, "expert", split_axis=0, concat_axis=0, tiled=True)
        grad_gates = jnp.swapaxes(grad_gates, 0, 1).reshape(rows, all_experts)
        back_run = Stages(scatter_chips(mine + both))
        back_run.step()
        deltas = [grad_rows]
        for e in range(local_count):
            deltas = list(
                run_deltas(
                    e, deltas, totals, x_rows, g_rows, low_gate, low_up, weighted, expert_down
                )
            )
            if e == 0:
                deltas[0], deltas[3], pair_all, grad_gates = back_run.step(
                    deltas[0], deltas[3], pair_all, grad_gates
                )
            if e == 1:
                deltas[0], deltas[3] = back_run.step(deltas[0], deltas[3])
        parts = list(run_combine((0, 1, 2, 3), deltas[3], None, hiddens, down_w))
        parts = list(back_run.step(*parts))
        grad_from_experts = back_run.finish()
        delta_gate, delta_up, grad_expert_down, unused = deltas
        grad_expert_gate = jnp.swapaxes(delta_gate, 1, 2)
        grad_expert_up = jnp.swapaxes(delta_up, 1, 2)
        out_run = Stages(scatter_chips(over_cores(parts)))

    with jax.named_scope("feed_backward"):
        grad_out = cotangent.astype(F32)
        sig = jax.nn.sigmoid(product(ffn_low, router_full))
        chosen = sig * hit_own
        own_sum = jnp.sum(chosen, axis=1, keepdims=True)
        inner = jnp.sum(grad_gates * chosen, axis=1, keepdims=True)
        grad_chosen = ROUTE_SCALE * (grad_gates / own_sum - inner / (own_sum * own_sum))
        grad_logits = (grad_chosen * hit_own * sig * (1.0 - sig)).astype(LOW)
        grad_ffn = back_product(grad_logits, router_full) + grad_from_experts
        grad_resid_part, feed_terms = norm_back(resid, resid_scale, feed_gain_full, grad_ffn)
        grad_resid = grad_out + grad_resid_part
        grad_attended = grad_resid.astype(LOW)
        feed_gain_delta = jnp.sum(feed_terms, axis=0)

    with jax.named_scope("attention_backward"):
        attended_grads = jnp.concatenate(relative(grad_attended), axis=0)
        logit_grads = jnp.concatenate(relative(grad_logits), axis=0)
        delta_out = outer_sum(mixed, attended_grads).astype(LOW)
        ffn_sequence = cut(jnp.concatenate([part[0] for part in ffn_parts]), 1)[0]
        delta_router = outer_sum(logit_grads, ffn_sequence)
        grad_mixed = (
            back_product(attended_grads, attention_out).astype(LOW).reshape(span, own_heads, VDIM)
        )
        grad_mixed, delta_out, pair_all = out_run.step(grad_mixed, delta_out, pair_all)
        sum_out = lax.psum(delta_out, "expert")
        grad_probs = jnp.einsum("qhv,khv->hqk", grad_mixed, values, preferred_element_type=F32)
        row_delta = jnp.sum(grad_probs * probabilities, axis=-1, keepdims=True)
        grad_raw = (score_scale * probabilities * (grad_probs - row_delta)).astype(LOW)
        grad_shared_gate = transpose(0, pair_all)
        grad_raw, grad_shared_gate, pair_all = out_run.step(grad_raw, grad_shared_gate, pair_all)
        grad_shared_up = transpose(1, pair_all)
        grad_query_nope = jnp.einsum("hqk,khd->qhd", grad_raw, key_nope, preferred_element_type=F32)
        grad_query_rope = jnp.einsum("hqk,kr->qhr", grad_raw, key_rope, preferred_element_type=F32)
        grad_key_nope = jnp.einsum("hqk,qhd->khd", grad_raw, query_nope, preferred_element_type=F32)
        grad_key_rope = jnp.einsum("hqk,qhr->kr", grad_raw, query_rope, preferred_element_type=F32)
        grad_values = jnp.einsum("hqk,qhv->khv", p_low, grad_mixed, preferred_element_type=F32)
        grad_keys = (
            jnp.concatenate([grad_key_nope, grad_values], axis=-1)
            .reshape(span, own_heads * (NOPE + VDIM))
            .astype(LOW)
        )
        grad_query_turned = rotate(
            grad_query_rope, cosine_table[:, None, :], -sine_table[:, None, :]
        )
        grad_queries = (
            jnp.concatenate([grad_query_nope, grad_query_turned], axis=-1)
            .reshape(span, own_heads * (NOPE + ROPE))
            .astype(LOW)
        )

        def reorder(values, s):
            pieces = jnp.split(values, shards, axis=0)
            return jnp.concatenate([pieces[(t - s) % shards] for t in range(shards)], axis=0)

        def every_core(values):
            return [values] + [reorder(from_core(values, s), s) for s in range(1, shards)]

        grad_queries, grad_keys, grad_key_rope, down_all, grad_shared_up = out_run.step(
            grad_queries, grad_keys, grad_key_rope, down_all, grad_shared_up
        )
        grad_shared_down = down_all.astype(F32)
        queries_back = natural(every_core(grad_queries), 1)
        keys_back = natural(every_core(grad_keys), 1)
        rope_back = total(every_core(grad_key_rope))
        grad_latent_normed = natural([back_product(keys_back, w) for w in latent_up_parts], 1)
        grad_latent_part, latent_terms = norm_back(
            latent_c, latent_scale, latent_gain_full, grad_latent_normed
        )
        grad_latent = jnp.concatenate(
            [grad_latent_part, rotate(rope_back, cosine_table, -sine_table)], axis=-1
        ).astype(LOW)
        grad_query_normed = natural([back_product(queries_back, w) for w in query_up_parts], 1)
        grad_query_normed, grad_latent, grad_shared_down = out_run.step(
            grad_query_normed, grad_latent, grad_shared_down
        )
        layer_out = (resid + out_run.finish()).astype(LOW)
        grad_query_part, query_terms = norm_back(
            query_latent, query_scale, query_gain_full, grad_query_normed
        )
        grad_query_latent = grad_query_part.astype(LOW)
        down_delta = outer_sum(
            normed_parts[0], jnp.concatenate([grad_query_latent, grad_latent], axis=1)
        ).astype(LOW)
        up_delta = outer_sum(query_low_parts[0], queries_back).astype(LOW)
        latent_delta_rows = outer_sum(latent_low_parts[0], keys_back).astype(LOW)
        down_run = Stages(scatter_chips(shares(down_delta)))
        down_run.step()
        up_delta, latent_delta_rows = down_run.step(up_delta, latent_delta_rows)
        down_sum = lax.all_gather(down_run.finish().astype(LOW), "expert", axis=0, tiled=True)
        mine_up = Stages(scatter_chips(shares(up_delta))).finish().astype(LOW)
        grad_normed = jnp.concatenate(
            [
                back_product(grad_query_latent[:rows], a) + back_product(grad_latent[:rows], b)
                for a, b in zip(query_down_parts, latent_down_parts)
            ],
            axis=1,
        )
        grad_source, attention_terms = norm_back(
            source[:rows], source_scale[:rows], gain_rel, grad_normed
        )
        grad_tokens = grad_resid + natural(jnp.split(grad_source, shards, axis=1), 1)

    with jax.named_scope("gain_gradients"):
        attention_delta = jnp.split(jnp.sum(attention_terms, axis=0), shards)
        feed_delta = cut(feed_gain_delta, 0)
        both = sum_parts(
            [jnp.concatenate([a, f]) for a, f in zip(attention_delta, feed_delta)], F32
        )
        query_delta = cut(jnp.sum(query_terms, axis=0), 0)[0]
        latent_delta = cut(jnp.sum(latent_terms, axis=0), 0)[0]
        sums = jnp.concatenate([delta_router.reshape(-1), both, query_delta, latent_delta])
        sizes = [all_experts * part_cols, part_cols, part_cols]
        sizes += [query_gain.shape[0], latent_gain.shape[0]]
        height = latent_delta_rows.shape[0]
        sums = sums.reshape(height, -1).astype(LOW)
        mine_latent = Stages(
            scatter_chips(shares(jnp.concatenate([latent_delta_rows, sums], axis=1)))
        ).finish()
        up_run = Stages(gather_chips(mine_up))
        up_run.step()
        up_run.step()
        up_run.step()
        (sum_out,) = up_run.step(sum_out)
        (grad_query_up,) = in_rows(up_run.finish())
        grad_latent_up, sums = in_rows(
            Stages(gather_chips(mine_latent.astype(LOW))).finish(),
            (latent_delta_rows.shape[1], sums.shape[1]),
        )
        sums = sums.reshape(-1)
        grad_attention_out = sum_out.astype(F32)
        grad_query_down, grad_latent_down = jnp.split(
            down_sum.astype(F32), [grad_query_latent.shape[1]], axis=1
        )
        marks = [0]
        for size in sizes:
            marks.append(marks[-1] + size)
        grad_router, grad_attention_gain, grad_feed_gain, grad_query_gain, grad_latent_gain = [
            sums[a:b] for a, b in zip(marks, marks[1:])
        ]
        grad_router = grad_router.reshape(all_experts, part_cols).T

    return (
        layer_out,
        grad_tokens,
        grad_attention_gain,
        grad_query_down,
        grad_query_gain,
        grad_query_up,
        grad_latent_down,
        grad_latent_gain,
        grad_latent_up,
        grad_attention_out,
        grad_feed_gain,
        grad_router,
        grad_shared_gate,
        grad_shared_up,
        grad_shared_down,
        grad_expert_gate,
        grad_expert_up,
        grad_expert_down,
    )


def solution(mesh):
    tokens_spec = P(("expert", "shard"), None)
    rows_spec = P("shard", None)
    gain_spec = P("shard")
    expert_specs = (
        P("expert", None, "shard"),
        P("expert", None, "shard"),
        P("expert", "shard", None),
    )
    weight_specs = (
        gain_spec,
        rows_spec,
        gain_spec,
        rows_spec,
        rows_spec,
        gain_spec,
        rows_spec,
        rows_spec,
        gain_spec,
        rows_spec,
        rows_spec,
        rows_spec,
        rows_spec,
    ) + expert_specs
    return jax.shard_map(
        local,
        mesh=mesh,
        in_specs=(tokens_spec, tokens_spec, P("expert"), tokens_spec) + weight_specs,
        out_specs=(tokens_spec, tokens_spec) + weight_specs,
        check_vma=False,
    )
```

```python
import jax
import jax.numpy as jnp
import functools

from jax import lax
from jax.experimental import pallas as pl
from jax.experimental.pallas import tpu as pltpu
from jax.sharding import PartitionSpec as P

HEADS = 16
NOPE = 128
ROPE = 64
VDIM = 128
KVL = 512
TOP = 6

EPS = 1e-06
ROUTE_SCALE = 2.446
ROPE_BASE = 50000.0
NEG = -1e30

LOW = jnp.bfloat16
F32 = jnp.float32

LANES = 128
ROW_TILE = 512
HALF_TILE = 256
COL_TILE = 512
ROW_STEP = 16
VMEM_BYTES = 58 << 20


def tables(positions, rope_width):
    half_width = rope_width // 2
    frequencies = ROPE_BASE ** (-2.0 * jnp.arange(half_width, dtype=F32) / rope_width)
    angles = positions.astype(F32)[:, None] * frequencies[None, :]
    return (jnp.cos(angles), jnp.sin(angles))


def rotate(values, cosine_table, sine_table):
    half_width = values.shape[-1] // 2
    first_half = values[..., :half_width]
    second_half = values[..., half_width:]
    return jnp.concatenate(
        [
            first_half * cosine_table - second_half * sine_table,
            second_half * cosine_table + first_half * sine_table,
        ],
        axis=-1,
    )


def product(left_side, right_side):
    return jnp.dot(left_side, right_side, preferred_element_type=F32)


def outer_sum(left_side, right_side):
    return lax.dot_general(
        left_side, right_side, (((0,), (0,)), ((), ())), preferred_element_type=F32
    )


def back_product(left_side, right_side):
    return lax.dot_general(
        left_side, right_side, (((1,), (1,)), ((), ())), preferred_element_type=F32
    )


def tie(*arrays):
    return lax.optimization_barrier(arrays)


class Stages:
    def __init__(self, run):
        self.run, self.got, self.result = run, None, None

    def step(self, *beside):
        try:
            brought = self.run.send(self.got)
        except StopIteration as stop:
            self.run, self.result = None, stop.value
            return beside
        tied = tie(*brought, *beside)
        self.got = list(tied[: len(brought)])
        return tied[len(brought) :]

    def finish(self):
        while self.run is not None:
            self.step()
        return self.result


def total(terms):
    result = terms[0]
    for term in terms[1:]:
        result = result + term
    return result


def inverse_rms(values):
    return lax.rsqrt(jnp.mean(values * values, axis=-1, keepdims=True) + EPS)


def norm_back(values, scale, gain, grad):
    weighted = grad * gain
    inner = jnp.mean(weighted * values, axis=-1, keepdims=True)
    return scale * weighted - values * (scale * scale * scale) * inner, grad * values * scale


def silu_parts(gate_part):
    sig = jax.nn.sigmoid(gate_part)
    return gate_part * sig, sig * (1.0 + gate_part * (1.0 - sig))


def fetch_group(x_parts, g_parts, order, x_buf, g_buf, sems, slot, q, rows):
    cols = pl.ds(0, g_buf.shape[2])
    for s, array in enumerate(g_parts):
        here = g_buf.at[slot, pl.ds(s * rows, rows)]
        pltpu.make_async_copy(array.at[order[q], :, cols], here, sems.at[slot, 0, s]).start()
    for number in range(len(x_parts[0])):

        @pl.when(q == number)
        def _(number=number):
            for s, arrays in enumerate(x_parts):
                here = pl.ds(s * rows, rows)
                pltpu.make_async_copy(
                    arrays[number], x_buf.at[slot, here], sems.at[slot, 1, s]
                ).start()


def wait_group(x_parts, x_buf, g_buf, sems, slot, rows):
    for kind, buffer in enumerate((g_buf, x_buf)):
        for s, arrays in enumerate(x_parts):
            here = buffer.at[slot, pl.ds(s * rows, rows)]
            pltpu.make_async_copy(arrays[0], here, sems.at[slot, kind, s]).wait()


def dispatch_kernel(owners, shards, rows, room, offsets, first, order, hits, pos, router_t, pair_w, down_w, *rest):
    x_parts = [rest[owners * s : owners * (s + 1)] for s in range(shards)]
    g_parts = rest[owners * shards : (owners + 1) * shards]
    rest = rest[(owners + 1) * shards :]
    x_rows, g_rows, row_gates, feats, hiddens, delta_pair, delta_down = rest[:7]
    x_buf, g_buf, in_sem, x_stage, g_stage, gate_stage, out_sem, zeros, zero_gates, acc_pair, acc_down = rest[7:]
    q, count = pl.program_id(0), pl.num_programs(0)
    slot = lax.rem(q, 2)
    local_count = pos.shape[1]
    width = down_w.shape[0]

    @pl.when(q == 0)
    def _():
        fetch_group(x_parts, g_parts, order, x_buf, g_buf, in_sem, 0, 0, rows)
        acc_pair[...] = jnp.zeros_like(acc_pair)
        acc_down[...] = jnp.zeros_like(acc_down)
        zeros[...] = jnp.zeros_like(zeros)
        zero_gates[...] = jnp.zeros_like(zero_gates)

    @pl.when(q + 1 < count)
    def _():
        fetch_group(x_parts, g_parts, order, x_buf, g_buf, in_sem, 1 - slot, q + 1, rows)

    wait_group(x_parts, x_buf, g_buf, in_sem, slot, rows)
    x, g = x_buf[slot], g_buf[slot]

    sig = jax.nn.sigmoid(back_product(router_t[...], x))
    chosen = sig * hits[0]
    gates = ROUTE_SCALE * chosen / jnp.sum(chosen, axis=0, keepdims=True)
    numbers = lax.broadcasted_iota(jnp.int32, gates.shape, 0)
    places = lax.broadcasted_iota(jnp.int32, (room, x.shape[0]), 0)
    picks = []
    for e in range(local_count):
        gate = jnp.sum(jnp.where(numbers == first[0] + e, gates, 0.0), axis=0, keepdims=True)
        pick = places == pos[0, e : e + 1]
        row_gate = jnp.sum(jnp.where(pick, gate, 0.0), axis=1, keepdims=True)
        gate_stage[slot, e] = jnp.broadcast_to(row_gate, (room, LANES))
        picks.append(jnp.where(pick, 1.0, 0.0).astype(LOW))
    picks = jnp.concatenate(picks, axis=0)
    x_stage[slot] = product(picks, x).astype(LOW).reshape(local_count, room, -1)
    g_stage[slot] = product(picks, g).astype(LOW).reshape(local_count, room, -1)

    def writes(which, at):
        start = [pl.multiple_of(offsets[e * count + at], ROW_STEP) for e in range(local_count)]
        return [
            pltpu.make_async_copy(
                stage.at[which, e], array.at[e, pl.ds(start[e], room)], out_sem.at[which, k, e]
            )
            for e in range(local_count)
            for k, (stage, array) in enumerate(
                ((x_stage, x_rows), (g_stage, g_rows), (gate_stage, row_gates))
            )
        ]

    @pl.when(q > 0)
    def _():
        for copy in writes(1 - slot, q - 1):
            copy.wait()

    for copy in writes(slot, q):
        copy.start()

    both = back_product(x, pair_w[...])
    gate_part, up_part = both[:, :width], both[:, width:]
    silu_part, slope = silu_parts(gate_part)
    hidden = (silu_part * up_part).astype(LOW)
    back = back_product(g, down_w[...])
    feat = jnp.concatenate(
        [(back * up_part * slope).astype(LOW), (back * silu_part).astype(LOW)], axis=1
    )
    feats[...] = feat
    hiddens[...] = hidden
    acc_pair[...] += outer_sum(feat, x)
    acc_down[...] += outer_sum(hidden, g)

    @pl.when(q == count - 1)
    def _():
        for copy in writes(slot, q):
            copy.wait()
        tails = []
        for e in range(local_count):
            end = pl.multiple_of(offsets[local_count * count + e], ROW_STEP)
            for k, (stage, array) in enumerate(
                ((zeros, x_rows), (zeros, g_rows), (zero_gates, row_gates))
            ):
                tails.append(
                    pltpu.make_async_copy(
                        stage, array.at[e, pl.ds(end, HALF_TILE)], out_sem.at[slot, k, e]
                    )
                )
        for copy in tails:
            copy.start()
        delta_pair[...] = acc_pair[...].astype(LOW)
        delta_down[...] = acc_down[...].astype(LOW)
        for copy in tails:
            copy.wait()


def expert_kernel(totals, first, x, g, row_gate, w_gate, w_up, w_down, grad_row, grad_gate, grad_up, weighted, gate_grad):
    e, t = pl.program_id(0), pl.program_id(1)
    left = totals[e] - t * ROW_TILE

    def work(count):
        here = pl.ds(0, count)
        width = x.shape[2]
        gate = row_gate[0, here][:, :1]
        gate_part = back_product(x[0, here], w_gate[0])
        up_part = back_product(x[0, here], w_up[0])
        silu_part, slope = silu_parts(gate_part)
        hidden = (silu_part * up_part).astype(LOW)
        back = back_product(g[0, here], w_down[0])
        wide = hidden.astype(F32)
        own = jnp.sum(wide * back, axis=1, keepdims=True)
        lanes = lax.broadcasted_iota(jnp.int32, (count, LANES), 1)
        gate_grad[0, here] = jnp.where(lanes == first[0] + e, own, 0.0)
        back = back * gate
        low_gate = (back * up_part * slope).astype(LOW)
        low_up = (back * silu_part).astype(LOW)
        grad_gate[0, here] = low_gate
        grad_up[0, here] = low_up
        weighted[0, here] = (wide * gate).astype(LOW)
        for at in range(0, width, COL_TILE):
            cols = pl.ds(at, COL_TILE)
            grad_row[0, here, cols] = (
                product(low_gate, w_gate[0, :, cols]) + product(low_up, w_up[0, :, cols])
            ).astype(LOW)

    @pl.when(left > HALF_TILE)
    def _():
        work(ROW_TILE)

    @pl.when((left > 0) & (left <= HALF_TILE))
    def _():
        work(HALF_TILE)


def delta_kernel(e, chained, totals, x, g, grad_gate, grad_up, weighted, w_down, *rest):
    delta_gate, delta_up, delta_down, result = rest[chained:]
    t = pl.program_id(0)
    left = totals[e] - t * ROW_TILE

    @pl.when(t == 0)
    def _():
        delta_gate[...] = jnp.zeros_like(delta_gate)
        delta_up[...] = jnp.zeros_like(delta_up)
        delta_down[...] = jnp.zeros_like(delta_down)

    def work(count):
        here = pl.ds(0, count)
        delta_gate[0] += outer_sum(grad_gate[0, here], x[0, here])
        delta_up[0] += outer_sum(grad_up[0, here], x[0, here])
        delta_down[0] += outer_sum(weighted[0, here], g[0, here])
        for at in range(0, x.shape[2], COL_TILE):
            cols = pl.ds(at, COL_TILE)
            result[0, here, cols] = product(weighted[0, here], w_down[0, :, cols]).astype(LOW)

    @pl.when(left > HALF_TILE)
    def _():
        work(ROW_TILE)

    @pl.when((left > 0) & (left <= HALF_TILE))
    def _():
        work(HALF_TILE)


def combine_kernel(base, columns, ring, room, shards, with_gates, offsets, counts, order, rows_all, gates_all, pos, feat, weight, *rest):
    number = max(len(columns), 1) * shards
    outs, rest = rest[:number], rest[number:]
    if with_gates:
        gate_out, rest = rest[0], rest[1:]
    rows_buf, gates_buf, sems = rest
    step, steps = pl.program_id(0), pl.num_programs(0)
    slot = lax.rem(step, 2)
    local_count = rows_all.shape[0]
    count = counts.shape[0] // local_count

    def reads(which, at):
        copies = []
        for e in range(local_count):
            start = pl.multiple_of(offsets[e * count + base + at], ROW_STEP)
            copies.append(
                pltpu.make_async_copy(
                    rows_all.at[e, pl.ds(start, room)], rows_buf.at[which, e], sems.at[which, 0, e]
                )
            )
            if with_gates:
                copies.append(
                    pltpu.make_async_copy(
                        gates_all.at[e, pl.ds(start, room)],
                        gates_buf.at[which, e],
                        sems.at[which, 1, e],
                    )
                )
        return copies

    @pl.when(step == 0)
    def _():
        for copy in reads(0, 0):
            copy.start()

    @pl.when(step + 1 < steps)
    def _():
        for copy in reads(1 - slot, step + 1):
            copy.start()

    for copy in reads(slot, step):
        copy.wait()

    tokens = pos.shape[1]
    places = lax.broadcasted_iota(jnp.int32, (tokens, room), 1)
    row_ids = lax.broadcasted_iota(jnp.int32, (room, 1), 0)
    picks, rows, gate_sum = [], [], None
    for e in range(local_count):
        valid = row_ids < counts[e * count + base + step]
        pick = jnp.where(places == pos[0][:, e : e + 1], 1.0, 0.0)
        picks.append(pick.astype(LOW))
        rows.append(jnp.where(valid, rows_buf[slot, e], jnp.zeros((), LOW)))
        if with_gates:
            gates = jnp.where(valid, gates_buf[slot, e], 0.0)
            for _ in range(3):
                term = gates.astype(LOW)
                gates = gates - term.astype(F32)
                term = product(picks[-1], term)
                gate_sum = term if gate_sum is None else gate_sum + term
    low = (
        product(feat[...], weight[...])
        + product(jnp.concatenate(picks, axis=1), jnp.concatenate(rows, axis=0))
    ).astype(LOW)
    share = tokens // shards
    for s in range(shards):
        mine = low[s * share : (s + 1) * share]
        if columns:
            for n in range(len(columns)):

                @pl.when(step // ring == n)
                def _(n=n, s=s, mine=mine):
                    outs[len(columns) * s + n][0] = mine
        else:
            outs[s][0] = mine
    if with_gates:
        gate_out[0] = gate_sum


def assemble_kernel(owners, widths, order, *refs):
    outs = refs[owners:]
    for q in range(owners):
        at = 0
        for out, width in zip(outs, widths):
            out[order[q]] = refs[q][:, at : at + width].astype(F32)
            at += width


def transpose_kernel(shards, owners, own, every, out, table):
    k = pl.program_id(0)

    @pl.when(k == 0)
    def _():
        for s in range(shards):
            for q in range(owners):
                table[pl.ds((s * owners + q) * own, own)] = every[q, s, 0].astype(F32)

    out[...] = table[pl.ds(pl.multiple_of(k * LANES, LANES), LANES)].T


def params(*semantics):
    return pltpu.CompilerParams(dimension_semantics=semantics, vmem_limit_bytes=VMEM_BYTES)


def assemble(order, arrays, widths):
    owners = len(arrays)
    rows = arrays[0].shape[0]
    whole = lambda *_: (0, 0)
    return pl.pallas_call(
        functools.partial(assemble_kernel, owners, widths),
        grid_spec=pltpu.PrefetchScalarGridSpec(
            num_scalar_prefetch=1,
            grid=(1,),
            in_specs=[pl.BlockSpec(a.shape, whole) for a in arrays],
            out_specs=[pl.BlockSpec((owners, rows, w), lambda *_: (0, 0, 0)) for w in widths],
        ),
        out_shape=[jax.ShapeDtypeStruct((owners, rows, w), F32) for w in widths],
        compiler_params=params("arbitrary"),
        cost_estimate=pl.CostEstimate(
            flops=0, bytes_accessed=owners * rows * sum(widths) * 6, transcendentals=0
        ),
    )(order, *arrays)


def transpose(which, every):
    owners, shards, unused, own, cols = every.shape
    hidden = owners * shards * own
    return pl.pallas_call(
        functools.partial(transpose_kernel, shards, owners, own),
        grid=(hidden // LANES,),
        in_specs=[
            pl.BlockSpec((owners, shards, 1, own, cols), lambda k: (0, 0, which, 0, 0)),
        ],
        out_specs=pl.BlockSpec((cols, LANES), lambda k: (0, k)),
        out_shape=jax.ShapeDtypeStruct((cols, hidden), F32),
        scratch_shapes=[pltpu.VMEM((hidden, cols), F32)],
        compiler_params=params("arbitrary"),
        cost_estimate=pl.CostEstimate(
            flops=0, bytes_accessed=6 * hidden * cols, transcendentals=0
        ),
    )(every)


def dispatch(shards, rows, room, offsets, first, order, hits, pos, router_t, pair_w, down_w, x_parts, g_parts):
    owners, all_experts, span = hits.shape
    local_count = pos.shape[1]
    width = router_t.shape[1]
    hidden = down_w.shape[0]
    capacity = -(-(owners * room + HALF_TILE) // ROW_TILE) * ROW_TILE
    flat = [a for part in x_parts for a in part] + list(g_parts)
    whole = lambda q, *_: (0, 0)
    anywhere = pl.BlockSpec(memory_space=pl.ANY)
    return pl.pallas_call(
        functools.partial(dispatch_kernel, owners, shards, rows, room),
        grid_spec=pltpu.PrefetchScalarGridSpec(
            num_scalar_prefetch=3,
            grid=(owners,),
            in_specs=[
                pl.BlockSpec((1, all_experts, span), lambda q, *_: (q, 0, 0)),
                pl.BlockSpec((1, local_count, span), lambda q, *_: (q, 0, 0)),
                pl.BlockSpec((all_experts, width), whole),
                pl.BlockSpec((2 * hidden, width), whole),
                pl.BlockSpec((hidden, width), whole),
            ]
            + [anywhere] * len(flat),
            out_specs=[
                anywhere,
                anywhere,
                anywhere,
                pl.BlockSpec((span, 2 * hidden), lambda q, *_: (q, 0)),
                pl.BlockSpec((span, hidden), lambda q, *_: (q, 0)),
                pl.BlockSpec((2 * hidden, width), whole),
                pl.BlockSpec((hidden, width), whole),
            ],
            scratch_shapes=[
                pltpu.VMEM((2, span, width), LOW),
                pltpu.VMEM((2, span, width), LOW),
                pltpu.SemaphoreType.DMA((2, 2, shards)),
                pltpu.VMEM((2, local_count, room, width), LOW),
                pltpu.VMEM((2, local_count, room, width), LOW),
                pltpu.VMEM((2, local_count, room, LANES), F32),
                pltpu.SemaphoreType.DMA((2, 3, local_count)),
                pltpu.VMEM((HALF_TILE, width), LOW),
                pltpu.VMEM((HALF_TILE, LANES), F32),
                pltpu.VMEM((2 * hidden, width), F32),
                pltpu.VMEM((hidden, width), F32),
            ],
        ),
        out_shape=[
            jax.ShapeDtypeStruct((local_count, capacity, width), LOW),
            jax.ShapeDtypeStruct((local_count, capacity, width), LOW),
            jax.ShapeDtypeStruct((local_count, capacity, LANES), F32),
            jax.ShapeDtypeStruct((owners * span, 2 * hidden), LOW),
            jax.ShapeDtypeStruct((owners * span, hidden), LOW),
            jax.ShapeDtypeStruct((2 * hidden, width), LOW),
            jax.ShapeDtypeStruct((hidden, width), LOW),
        ],
        compiler_params=params("arbitrary"),
        cost_estimate=pl.CostEstimate(
            flops=14 * owners * span * width * span,
            bytes_accessed=4 * owners * span * width,
            transcendentals=0,
        ),
    )(offsets, first, order, hits, pos, router_t, pair_w, down_w, *flat)


def tile_map(e, t, totals, *_):
    last = jnp.maximum((totals[e] + ROW_TILE - 1) // ROW_TILE - 1, 0)
    return (e, jnp.minimum(t, last), 0)


def expert_map(e, t, *_):
    return (e, 0, 0)


def run_experts(totals, first, x, g, row_gate, w_gate, w_up, w_down):
    local_count, capacity, width = x.shape
    hidden = w_gate.shape[1]
    tiles = capacity // ROW_TILE
    wide = pl.BlockSpec((1, ROW_TILE, width), tile_map)
    slim = pl.BlockSpec((1, ROW_TILE, hidden), tile_map)
    lane = pl.BlockSpec((1, ROW_TILE, LANES), tile_map)
    return pl.pallas_call(
        expert_kernel,
        grid_spec=pltpu.PrefetchScalarGridSpec(
            num_scalar_prefetch=2,
            grid=(local_count, tiles),
            in_specs=[
                wide,
                wide,
                lane,
                pl.BlockSpec((1, hidden, width), expert_map),
                pl.BlockSpec((1, hidden, width), expert_map),
                pl.BlockSpec((1, hidden, width), expert_map),
            ],
            out_specs=[wide, slim, slim, slim, lane],
        ),
        out_shape=[
            jax.ShapeDtypeStruct(x.shape, LOW),
            jax.ShapeDtypeStruct((local_count, capacity, hidden), LOW),
            jax.ShapeDtypeStruct((local_count, capacity, hidden), LOW),
            jax.ShapeDtypeStruct((local_count, capacity, hidden), LOW),
            jax.ShapeDtypeStruct(row_gate.shape, F32),
        ],
        compiler_params=params("arbitrary", "arbitrary"),
        cost_estimate=pl.CostEstimate(
            flops=5 * local_count * capacity * width * hidden,
            bytes_accessed=6 * local_count * width * (capacity + hidden),
            transcendentals=0,
        ),
    )(totals, first, x, g, row_gate, w_gate, w_up, w_down)


def run_deltas(e, before, totals, x, g, grad_gate, grad_up, weighted, w_down):
    local_count, capacity, width = x.shape
    hidden = grad_gate.shape[2]
    tiles = capacity // ROW_TILE

    def rows_at(t, totals):
        return tile_map(e, t, totals)

    def expert_at(t, totals):
        return (e, 0, 0)

    wide = pl.BlockSpec((1, ROW_TILE, width), rows_at)
    slim = pl.BlockSpec((1, ROW_TILE, hidden), rows_at)
    once = pl.BlockSpec((1, hidden, width), expert_at, pipeline_mode=pl.Buffered(1))
    return pl.pallas_call(
        functools.partial(delta_kernel, e, len(before)),
        grid_spec=pltpu.PrefetchScalarGridSpec(
            num_scalar_prefetch=1,
            grid=(tiles,),
            in_specs=[wide, wide, slim, slim, slim, once]
            + [pl.BlockSpec(memory_space=pl.ANY)] * len(before),
            out_specs=[once] * 3 + [wide],
        ),
        out_shape=[jax.ShapeDtypeStruct((local_count, hidden, width), F32)] * 3
        + [jax.ShapeDtypeStruct(x.shape, LOW)],
        input_output_aliases={7 + i: i + 4 - len(before) for i in range(len(before))},
        compiler_params=params("arbitrary"),
        cost_estimate=pl.CostEstimate(
            flops=4 * capacity * width * hidden,
            bytes_accessed=12 * width * hidden,
            transcendentals=0,
        ),
    )(totals, x, g, grad_gate, grad_up, weighted, w_down, *before)


def combine(columns, ring, rows, shards, room, offsets, counts, order, rows_all, gates_all, pos, feat, weight):
    local_count, capacity, width = rows_all.shape
    owners, span = pos.shape[:2]
    with_gates = gates_all is not None
    base = columns[0] * ring if columns else 0
    steps = len(columns) * ring if columns else owners
    if columns:
        out_shape = [jax.ShapeDtypeStruct((ring, rows, width), LOW)] * (len(columns) * shards)
        out_specs = [
            pl.BlockSpec(
                (1, rows, width),
                lambda q, *_, n=n: (jnp.clip(q - n * ring, 0, ring - 1), 0, 0),
            )
            for s in range(shards)
            for n in range(len(columns))
        ]
    else:
        out_shape = [jax.ShapeDtypeStruct((owners, rows, width), LOW)] * shards
        out_specs = [
            pl.BlockSpec((1, rows, width), lambda q, offsets, counts, order: (order[q], 0, 0))
        ] * shards
    if with_gates:
        out_shape = out_shape + [jax.ShapeDtypeStruct((steps, span, LANES), F32)]
        out_specs = out_specs + [pl.BlockSpec((1, span, LANES), lambda q, *_: (q, 0, 0))]
    return pl.pallas_call(
        functools.partial(combine_kernel, base, columns, ring, room, shards, with_gates),
        grid_spec=pltpu.PrefetchScalarGridSpec(
            num_scalar_prefetch=3,
            grid=(steps,),
            in_specs=[
                pl.BlockSpec(memory_space=pl.ANY),
                pl.BlockSpec(memory_space=pl.ANY),
                pl.BlockSpec((1, span, local_count), lambda q, *_: (base + q, 0, 0)),
                pl.BlockSpec((span, feat.shape[1]), lambda q, *_: (base + q, 0)),
                pl.BlockSpec(weight.shape, lambda q, *_: (0, 0)),
            ],
            out_specs=out_specs,
            scratch_shapes=[
                pltpu.VMEM((2, local_count, room, width), LOW),
                pltpu.VMEM((2, local_count, room, LANES), F32),
                pltpu.SemaphoreType.DMA((2, 2, local_count)),
            ],
        ),
        out_shape=out_shape,
        compiler_params=params("arbitrary"),
        cost_estimate=pl.CostEstimate(
            flops=4 * steps * span * width * span,
            bytes_accessed=4 * steps * span * width,
            transcendentals=0,
        ),
    )(offsets, counts, order, rows_all, gates_all if with_gates else rows_all, pos, feat, weight)


def local(
    tokens,
    cotangent,
    seq_len,
    routes,
    attention_gain,
    query_down,
    query_gain,
    query_up,
    latent_down,
    latent_gain,
    latent_up,
    attention_out,
    feedforward_gain,
    router,
    shared_gate,
    shared_up,
    shared_down,
    expert_gate,
    expert_up,
    expert_down,
):
    rows, width = tokens.shape
    shards = lax.axis_size("shard")
    owners = lax.axis_size("expert")
    core = lax.axis_index("shard")
    chip = lax.axis_index("expert")
    local_count = expert_gate.shape[0]
    all_experts = local_count * owners
    capacity = 2 * rows * TOP // all_experts
    span = rows * shards
    blocks = shards * owners
    own_heads = HEADS // shards
    part_cols = width // shards

    def place(s):
        return (core - s) % shards

    def from_core(values, s):
        return lax.ppermute(values, "shard", [(i, (i + s) % shards) for i in range(shards)])

    def to_core(values, s):
        return lax.ppermute(values, "shard", [(i, (i - s) % shards) for i in range(shards)])

    def relative(values):
        return [values] + [from_core(values, s) for s in range(1, shards)]

    def sum_parts(parts, kind):
        got = [to_core(parts[s].astype(kind), s).astype(F32) for s in range(1, shards)]
        return total([parts[0].astype(F32)] + got)

    ring = owners // 4
    z_at, y_at, x_at = chip // 4, chip // 2 % 2, chip % 2

    def send(values, dz=0, dy=0, dx=0):
        pairs = []
        for i in range(owners):
            z, y, x = i // 4, i // 2 % 2, i % 2
            pairs.append((i, (z + dz) % ring * 4 + (y ^ dy) * 2 + (x ^ dx)))
        return lax.ppermute(values, "expert", pairs)

    slot_chip = jnp.stack(
        [
            (z_at - k) % ring * 4 + (y_at ^ (col // 2)) * 2 + (x_at ^ (col % 2))
            for col in range(4)
            for k in range(ring)
        ]
    ).astype(jnp.int32)

    half_ring = ring // 2

    def middle(values):
        return max(values.shape[-1] // 2 // LANES * LANES, 1)

    steps_z = [1, ring - 1] + [k for k in range(2, ring - 1) if k != half_ring] + [half_ring]

    def gather_chips(values, relay=None):
        half = middle(values)
        slots, relayed = {("own", 0): values}, {}
        waiting = [("own", 0)]

        def stage(sends):
            nonlocal waiting
            fresh = {}
            for key in waiting:
                fresh[key] = relay(slots[key]) if relay else []
            flat, marks = [], []
            for key, arrays in list(sends.items()) + [(("core",) + k, v) for k, v in fresh.items()]:
                marks.append((key, len(arrays)))
                flat += arrays
            flat = list((yield flat))
            waiting = []
            for key, number in marks:
                arrays, flat = flat[:number], flat[number:]
                if key[0] == "core":
                    relayed[key[1:]] = arrays
                else:
                    slots[key] = arrays[0] if number == 1 else jnp.concatenate(arrays, axis=1)
                    waiting.append(key)

        def along(k):
            source = slots["own", half_ring - 1] if k == half_ring else values
            return {("own", k): [send(source, dz=1 if k == half_ring else k)]}

        def sides(k):
            return {
                ("x", k): [send(slots["own", k], dx=1)],
                ("y", k): [send(slots["own", k], dy=1)],
            }

        def corner(k):
            left = send(slots["y", k][:, :half], dx=1)
            right = send(slots["x", k][:, half:], dy=1)
            return {("both", k): [left, right]}

        def far(k):
            return {("both", k): [send(slots["both", 0], dz=k)]}

        for i, k in enumerate(steps_z):
            group = along(k) | sides(steps_z[i - 1] if i else 0)
            yield from stage(group | corner(0) if i == 1 else group)
        yield from stage(sides(half_ring) | far(steps_z[0]))
        last = corner(half_ring)
        for k in steps_z[1:-1]:
            last = last | far(k)
        yield from stage(last)
        for key in waiting:
            relayed[key] = relay(slots[key]) if relay else []
        keys = [(col, k) for col in ("own", "x", "y", "both") for k in range(ring)]
        if relay:
            return [[slots[key]] + relayed[key] for key in keys]
        return [slots[key] for key in keys]

    def add(a, *terms):
        return total([v.astype(F32) for v in (a,) + terms]).astype(LOW)

    def scatter_chips(parts):
        own, side_x, side_y, both = (list(parts[i * ring : (i + 1) * ring]) for i in range(4))
        half = middle(both[0])

        def from_corner(block):
            return [send(block[:, :half], dx=1), send(block[:, half:], dy=1)]

        def spread(k, for_y, for_x):
            side_y[k] = jnp.concatenate([add(side_y[k][:, :half], for_y), side_y[k][:, half:]], axis=1)
            side_x[k] = jnp.concatenate([side_x[k][:, :half], add(side_x[k][:, half:], for_x)], axis=1)

        def fold(k):
            return [send(side_x[k], dx=1), send(side_y[k], dy=1)]

        others = steps_z[:-1]
        got = yield from_corner(both[half_ring]) + [send(both[1], dz=-1)] + fold(1)
        spread(half_ring, *got[:2])
        both[0] = add(both[0], got[2])
        own[1] = add(own[1], *got[3:])
        got = yield (fold(half_ring) + [send(both[k], dz=-k) for k in others[1:]])
        own[half_ring] = add(own[half_ring], *got[:2])
        both[0] = add(both[0], *got[2:])
        got = from_corner(both[0]) + [send(own[half_ring], dz=-1)]
        for k in others[1:]:
            got = got + fold(k)
        got = yield got
        spread(0, *got[:2])
        own[half_ring - 1] = add(own[half_ring - 1], got[2])
        for n, k in enumerate(others[1:]):
            own[k] = add(own[k], *got[3 + 2 * n : 5 + 2 * n])
        got = yield ([send(own[k], dz=-k) for k in others] + fold(0))
        return total([v.astype(F32) for v in [own[0]] + list(got)])

    def shares(delta):
        height = delta.shape[0] // owners
        return [
            lax.dynamic_slice_in_dim(delta, slot_chip[q] * height, height, 0)
            for q in range(owners)
        ]

    def in_rows(slots, widths=None):
        widths = (slots[0].shape[1],) if widths is None else widths
        return [
            v.reshape(owners * v.shape[1], v.shape[2]) for v in assemble(slot_chip, slots, widths)
        ]

    def cut(values, axis):
        size = values.shape[axis] // shards
        return [
            lax.dynamic_slice_in_dim(values, place(s) * size, size, axis) for s in range(shards)
        ]

    def natural(parts, axis):
        pieces = []
        for i in range(shards):
            piece = parts[0]
            for s in range(1, shards):
                piece = jnp.where(place(s) == i, parts[s], piece)
            pieces.append(piece)
        return jnp.concatenate(pieces, axis=axis)

    with jax.named_scope("early_gathers"):
        token_parts = relative(tokens)
        gains_own = jnp.concatenate([attention_gain, query_gain, latent_gain, feedforward_gain])
        gain_parts = relative(gains_own)
        query_down_parts = relative(query_down)
        latent_down_parts = relative(latent_down)
        query_up_parts = relative(query_up)
        latent_up_parts = relative(latent_up)
        router_parts = relative(router)
        relay = lambda v: relative(v)[1:]
        expert_ids = jnp.arange(all_experts, dtype=jnp.int32)
        hit_own = jnp.any(routes[:, :, None] == expert_ids, axis=1).astype(F32)
        marks_own = jnp.pad(hit_own.astype(LOW), ((0, 0), (0, -all_experts % LANES)))
        grad_own = lax.all_gather(jnp.concatenate([cotangent, marks_own], axis=1), "expert", axis=0)

    hidden_all = shared_gate.shape[1]
    hidden_own = hidden_all // blocks
    hidden_shard = hidden_all // shards

    def shared_columns(weight):
        pieces = [
            lax.dynamic_slice_in_dim(
                weight, place(s) * hidden_shard + chip * hidden_own, hidden_own, 1
            ).T
            for s in range(shards)
        ]
        got = [pieces[0]] + [None] * (shards - 1)
        for s in range(1, shards):
            got[shards - s] = to_core(pieces[s], s)
        return natural(got, 1)

    with jax.named_scope("shared_weights"):
        padded = -(-hidden_own // LANES) * LANES
        pad = ((0, padded - hidden_own), (0, 0))
        pair_w = jnp.concatenate(
            [jnp.pad(shared_columns(shared_gate), pad), jnp.pad(shared_columns(shared_up), pad)]
        )
        down_w = jnp.pad(
            lax.dynamic_slice_in_dim(shared_down, chip * hidden_own, hidden_own, 0), pad
        )
        router_full = natural(router_parts, 0)

    bounds = [0]
    for size in (part_cols, query_gain.shape[0], latent_gain.shape[0], part_cols):
        bounds.append(bounds[-1] + size)
    attention_gain_parts = [g[bounds[0] : bounds[1]].astype(F32) for g in gain_parts]
    query_gain_full = natural([g[bounds[1] : bounds[2]] for g in gain_parts], 0).astype(F32)
    latent_gain_full = natural([g[bounds[2] : bounds[3]] for g in gain_parts], 0).astype(F32)
    feed_gain_full = natural([g[bounds[3] : bounds[4]] for g in gain_parts], 0).astype(F32)
    gain_rel = jnp.concatenate(attention_gain_parts)

    with jax.named_scope("attention_forward"):
        positions = jnp.concatenate(
            [place(s) * rows + jnp.arange(rows, dtype=jnp.int32) for s in range(shards)]
        )
        cosine_table, sine_table = tables(positions, ROPE)
        length = seq_len[0]
        sequence = jnp.concatenate(token_parts, axis=0)
        source = jnp.concatenate(cut(sequence, 1), axis=1).astype(F32)
        source_scale = inverse_rms(source)
        normed = (source * source_scale * gain_rel).astype(LOW)
        normed_parts = jnp.split(normed, shards, axis=1)
        query_latent = total([product(a, w) for a, w in zip(normed_parts, query_down_parts)])
        query_scale = inverse_rms(query_latent)
        query_low = (query_latent * query_scale * query_gain_full).astype(LOW)
        latent = total([product(a, w) for a, w in zip(normed_parts, latent_down_parts)])
        latent_c = latent[:, :KVL]
        latent_scale = inverse_rms(latent_c)
        latent_low = (latent_c * latent_scale * latent_gain_full).astype(LOW)
        key_rope = rotate(latent[:, KVL:], cosine_table, sine_table).astype(LOW)
        query_low_parts = cut(query_low, 1)
        latent_low_parts = cut(latent_low, 1)
        query_raw = total(
            [product(a, cut(w, 1)[0]) for a, w in zip(query_low_parts, query_up_parts)]
        ).reshape(span, own_heads, NOPE + ROPE)
        query_nope = query_raw[..., :NOPE].astype(LOW)
        query_rope = rotate(
            query_raw[..., NOPE:], cosine_table[:, None, :], sine_table[:, None, :]
        ).astype(LOW)
        keys_values = (
            total([product(a, cut(w, 1)[0]) for a, w in zip(latent_low_parts, latent_up_parts)])
            .astype(LOW)
            .reshape(span, own_heads, NOPE + VDIM)
        )
        key_nope = keys_values[..., :NOPE]
        values = keys_values[..., NOPE:]
        score_scale = (NOPE + ROPE) ** (-0.5)
        allowed = (positions[None, :] <= positions[:, None]) & (positions[None, :] < length)
        raw_scores = jnp.einsum("qhd,khd->hqk", query_nope, key_nope, preferred_element_type=F32)
        raw_scores = raw_scores + jnp.einsum(
            "qhr,kr->hqk", query_rope, key_rope, preferred_element_type=F32
        )
        scores = jnp.where(allowed[None], raw_scores * score_scale, NEG)
        row_peak = jnp.max(scores, axis=-1, keepdims=True)
        exp_terms = jnp.exp(scores - row_peak)
        probabilities = exp_terms / jnp.sum(exp_terms, axis=-1, keepdims=True)
        p_low = probabilities.astype(LOW)
        mixed = jnp.einsum("hqk,khv->qhv", p_low, values, preferred_element_type=F32)
        mixed = mixed.astype(LOW).reshape(span, own_heads * VDIM)
        attended = product(mixed, attention_out)
        resid = tokens.astype(F32) + sum_parts(jnp.split(attended, shards, axis=0), F32)
        resid_scale = inverse_rms(resid)
        ffn_low = (resid * resid_scale * feed_gain_full).astype(LOW)

    with jax.named_scope("token_gather"):
        ffn_slots = Stages(gather_chips(ffn_low, relay)).finish()
        late = 2 * ring + half_ring
        ffn_slots[late][0], grad_own = tie(ffn_slots[late][0], grad_own)
        ffn_parts = list(zip(*ffn_slots))
        grad_parts = relative(grad_own)

    with jax.named_scope("routing"):
        marks = jnp.concatenate(relative(grad_own[:, :, width : width + all_experts]), axis=1)
        hits = jnp.swapaxes(marks[slot_chip], 1, 2) > 0
        first = chip * local_count
        hit = lax.dynamic_slice_in_dim(hits, first, local_count, 1).astype(jnp.int32)
        pos = jnp.where(hit > 0, jnp.cumsum(hit, axis=2) - hit, -1)
        pos_cols = jnp.swapaxes(pos, 1, 2)
        room = shards * capacity
        counts = jnp.sum(hit, axis=2).T
        steps = (counts + ROW_STEP - 1) // ROW_STEP * ROW_STEP
        ends = jnp.cumsum(steps, axis=1)
        totals = ends[:, -1]
        offsets = jnp.concatenate([(ends - steps).reshape(-1), totals])
        counts = counts.reshape(-1)
        hits = hits.astype(F32)
        first_at = first.reshape(1).astype(jnp.int32)

    with jax.named_scope("dispatch"):
        x_rows, g_rows, row_gates, feats, hiddens, delta_pair, delta_down = dispatch(
            shards, rows, room, offsets, first_at, slot_chip, hits, pos, router_full.T, pair_w,
            down_w, ffn_parts, grad_parts,
        )

    with jax.named_scope("routed_experts"):
        grad_rows, low_gate, low_up, weighted, gate_rows = run_experts(
            totals, first_at, x_rows, g_rows, row_gates, jnp.swapaxes(expert_gate, 1, 2),
            jnp.swapaxes(expert_up, 1, 2), expert_down,
        )

    with jax.named_scope("shared_gradients"):
        pair = jnp.stack(
            [delta_pair[:hidden_own], delta_pair[padded : padded + hidden_own]]
        )
        pieces = cut(pair, 2)
        got = [pieces[0]] + [None] * (shards - 1)
        for s in range(1, shards):
            got[shards - s] = to_core(pieces[s], s)
        pair = natural([v[None] for v in got], 0)
        pair_all = lax.all_gather(pair, "expert", axis=0)
        down_all = lax.all_gather(delta_down[:hidden_own], "expert", axis=0, tiled=True)

    with jax.named_scope("to_tokens"):

        def run_combine(columns, rows_all, gates_all, feat, weight):
            return combine(
                columns, ring, rows, shards, room, offsets, counts, slot_chip, rows_all, gates_all,
                pos_cols, feat, weight,
            )

        def over_cores(parts):
            number = len(parts) // shards
            sums = []
            for n in range(number):
                got = [to_core(parts[number * s + n], s) for s in range(1, shards)]
                for k in range(ring):
                    sums.append(add(parts[n][k], *[v[k] for v in got]))
            return sums

        *parts, gates_far = run_combine((3,), grad_rows, gate_rows, feats, pair_w)
        both = over_cores(parts)
        *both, grad_rows = tie(*both, grad_rows)
        *parts, gates_near = run_combine((0, 1, 2), grad_rows, gate_rows, feats, pair_w)
        mine = over_cores(parts)
        mine[-1], weighted = tie(mine[-1], weighted)
        gate_grid = jnp.concatenate([gates_near, gates_far])
        gate_grid = lax.dynamic_slice_in_dim(gate_grid, first, local_count, 2)
        gate_grid = gate_grid.reshape(owners, shards, rows, local_count)
        gate_grid = sum_parts([gate_grid[:, s] for s in range(shards)], F32)
        gate_grid = jnp.zeros_like(gate_grid).at[slot_chip].set(gate_grid)
        grad_gates = lax.all_to_all(gate_grid, "expert", split_axis=0, concat_axis=0, tiled=True)
        grad_gates = jnp.swapaxes(grad_gates, 0, 1).reshape(rows, all_experts)
        back_run = Stages(scatter_chips(mine + both))
        back_run.step()
        deltas = [grad_rows]
        for e in range(local_count):
            deltas = list(
                run_deltas(
                    e, deltas, totals, x_rows, g_rows, low_gate, low_up, weighted, expert_down
                )
            )
            if e == 0:
                deltas[0], deltas[3], pair_all, grad_gates = back_run.step(
                    deltas[0], deltas[3], pair_all, grad_gates
                )
            if e == 1:
                deltas[0], deltas[3] = back_run.step(deltas[0], deltas[3])
        parts = list(run_combine((0, 1, 2, 3), deltas[3], None, hiddens, down_w))
        parts = list(back_run.step(*parts))
        grad_from_experts = back_run.finish()
        delta_gate, delta_up, grad_expert_down, unused = deltas
        grad_expert_gate = jnp.swapaxes(delta_gate, 1, 2)
        grad_expert_up = jnp.swapaxes(delta_up, 1, 2)
        out_run = Stages(scatter_chips(over_cores(parts)))

    with jax.named_scope("feed_backward"):
        grad_out = cotangent.astype(F32)
        sig = jax.nn.sigmoid(product(ffn_low, router_full))
        chosen = sig * hit_own
        own_sum = jnp.sum(chosen, axis=1, keepdims=True)
        inner = jnp.sum(grad_gates * chosen, axis=1, keepdims=True)
        grad_chosen = ROUTE_SCALE * (grad_gates / own_sum - inner / (own_sum * own_sum))
        grad_logits = (grad_chosen * hit_own * sig * (1.0 - sig)).astype(LOW)
        grad_ffn = back_product(grad_logits, router_full) + grad_from_experts
        grad_resid_part, feed_terms = norm_back(resid, resid_scale, feed_gain_full, grad_ffn)
        grad_resid = grad_out + grad_resid_part
        grad_attended = grad_resid.astype(LOW)
        feed_gain_delta = jnp.sum(feed_terms, axis=0)

    with jax.named_scope("attention_backward"):
        attended_grads = jnp.concatenate(relative(grad_attended), axis=0)
        logit_grads = jnp.concatenate(relative(grad_logits), axis=0)
        delta_out = outer_sum(mixed, attended_grads).astype(LOW)
        ffn_sequence = cut(jnp.concatenate([part[0] for part in ffn_parts]), 1)[0]
        delta_router = outer_sum(logit_grads, ffn_sequence)
        grad_mixed = (
            back_product(attended_grads, attention_out).astype(LOW).reshape(span, own_heads, VDIM)
        )
        grad_mixed, delta_out, pair_all = out_run.step(grad_mixed, delta_out, pair_all)
        sum_out = lax.psum(delta_out, "expert")
        grad_probs = jnp.einsum("qhv,khv->hqk", grad_mixed, values, preferred_element_type=F32)
        row_delta = jnp.sum(grad_probs * probabilities, axis=-1, keepdims=True)
        grad_raw = (score_scale * probabilities * (grad_probs - row_delta)).astype(LOW)
        grad_shared_gate = transpose(0, pair_all)
        grad_raw, grad_shared_gate, pair_all = out_run.step(grad_raw, grad_shared_gate, pair_all)
        grad_shared_up = transpose(1, pair_all)
        grad_query_nope = jnp.einsum("hqk,khd->qhd", grad_raw, key_nope, preferred_element_type=F32)
        grad_query_rope = jnp.einsum("hqk,kr->qhr", grad_raw, key_rope, preferred_element_type=F32)
        grad_key_nope = jnp.einsum("hqk,qhd->khd", grad_raw, query_nope, preferred_element_type=F32)
        grad_key_rope = jnp.einsum("hqk,qhr->kr", grad_raw, query_rope, preferred_element_type=F32)
        grad_values = jnp.einsum("hqk,qhv->khv", p_low, grad_mixed, preferred_element_type=F32)
        grad_keys = (
            jnp.concatenate([grad_key_nope, grad_values], axis=-1)
            .reshape(span, own_heads * (NOPE + VDIM))
            .astype(LOW)
        )
        grad_query_turned = rotate(
            grad_query_rope, cosine_table[:, None, :], -sine_table[:, None, :]
        )
        grad_queries = (
            jnp.concatenate([grad_query_nope, grad_query_turned], axis=-1)
            .reshape(span, own_heads * (NOPE + ROPE))
            .astype(LOW)
        )

        def reorder(values, s):
            pieces = jnp.split(values, shards, axis=0)
            return jnp.concatenate([pieces[(t - s) % shards] for t in range(shards)], axis=0)

        def every_core(values):
            return [values] + [reorder(from_core(values, s), s) for s in range(1, shards)]

        grad_queries, grad_keys, grad_key_rope, down_all, grad_shared_up = out_run.step(
            grad_queries, grad_keys, grad_key_rope, down_all, grad_shared_up
        )
        grad_shared_down = down_all.astype(F32)
        queries_back = natural(every_core(grad_queries), 1)
        keys_back = natural(every_core(grad_keys), 1)
        rope_back = total(every_core(grad_key_rope))
        grad_latent_normed = natural([back_product(keys_back, w) for w in latent_up_parts], 1)
        grad_latent_part, latent_terms = norm_back(
            latent_c, latent_scale, latent_gain_full, grad_latent_normed
        )
        grad_latent = jnp.concatenate(
            [grad_latent_part, rotate(rope_back, cosine_table, -sine_table)], axis=-1
        ).astype(LOW)
        grad_query_normed = natural([back_product(queries_back, w) for w in query_up_parts], 1)
        grad_query_normed, grad_latent, grad_shared_down = out_run.step(
            grad_query_normed, grad_latent, grad_shared_down
        )
        layer_out = (resid + out_run.finish()).astype(LOW)
        grad_query_part, query_terms = norm_back(
            query_latent, query_scale, query_gain_full, grad_query_normed
        )
        grad_query_latent = grad_query_part.astype(LOW)
        down_delta = outer_sum(
            normed_parts[0], jnp.concatenate([grad_query_latent, grad_latent], axis=1)
        ).astype(LOW)
        up_delta = outer_sum(query_low_parts[0], queries_back).astype(LOW)
        latent_delta_rows = outer_sum(latent_low_parts[0], keys_back).astype(LOW)
        down_run = Stages(scatter_chips(shares(down_delta)))
        up_run = Stages(scatter_chips(shares(up_delta)))
        down_run.step()
        up_run.step()
        (latent_delta_rows,) = up_run.step(latent_delta_rows)
        down_sum = lax.all_gather(down_run.finish().astype(LOW), "expert", axis=0, tiled=True)
        mine_up = up_run.finish().astype(LOW)
        grad_normed = jnp.concatenate(
            [
                back_product(grad_query_latent[:rows], a) + back_product(grad_latent[:rows], b)
                for a, b in zip(query_down_parts, latent_down_parts)
            ],
            axis=1,
        )
        grad_source, attention_terms = norm_back(
            source[:rows], source_scale[:rows], gain_rel, grad_normed
        )
        grad_tokens = grad_resid + natural(jnp.split(grad_source, shards, axis=1), 1)

    with jax.named_scope("gain_gradients"):
        attention_delta = jnp.split(jnp.sum(attention_terms, axis=0), shards)
        feed_delta = cut(feed_gain_delta, 0)
        both = sum_parts(
            [jnp.concatenate([a, f]) for a, f in zip(attention_delta, feed_delta)], F32
        )
        query_delta = cut(jnp.sum(query_terms, axis=0), 0)[0]
        latent_delta = cut(jnp.sum(latent_terms, axis=0), 0)[0]
        sums = jnp.concatenate([delta_router.reshape(-1), both, query_delta, latent_delta])
        sizes = [all_experts * part_cols, part_cols, part_cols]
        sizes += [query_gain.shape[0], latent_gain.shape[0]]
        height = latent_delta_rows.shape[0]
        sums = sums.reshape(height, -1).astype(LOW)
        mine_latent = Stages(
            scatter_chips(shares(jnp.concatenate([latent_delta_rows, sums], axis=1)))
        ).finish()
        up_run = Stages(gather_chips(mine_up))
        up_run.step()
        (mine_latent,) = up_run.step(mine_latent.astype(LOW))
        latent_run = Stages(gather_chips(mine_latent))
        latent_run.step()
        latent_run.step()
        (grad_query_up,) = in_rows(up_run.finish())
        (sum_out,) = latent_run.step(sum_out)
        (grad_attention_out,) = latent_run.step(sum_out.astype(F32))
        grad_latent_up, sums = in_rows(
            latent_run.finish(), (latent_delta_rows.shape[1], sums.shape[1])
        )
        sums = sums.reshape(-1)
        grad_query_down, grad_latent_down = jnp.split(
            down_sum.astype(F32), [grad_query_latent.shape[1]], axis=1
        )
        marks = [0]
        for size in sizes:
            marks.append(marks[-1] + size)
        grad_router, grad_attention_gain, grad_feed_gain, grad_query_gain, grad_latent_gain = [
            sums[a:b] for a, b in zip(marks, marks[1:])
        ]
        grad_router = grad_router.reshape(all_experts, part_cols).T

    return (
        layer_out,
        grad_tokens,
        grad_attention_gain,
        grad_query_down,
        grad_query_gain,
        grad_query_up,
        grad_latent_down,
        grad_latent_gain,
        grad_latent_up,
        grad_attention_out,
        grad_feed_gain,
        grad_router,
        grad_shared_gate,
        grad_shared_up,
        grad_shared_down,
        grad_expert_gate,
        grad_expert_up,
        grad_expert_down,
    )


def solution(mesh):
    tokens_spec = P(("expert", "shard"), None)
    rows_spec = P("shard", None)
    gain_spec = P("shard")
    expert_specs = (
        P("expert", None, "shard"),
        P("expert", None, "shard"),
        P("expert", "shard", None),
    )
    weight_specs = (
        gain_spec,
        rows_spec,
        gain_spec,
        rows_spec,
        rows_spec,
        gain_spec,
        rows_spec,
        rows_spec,
        gain_spec,
        rows_spec,
        rows_spec,
        rows_spec,
        rows_spec,
    ) + expert_specs
    return jax.shard_map(
        local,
        mesh=mesh,
        in_specs=(tokens_spec, tokens_spec, P("expert"), tokens_spec) + weight_specs,
        out_specs=(tokens_spec, tokens_spec) + weight_specs,
        check_vma=False,
    )
```
